32 devices in a mesh: rcv: 8 (over z, y), ref: 4 (over x, core).
Axes of the slice: x: 2, y: 2, z: 4, core: 2. Of those that a mesh axis runs over, the one named last changes fastest.
Arguments:
- receiver_spectra: bfloat16 [64, 8192], P('rcv', 'ref'), may hold values from -6 to 6
- reference_spectra: bfloat16 [8192, 1024], P('rcv', 'ref'), may hold values from -6 to 6
- receiver_counts: int32 [64], P('rcv'), may hold values from 1 to 16
- reference_counts: int32 [1024], P('ref'), may hold values from 1 to 16
- column_station: int32 [1024], P('ref'), may hold values from 0 to 1023, as said below
- lag_window: int32 [2, 64, 1024], P(None, 'rcv', 'ref'), may hold values from 0 to 256, as said below
- observed: bfloat16 [64, 1024, 512], P('rcv', 'ref'), may hold values from 0.19921875 to 2
Outputs:
- receiver_grad: float32 [64, 8192], P('rcv', 'ref')
- reference_grad: float32 [8192, 1024], P('rcv', 'ref')
The draws below stay inside these ranges and needn't reach their ends.
Inputs may be any that keep to these rules, and one draw needn't show every extreme that they name: `receiver_counts`: number of valid leading segments of each station. `column_station`: A permutation of the 1024 reference stations that maps each block of 256 consecutive pair columns onto the same block of stations. lag_window[0] is a first lag below 256; lag_window[1] is a number of lags from 64 to 256.
All inputs are finite; a program needn't handle non-finite values.
Results may differ from the reference program's by a relative error of at most 0.0014.
Values may be sent and summed in bfloat16 or wider, within the bound.
No kernel may reach another device: no remote copies, remote signals or barrier semaphores. Data moves between devices by JAX's collectives and lax.ppermute only.
A program may use at most 64 MiB of HBM per device.

```python
import math
import jax
import jax.numpy as jnp
from jax import lax

RCV_DEV = 8
REF_DEV = 256
L = 512
S = 16
F = 256
K = 8192
NR = 64
NS = 1024


def draw_column_station(key, part):
    block_total = NS // REF_DEV

    def one_block(block_id):
        shuffled = jax.random.permutation(jax.random.fold_in(jax.random.fold_in(key, 11), block_id), REF_DEV)
        return shuffled.astype(jnp.int32) + block_id * REF_DEV
    return jax.vmap(one_block)(jnp.arange(block_total, dtype=jnp.int32)).reshape(NS).astype(jnp.int32)


def draw_lag_window(key, part):
    start_key, span_key = jax.random.split(jax.random.fold_in(key, 7))
    starts = jax.random.randint(start_key, (NR, NS), 0, L // 2)
    spans = jax.random.randint(span_key, (NR, NS), L // 8, L // 2 + 1)
    return jnp.stack([starts, spans]).astype(jnp.int32)


def place_ends(values, own_key, least, top_value):
    place = [jax.random.randint(jax.random.fold_in(own_key, axis), (), 0, length) for axis, length in enumerate(values.shape)]
    longest = values.shape.index(max(values.shape))
    beside = place[:longest] + [(place[longest] + 1) % values.shape[longest]] + place[longest + 1:]
    return values.at[tuple(place)].set(least).at[tuple(beside)].set(top_value)


def block_scale(own_key, extent, cuts, least, largest):
    gain = 1.0
    for position, parts in cuts:
        draws = jax.random.uniform(jax.random.fold_in(jax.random.fold_in(own_key, 6), position), (parts,), jnp.float32, least / len(cuts), largest / len(cuts))
        gain = gain * jnp.repeat(jnp.exp(draws), extent[position] // parts).reshape((-1,) + (1,) * (len(extent) - 1 - position))
    return gain


def bell_draw(own_key, dims, width, reach, cuts=(), held_as=jnp.bfloat16):
    drawn = width * jax.random.normal(own_key, dims, jnp.float32)
    if cuts:
        drawn = drawn * block_scale(own_key, dims, cuts, -0.22, 0.18)
    return jnp.clip(drawn, -reach, reach).astype(held_as)


def setup_inputs(seed: int = 0) -> dict:
    key_list = jax.random.split(jax.random.key(seed), 8)
    receiver_spectra = bell_draw(key_list[0], (NR, K), 1.0, 6.0, ((0, 8), (1, 4)))
    reference_spectra = bell_draw(key_list[1], (K, NS), 1.0, 6.0, ((0, 8), (1, 4)))
    receiver_counts = place_ends(jax.random.randint(key_list[2], (NR,), 1, S + 1), jax.random.fold_in(key_list[2], 1), 1, S).astype(jnp.int32)
    reference_counts = place_ends(jax.random.randint(key_list[3], (NS,), 1, S + 1), jax.random.fold_in(key_list[3], 1), 1, S).astype(jnp.int32)
    column_station = draw_column_station(jax.random.fold_in(key_list[7], 71), 0)
    lag_window = draw_lag_window(jax.random.fold_in(key_list[7], 71), 0)
    observed = jnp.clip(0.19921875 + 1.8007812 * jax.random.uniform(key_list[6], (NR, NS, L), jnp.float32) ** block_scale(key_list[6], (NR, NS, L), ((0, 8), (1, 4)), -0.2, 0.2), 0.19921875, 2.0).astype(jnp.bfloat16)
    return dict(receiver_spectra=receiver_spectra, reference_spectra=reference_spectra, receiver_counts=receiver_counts, reference_counts=reference_counts, column_station=column_station, lag_window=lag_window, observed=observed)


env_floor = 0.05
misfit_scale = 0.03125

def lag_table(freq_total, lag_total):
    freq_ids = jnp.arange(freq_total, dtype=jnp.int32)[:, None]
    lag_ids = jnp.arange(lag_total, dtype=jnp.int32)[None, :] - lag_total // 2
    phase_ids = freq_ids * lag_ids % lag_total
    phase_angle = phase_ids.astype(jnp.float32) * (2.0 * math.pi / lag_total)
    cosine = jnp.cos(phase_angle) / math.sqrt(freq_total)
    sine_part = jnp.sin(phase_angle) / math.sqrt(freq_total)
    real_rows = jnp.concatenate([cosine, sine_part], axis=1)
    imag_rows = jnp.concatenate([-sine_part, cosine], axis=1)
    stacked = jnp.stack([real_rows, imag_rows], axis=1)
    return stacked.reshape(2 * freq_total, 2 * lag_total).astype(jnp.bfloat16)

def segment_masks(receiver_counts, pair_counts, seg_total):
    seg_ids = jnp.arange(seg_total, dtype=jnp.int32)
    receiver_mask = (seg_ids[None, :] < receiver_counts[:, None]).astype(jnp.float32)
    reference_mask = (seg_ids[:, None] < pair_counts[None, :]).astype(jnp.float32)
    return (receiver_mask, reference_mask)

def receiver_operand(receiver_vals):
    real_part = receiver_vals[:, :, 0, :]
    imag_part = receiver_vals[:, :, 1, :]
    first_row = jnp.concatenate([real_part, imag_part], axis=-1)
    second_row = jnp.concatenate([imag_part, -real_part], axis=-1)
    return jnp.stack([first_row, second_row], axis=2)

def reference_operand(reference_vals):
    real_part = reference_vals[:, 0]
    imag_part = reference_vals[:, 1]
    first_row = jnp.stack([real_part, imag_part], axis=1)
    second_row = jnp.stack([-imag_part, real_part], axis=1)
    return jnp.stack([first_row, second_row], axis=1)

def pair_block(receiver_op, reference_flat, pair_norm, window, observed_block, lag_matrix):
    row_total = receiver_op.shape[0]
    col_total = reference_flat.shape[2]
    highest = lax.Precision.HIGHEST
    cross_spec = jnp.einsum('ifqk,fkj->ijfq', receiver_op, reference_flat, precision=highest)
    spectra = (cross_spec / pair_norm[:, :, None, None]).astype(jnp.bfloat16)
    matrix_wide = lag_matrix.astype(jnp.float32)
    lagged = jnp.dot(spectra.reshape(row_total * col_total, 2 * F).astype(jnp.float32), matrix_wide, precision=highest)
    lagged = lagged.reshape(row_total, col_total, 2 * L)
    correlation = lagged[..., :L]
    hilbert_part = lagged[..., L:]
    envelope = jnp.sqrt(correlation * correlation + hilbert_part * hilbert_part + env_floor)
    lag_ids = jnp.arange(L, dtype=jnp.int32)
    inside = (lag_ids >= window[0][..., None]) & (lag_ids < (window[0] + window[1])[..., None])
    misfit = jnp.where(inside, envelope - observed_block.astype(jnp.float32), 0.0) * misfit_scale
    weights = jnp.concatenate([misfit * correlation / envelope, misfit * hilbert_part / envelope], axis=-1).astype(jnp.bfloat16)
    back_proj = jnp.dot(weights.reshape(row_total * col_total, 2 * L).astype(jnp.float32), matrix_wide.T, precision=highest)
    back_proj = back_proj.reshape(row_total, col_total, F, 2)
    return (back_proj / pair_norm[:, :, None, None]).astype(jnp.bfloat16)

def reference(receiver_spectra, reference_spectra, receiver_counts, reference_counts, column_station, lag_window, observed):
    highest = lax.Precision.HIGHEST
    lag_matrix = lag_table(F, L)
    pair_counts = jnp.take(reference_counts, column_station)
    receiver_mask, reference_mask = segment_masks(receiver_counts, pair_counts, S)
    receiver_vals = receiver_spectra.astype(jnp.float32).reshape(NR, F, 2, S) * receiver_mask[:, None, None, :]
    reference_vals = jnp.take(reference_spectra, column_station, axis=1).astype(jnp.float32).reshape(F, 2, S, NS)
    reference_vals = reference_vals * reference_mask[None, None, :, :]
    receiver_op = receiver_operand(receiver_vals)
    reference_flat = reference_vals.reshape(F, 2 * S, NS)
    reference_op = reference_operand(reference_vals)
    block_total = NR // RCV_DEV

    def block_step(carry_sum, block_id):
        begin_row = block_id * RCV_DEV
        op_block = lax.dynamic_slice_in_dim(receiver_op, begin_row, RCV_DEV, 0)
        count_block = lax.dynamic_slice_in_dim(receiver_counts, begin_row, RCV_DEV, 0)
        mask_block = lax.dynamic_slice_in_dim(receiver_mask, begin_row, RCV_DEV, 0)
        window = lax.dynamic_slice_in_dim(lag_window, begin_row, RCV_DEV, 1)
        observed_block = lax.dynamic_slice_in_dim(observed, begin_row, RCV_DEV, 0)
        pair_norm = jnp.minimum(count_block[:, None], pair_counts[None, :]).astype(jnp.float32)
        grad_spec = pair_block(op_block, reference_flat, pair_norm, window, observed_block, lag_matrix).astype(jnp.float32)
        receiver_part = jnp.einsum('ijfq,fqcsj->ifcs', grad_spec, reference_op, precision=highest)
        receiver_part = receiver_part * mask_block[:, None, None, :]
        reference_part = jnp.einsum('ijfq,ifqk->fkj', grad_spec, op_block, precision=highest)
        return (carry_sum + reference_part, receiver_part.reshape(RCV_DEV, K))
    reference_total, receiver_blocks = lax.scan(block_step, jnp.zeros((F, 2 * S, NS), jnp.float32), jnp.arange(block_total, dtype=jnp.int32))
    receiver_grad = receiver_blocks.reshape(NR, K)
    permuted = (reference_total.reshape(F, 2, S, NS) * reference_mask[None, None, :, :]).reshape(K, NS)
    reference_grad = jnp.zeros((K, NS), jnp.float32).at[:, column_station].set(permuted)
    return (receiver_grad, reference_grad)
```

```python
import functools
import math

import jax
import jax.numpy as jnp
import numpy as np
from jax import lax
from jax.experimental import pallas as pl
from jax.experimental.pallas import tpu as pltpu
from jax.sharding import PartitionSpec as P

L = 512
S = 16
F = 256

env_floor = 0.05
misfit_scale = 0.03125
GROUP = 4
LANES = 128
FB = LANES // (2 * S)


def lag_tables(freq_total, lag_total):
    half = lag_total // 2
    freq_ids = np.arange(freq_total)[:, None]
    phase = 2.0 * np.pi * (freq_ids * np.arange(half)[None, :] % lag_total) / lag_total
    cosine = np.cos(phase) / math.sqrt(freq_total)
    sine = np.sin(phase) / math.sqrt(freq_total)
    back = [np.concatenate([cosine[p::2], sine[p::2]], axis=1) for p in (0, 1)]
    ahead = [np.concatenate([cosine[p::2].T, sine[p::2].T], axis=1) for p in (0, 1)]
    return [jnp.asarray(t.astype(np.float32)).astype(jnp.bfloat16) for t in ahead + back]


def nt(a, b):
    return lax.dot_general(a, b, (((1,), (1,)), ((), ())), preferred_element_type=jnp.float32)


def nn(a, b):
    return jnp.dot(a, b, preferred_element_type=jnp.float32)


def tn(a, b):
    return lax.dot_general(a, b, (((0,), (0,)), ((), ())), preferred_element_type=jnp.float32)


def pair_kernel(
    v_ref, u_ref, e_ref, invn_ref, eye_ref, ye_ref, yo_ref, ze_ref, zo_ref, w_ref, r_ref, x_ref
):
    src_total, col_total, k_own = v_ref.shape
    irec = u_ref.shape[0] // 2
    jj_total = LANES // (2 * irec)
    jp_total = col_total // jj_total
    ref_total, _, k_quarter = r_ref.shape
    k_total = src_total * k_own
    half_f = k_total // (4 * S)
    freq_total = 2 * half_f
    blocks = k_total // LANES
    own_blocks = k_own // LANES
    quarter_blocks = k_quarter // LANES

    group_ids = lax.broadcasted_iota(jnp.int32, (jp_total, LANES), 1) // (2 * S)

    def lanes_of(fb, per):
        return fb // per, pl.multiple_of(fb % per * LANES, LANES)

    def v_block(fb):
        src, off = lanes_of(fb, own_blocks)
        parts = [
            v_ref[src, jj * jp_total : (jj + 1) * jp_total, pl.ds(off, LANES)]
            for jj in range(jj_total)
        ]
        zero = jnp.zeros((jp_total, LANES), jnp.bfloat16)
        rows = [
            jnp.concatenate([jnp.where(group_ids == f, part, zero) for part in parts], axis=1)
            for f in range(FB)
        ]
        return jnp.concatenate(rows, axis=0)

    def u_block(fb):
        off = pl.multiple_of(fb * LANES, LANES)
        zero = jnp.zeros((irec, LANES), jnp.bfloat16)
        rows = []
        for q in range(2):
            part = u_ref[q * irec : (q + 1) * irec, pl.ds(off, LANES)]
            for jj in range(jj_total):
                rows.append(
                    jnp.concatenate([part if k == jj else zero for k in range(jj_total)], axis=1)
                )
        return jnp.concatenate(rows, axis=0)

    def place(fb, f):
        return pl.ds((f % 2) * half_f + fb * (FB // 2) + f // 2, jp_total, stride=freq_total)

    def forward(fb, _):
        out = nt(v_block(fb), u_block(fb))
        scale = invn_ref[...]
        for f in range(FB):
            x_ref[place(fb, f), :] = out[f * jp_total : (f + 1) * jp_total] * scale
        return 0

    lax.fori_loop(0, blocks, forward, 0, unroll=4)

    lane_ids = lax.broadcasted_iota(jnp.int32, (1, LANES), 1)
    sign = jnp.where(lane_ids < LANES // 2, -1.0, 1.0).astype(jnp.float32)
    width = 2

    def pairs(step, _):
        cols = [step * width + k for k in range(width)]
        rhs_e, rhs_o, obs = [], [], []
        for jp in cols:
            x = x_ref[pl.ds(pl.multiple_of(jp * freq_total, freq_total), freq_total), :]
            x = x.astype(jnp.bfloat16).astype(jnp.float32)
            turned = pltpu.roll(x, LANES // 2, 1) * sign
            rhs_e.append(jnp.concatenate([x[:half_f], turned[:half_f]], axis=0))
            rhs_o.append(jnp.concatenate([x[half_f:], turned[half_f:]], axis=0))
            rows = [e_ref[:, jj * jp_total + jp].astype(jnp.float32) for jj in range(jj_total)]
            rows = [r.reshape(irec, r.shape[-1]) for r in rows]
            obs.append(jnp.concatenate(rows * 2, axis=0))
        rhs_e = jnp.concatenate(rhs_e, axis=1).astype(jnp.bfloat16)
        rhs_o = jnp.concatenate(rhs_o, axis=1).astype(jnp.bfloat16)
        even = nn(ye_ref[...], rhs_e)
        odd = nn(yo_ref[...], rhs_o)
        seen = nt(eye_ref[...], jnp.concatenate(obs, axis=0).astype(jnp.bfloat16))
        g_e, g_o = [], []
        for k in range(width):
            lanes = slice(k * LANES, (k + 1) * LANES)
            e, d0, d1 = seen[:, lanes], even[:, lanes], odd[:, lanes]
            high = e < 0.0
            d = d0 + jnp.where(high, d1, -d1)
            power = d * d
            power = power + pltpu.roll(power, LANES // 2, 1) + env_floor
            g = d * (1.0 - jnp.abs(e) * lax.rsqrt(power)) * misfit_scale
            g = jnp.where(e == 0.0, 0.0, g)
            turned = -pltpu.roll(g, LANES // 2, 1) * sign
            g_e.append(jnp.concatenate([g, turned], axis=0))
            g_o.append(
                jnp.concatenate([jnp.where(high, g, -g), jnp.where(high, turned, -turned)], axis=0)
            )
        z_e = nn(ze_ref[...], jnp.concatenate(g_e, axis=1).astype(jnp.bfloat16))
        z_o = nn(zo_ref[...], jnp.concatenate(g_o, axis=1).astype(jnp.bfloat16))
        for k, jp in enumerate(cols):
            lanes = slice(k * LANES, (k + 1) * LANES)
            scale = invn_ref[pl.ds(jp, 1), :]
            base = pl.multiple_of(jp * freq_total, freq_total)
            x_ref[pl.ds(base, half_f), :] = z_e[:, lanes] * scale
            x_ref[pl.ds(base + half_f, half_f), :] = z_o[:, lanes] * scale
        return 0

    lax.fori_loop(0, jp_total // width, pairs, 0)

    first_part = lax.broadcasted_iota(jnp.int32, (irec, LANES), 1) % (2 * S) < S

    def backward(fb, _):
        z = jnp.concatenate([x_ref[place(fb, f), :] for f in range(FB)], axis=0)
        z = z.astype(jnp.bfloat16)
        w = nn(z, u_block(fb))
        src, off = lanes_of(fb, own_blocks)
        for jj in range(jj_total):
            lanes = slice(jj * LANES, (jj + 1) * LANES)
            total = w[:jp_total, lanes]
            for f in range(1, FB):
                total = jnp.where(group_ids == f, w[f * jp_total : (f + 1) * jp_total, lanes], total)
            w_ref[src, jj * jp_total : (jj + 1) * jp_total, pl.ds(off, LANES)] = total
        r = tn(z, v_block(fb))
        sums = []
        for q in range(2):
            total = None
            for jj in range(jj_total):
                begin = (q * jj_total + jj) * irec
                part = r[begin : begin + irec, jj * LANES : (jj + 1) * LANES]
                total = part if total is None else total + part
            sums.append(total)
        crossed = jnp.where(
            first_part, -pltpu.roll(sums[1], LANES - S, 1), pltpu.roll(sums[1], S, 1)
        )
        quarter, off = lanes_of(fb, quarter_blocks)
        r_ref[quarter, :, pl.ds(off, LANES)] = sums[0] + crossed
        return 0

    lax.fori_loop(0, blocks, backward, 0, unroll=4)


def shards(
    receiver_spectra,
    reference_spectra,
    receiver_counts,
    reference_counts,
    column_station,
    lag_window,
    observed,
    *,
    rcv_total,
    ref_total,
):
    row_total, k_quarter = receiver_spectra.shape
    k_own, col_total = reference_spectra.shape
    k_total = k_own * rcv_total
    lag_total = observed.shape[2]
    half = lag_total // 2
    members = math.gcd(GROUP, rcv_total)
    groups = [
        [begin + k for k in range(members)] for begin in range(0, rcv_total, members)
    ]
    irec = row_total * members
    cols = col_total // members
    jj_total = LANES // (2 * irec)
    jp_total = cols // jj_total
    bf16 = jnp.bfloat16

    seg_own = jnp.arange(k_own, dtype=jnp.int32) % S
    turned = reference_spectra.T
    turned = jnp.where(seg_own[None, :] < reference_counts[:, None], turned, jnp.zeros((), bf16))
    sent = jnp.broadcast_to(
        turned.reshape(1, members, cols, k_own), (rcv_total // members, members, cols, k_own)
    ).reshape(rcv_total, cols, k_own)
    v_all = lax.all_to_all(sent, "rcv", split_axis=0, concat_axis=0, tiled=True)

    local_order = column_station - lax.axis_index("ref") * col_total
    begin = lag_window[0][..., None]
    end = begin + lag_window[1][..., None]
    lag_ids = jnp.arange(half, dtype=jnp.int32)
    low = (lag_ids >= begin) & (lag_ids < end)
    high = (lag_ids + half >= begin) & (lag_ids + half < end)
    folded = jnp.where(
        low, observed[..., :half], jnp.where(high, -observed[..., half:], jnp.zeros((), bf16))
    )
    pick = (jnp.arange(col_total, dtype=jnp.int32)[:, None] == local_order[None, :]).astype(bf16)
    folded = jnp.transpose(folded, (1, 0, 2)).reshape(col_total, row_total * half)
    folded = jnp.dot(pick, folded, preferred_element_type=jnp.float32).astype(bf16)
    folded = folded.reshape(members, cols, row_total, half)
    e_all = lax.all_to_all(
        folded, "rcv", split_axis=0, concat_axis=0, axis_index_groups=groups, tiled=True
    )

    seg_quarter = jnp.arange(k_quarter, dtype=jnp.int32) % S
    masked = jnp.where(
        seg_quarter[None, :] < receiver_counts[:, None], receiver_spectra, jnp.zeros((), bf16)
    )
    counts = jnp.broadcast_to(receiver_counts.astype(bf16)[:, None], (row_total, LANES))
    own = jnp.concatenate([masked, counts], axis=1)
    near = lax.all_gather(own, "rcv", axis_index_groups=groups, axis=0, tiled=True)
    group_counts = near[:, k_quarter].astype(jnp.float32)
    u_all = lax.all_gather(near[:, :k_quarter], "ref", axis=1, tiled=True)
    parts = u_all.reshape(irec, k_total // (2 * S), 2, S)
    crossed = jnp.stack([parts[:, :, 1], -parts[:, :, 0]], axis=2).reshape(irec, k_total)
    u_rows = jnp.concatenate([u_all, crossed], axis=0)

    place = lax.axis_index("rcv") % members
    own_counts = lax.dynamic_slice_in_dim(reference_counts, place * cols, cols).astype(jnp.float32)
    least = jnp.minimum(
        own_counts.reshape(jj_total, jp_total).T[:, :, None], group_counts[None, None, :]
    )
    inverse = (1.0 / least).reshape(jp_total, jj_total * irec)
    inverse = jnp.concatenate([inverse, inverse], axis=1)

    tables = lag_tables(k_total // (2 * S), lag_total)
    eye = jnp.eye(half, dtype=bf16)
    w_part, r_part = pl.pallas_call(
        pair_kernel,
        out_shape=(
            jax.ShapeDtypeStruct((rcv_total, cols, k_own), jnp.float32),
            jax.ShapeDtypeStruct((ref_total, irec, k_quarter), jnp.float32),
        ),
        in_specs=[pl.BlockSpec(memory_space=pltpu.VMEM)] * 9,
        out_specs=[pl.BlockSpec(memory_space=pltpu.VMEM)] * 2,
        scratch_shapes=[pltpu.VMEM((jp_total * k_total // (2 * S), LANES), jnp.float32)],
        compiler_params=pltpu.CompilerParams(vmem_limit_bytes=48 * 1024 * 1024),
    )(v_all, u_rows, e_all, inverse, eye, *tables)

    got = lax.all_to_all(w_part, "rcv", split_axis=0, concat_axis=0, tiled=True)
    got = got.reshape(rcv_total // members, col_total, k_own).sum(axis=0)
    got = jnp.where(seg_own[None, :] < reference_counts[:, None], got, 0.0)
    reference_grad = got.T

    r_sum = lax.all_to_all(r_part, "ref", split_axis=0, concat_axis=0, tiled=True).sum(axis=0)
    r_sum = lax.all_to_all(
        r_sum.reshape(members, row_total, k_quarter),
        "rcv",
        split_axis=0,
        concat_axis=0,
        axis_index_groups=groups,
        tiled=True,
    ).sum(axis=0)
    receiver_grad = jnp.where(seg_quarter[None, :] < receiver_counts[:, None], r_sum, 0.0)
    return (receiver_grad, reference_grad)


def solution(mesh):
    return jax.shard_map(
        functools.partial(shards, rcv_total=mesh.shape["rcv"], ref_total=mesh.shape["ref"]),
        mesh=mesh,
        in_specs=(
            P("rcv", "ref"),
            P("rcv", "ref"),
            P("rcv"),
            P("ref"),
            P("ref"),
            P(None, "rcv", "ref"),
            P("rcv", "ref", None),
        ),
        out_specs=(P("rcv", "ref"), P("rcv", "ref")),
        check_vma=False,
    )
```

```python
import functools
import math

import jax
import jax.numpy as jnp
import numpy as np
from jax import lax
from jax.experimental import pallas as pl
from jax.experimental.pallas import tpu as pltpu
from jax.sharding import PartitionSpec as P

L = 512
S = 16
F = 256

env_floor = 0.05
misfit_scale = 0.03125
GROUP = 4
LANES = 128
FB = LANES // (2 * S)
WIDTH = 8
FIXED = 32000.0


def lag_tables(freq_total, lag_total):
    half = lag_total // 2
    freq_ids = np.arange(freq_total)[:, None]
    phase = 2.0 * np.pi * (freq_ids * np.arange(half)[None, :] % lag_total) / lag_total
    cosine = np.cos(phase) / math.sqrt(freq_total)
    sine = np.sin(phase) / math.sqrt(freq_total)
    back = [np.concatenate([cosine[p::2], sine[p::2]], axis=1) for p in (0, 1)]
    ahead = [np.concatenate([cosine[p::2].T, sine[p::2].T], axis=1) for p in (0, 1)]
    return [jnp.asarray(t.astype(np.float32)).astype(jnp.bfloat16) for t in ahead + back]


def nt(a, b):
    return lax.dot_general(a, b, (((1,), (1,)), ((), ())), preferred_element_type=jnp.float32)


def nn(a, b):
    return jnp.dot(a, b, preferred_element_type=jnp.float32)


def tn(a, b):
    return lax.dot_general(a, b, (((0,), (0,)), ((), ())), preferred_element_type=jnp.float32)


def pair_kernel(
    c_ref, v_ref, u_ref, invn_ref, eye_ref, ye_ref, yo_ref, ze_ref, zo_ref, *rest
):
    *e_refs, w_ref, r_ref, x_ref, urow_ref, code_ref = rest
    src_total, col_total, k_own = v_ref.shape
    ref_total, irec, k_quarter = u_ref.shape
    member_rows = irec // len(e_refs)
    jj_total = LANES // (2 * irec)
    jp_total = col_total // jj_total
    k_total = src_total * k_own
    half_f = k_total // (4 * S)
    freq_total = 2 * half_f
    blocks = k_total // LANES
    own_blocks = k_own // LANES
    quarter_blocks = k_quarter // LANES

    group_ids = lax.broadcasted_iota(jnp.int32, (jp_total, LANES), 1) // (2 * S)
    first_part = lax.broadcasted_iota(jnp.int32, (irec, LANES), 1) % (2 * S) < S
    me = c_ref[0]

    def lanes_of(fb, per):
        return fb // per, pl.multiple_of(fb % per * LANES, LANES)

    def v_block(fb):
        src, off = lanes_of(fb, own_blocks)
        parts = [
            v_ref[src, jj * jp_total : (jj + 1) * jp_total, pl.ds(off, LANES)]
            for jj in range(jj_total)
        ]
        zero = jnp.zeros((jp_total, LANES), jnp.bfloat16)
        rows = [
            jnp.concatenate([jnp.where(group_ids == f, part, zero) for part in parts], axis=1)
            for f in range(FB)
        ]
        return jnp.concatenate(rows, axis=0)

    def u_block(parts):
        zero = jnp.zeros((irec, LANES), jnp.bfloat16)
        return jnp.concatenate(
            [
                jnp.concatenate([part if k == jj else zero for k in range(jj_total)], axis=1)
                for part in parts
                for jj in range(jj_total)
            ],
            axis=0,
        )

    def place(fb, f):
        return pl.ds((f % 2) * half_f + fb * (FB // 2) + f // 2, jp_total, stride=freq_total)

    def forward(fb, _):
        quarter, off = lanes_of(fb, quarter_blocks)
        part = u_ref[quarter ^ me, :, pl.ds(off, LANES)]
        wide = part.astype(jnp.float32)
        crossed = jnp.where(first_part, pltpu.roll(wide, LANES - S, 1), -pltpu.roll(wide, S, 1))
        crossed = crossed.astype(jnp.bfloat16)
        lanes = pl.ds(pl.multiple_of(fb * LANES, LANES), LANES)
        urow_ref[0, :, lanes] = part
        urow_ref[1, :, lanes] = crossed
        out = nt(v_block(fb), u_block([part, crossed]))
        scale = invn_ref[...]
        for f in range(FB):
            x_ref[place(fb, f), :] = out[f * jp_total : (f + 1) * jp_total] * scale
        return 0

    lax.fori_loop(0, blocks, forward, 0, unroll=16)

    lane_ids = lax.broadcasted_iota(jnp.int32, (1, LANES), 1)
    sign = jnp.where(lane_ids < LANES // 2, -1.0, 1.0).astype(jnp.float32)

    def pairs(step, _):
        cols = [step * WIDTH + k for k in range(WIDTH)]
        rhs_e, rhs_o, obs = [], [], []
        for jp in cols:
            x = x_ref[pl.ds(pl.multiple_of(jp * freq_total, freq_total), freq_total), :]
            x = x.astype(jnp.bfloat16).astype(jnp.float32)
            turned = pltpu.roll(x, LANES // 2, 1) * sign
            rhs_e.append(jnp.concatenate([x[:half_f], turned[:half_f]], axis=0))
            rhs_o.append(jnp.concatenate([x[half_f:], turned[half_f:]], axis=0))
            rows = [
                ref[jj * jp_total + jp].astype(jnp.float32)
                for jj in range(jj_total)
                for ref in e_refs
            ]
            obs.append(jnp.concatenate(rows * 2, axis=0))
        rhs_e = jnp.concatenate(rhs_e, axis=1).astype(jnp.bfloat16)
        rhs_o = jnp.concatenate(rhs_o, axis=1).astype(jnp.bfloat16)
        even = nn(ye_ref[...], rhs_e)
        odd = nn(yo_ref[...], rhs_o)
        seen = nt(eye_ref[...], jnp.concatenate(obs, axis=0).astype(jnp.bfloat16))
        g_e, g_o = [], []
        for k in range(WIDTH):
            lanes = slice(k * LANES, (k + 1) * LANES)
            e, d0, d1 = seen[:, lanes], even[:, lanes], odd[:, lanes]
            high = e < 0.0
            d = d0 + jnp.where(high, d1, -d1)
            power = d * d
            power = power + pltpu.roll(power, LANES // 2, 1) + env_floor
            g = d * (1.0 - jnp.abs(e) * lax.rsqrt(power)) * misfit_scale
            g = jnp.where(e == 0.0, 0.0, g)
            turned = -pltpu.roll(g, LANES // 2, 1) * sign
            g_e.append(jnp.concatenate([g, turned], axis=0))
            g_o.append(
                jnp.concatenate([jnp.where(high, g, -g), jnp.where(high, turned, -turned)], axis=0)
            )
        z_e = nn(ze_ref[...], jnp.concatenate(g_e, axis=1).astype(jnp.bfloat16))
        z_o = nn(zo_ref[...], jnp.concatenate(g_o, axis=1).astype(jnp.bfloat16))
        for k, jp in enumerate(cols):
            lanes = slice(k * LANES, (k + 1) * LANES)
            scale = invn_ref[pl.ds(jp, 1), :]
            base = pl.multiple_of(jp * freq_total, freq_total)
            x_ref[pl.ds(base, half_f), :] = z_e[:, lanes] * scale
            x_ref[pl.ds(base + half_f, half_f), :] = z_o[:, lanes] * scale
        return 0

    lax.fori_loop(0, jp_total // WIDTH, pairs, 0)

    def backward(fb, _):
        z = jnp.concatenate([x_ref[place(fb, f), :] for f in range(FB)], axis=0)
        z = z.astype(jnp.bfloat16)
        lanes = pl.ds(pl.multiple_of(fb * LANES, LANES), LANES)
        w = nn(z, u_block([urow_ref[q, :, lanes] for q in range(2)]))
        totals = []
        for jj in range(jj_total):
            lanes = slice(jj * LANES, (jj + 1) * LANES)
            total = w[:jp_total, lanes]
            for f in range(1, FB):
                total = jnp.where(group_ids == f, w[f * jp_total : (f + 1) * jp_total, lanes], total)
            totals.append(total)
        total = jnp.concatenate(totals, axis=0)
        largest = jnp.max(jnp.abs(total), axis=0, keepdims=True)
        power = jnp.ceil(jnp.log2(jnp.maximum(largest, 1e-30)))
        code_ref[pl.ds(fb, 1), :] = power
        fixed = jnp.round(total * (jnp.exp2(-power) * FIXED)).astype(jnp.int32)
        src, off = lanes_of(fb, own_blocks)
        w_ref[src, :, pl.ds(off, LANES)] = fixed.astype(jnp.int16)
        r = tn(z, v_block(fb))
        sums = []
        for q in range(2):
            total = None
            for jj in range(jj_total):
                begin = (q * jj_total + jj) * irec
                part = r[begin : begin + irec, jj * LANES : (jj + 1) * LANES]
                total = part if total is None else total + part
            sums.append(total)
        crossed = jnp.where(
            first_part, -pltpu.roll(sums[1], LANES - S, 1), pltpu.roll(sums[1], S, 1)
        )
        quarter, off = lanes_of(fb, quarter_blocks)
        r_ref[quarter, :, pl.ds(off, LANES)] = sums[0] + crossed
        return 0

    lax.fori_loop(0, blocks, backward, 0, unroll=16)

    for src in range(src_total):
        codes = code_ref[src * own_blocks : (src + 1) * own_blocks, :]
        codes = jnp.concatenate(
            [codes, jnp.zeros((col_total - own_blocks, LANES), jnp.float32)], axis=0
        )
        w_ref[src, :, k_own:] = codes.astype(jnp.int32).astype(jnp.int16)


def join_kernel(got_ref, count_ref, out_ref):
    src_total, cols, width = got_ref.shape
    k_own, col_total = out_ref.shape
    members = col_total // cols
    seg_ids = lax.broadcasted_iota(jnp.int32, (LANES, col_total), 0) % S
    inside = seg_ids < count_ref[...]
    scales = []
    for src in range(src_total):
        codes = got_ref[src, :16, k_own:].astype(jnp.int32).astype(jnp.float32)
        scales.append(jnp.exp2(codes) * (1.0 / FIXED))
    for b in range(k_own // LANES):
        rows = []
        for m in range(members):
            total = None
            for src in range(m, src_total, members):
                part = got_ref[src, :, b * LANES : (b + 1) * LANES]
                part = part.astype(jnp.int32).astype(jnp.float32) * scales[src][b : b + 1]
                total = part if total is None else total + part
            rows.append(total)
        whole = jnp.concatenate(rows, axis=0).T
        out_ref[b * LANES : (b + 1) * LANES, :] = jnp.where(inside, whole, 0.0)


def swap(x, axis, total, k):
    return lax.ppermute(x, axis, [(r, r ^ k) for r in range(total)])


def shards(
    receiver_spectra,
    reference_spectra,
    receiver_counts,
    reference_counts,
    column_station,
    lag_window,
    observed,
    *,
    rcv_total,
    ref_total,
):
    row_total, k_quarter = receiver_spectra.shape
    k_own, col_total = reference_spectra.shape
    k_total = k_own * rcv_total
    lag_total = observed.shape[2]
    half = lag_total // 2
    members = math.gcd(GROUP, rcv_total)
    irec = row_total * members
    cols = col_total // members
    jj_total = LANES // (2 * irec)
    jp_total = cols // jj_total
    bf16 = jnp.bfloat16
    mine = lax.axis_index("rcv") % members
    quarter = lax.axis_index("ref")

    seg_quarter = jnp.arange(k_quarter, dtype=jnp.int32) % S
    masked = jnp.where(
        seg_quarter[None, :] < receiver_counts[:, None], receiver_spectra, jnp.zeros((), bf16)
    )
    counts = jnp.broadcast_to(receiver_counts.astype(bf16)[:, None], (row_total, LANES))
    own = jnp.concatenate([masked, counts], axis=1)
    near = jnp.concatenate(
        [own] + [swap(own, "rcv", rcv_total, k) for k in range(1, members)], axis=0
    )
    group_counts = near[:, k_quarter].astype(jnp.float32)
    near = near[:, :k_quarter]
    u_all = jnp.stack([near] + [swap(near, "ref", ref_total, k) for k in range(1, ref_total)])

    seg_own = jnp.arange(k_own, dtype=jnp.int32) % S
    turned = reference_spectra.T
    turned = jnp.where(seg_own[None, :] < reference_counts[:, None], turned, jnp.zeros((), bf16))
    sent = jnp.broadcast_to(
        turned.reshape(1, members, cols, k_own), (rcv_total // members, members, cols, k_own)
    ).reshape(rcv_total, cols, k_own)
    v_all = lax.all_to_all(sent, "rcv", split_axis=0, concat_axis=0, tiled=True)

    _, observed, lag_window = lax.optimization_barrier((sent, observed, lag_window))
    local_order = column_station - quarter * col_total
    begin = lag_window[0][..., None]
    end = begin + lag_window[1][..., None]
    lag_ids = jnp.arange(half, dtype=jnp.int32)
    low = (lag_ids >= begin) & (lag_ids < end)
    high = (lag_ids + half >= begin) & (lag_ids + half < end)
    folded = jnp.where(
        low, observed[..., :half], jnp.where(high, -observed[..., half:], jnp.zeros((), bf16))
    )
    pick = (jnp.arange(col_total, dtype=jnp.int32)[:, None] == local_order[None, :]).astype(bf16)
    folded = jnp.transpose(folded, (1, 0, 2)).reshape(col_total, row_total * half)
    folded = jnp.dot(pick, folded, preferred_element_type=jnp.float32).astype(bf16)
    folded = folded.reshape(members, cols, row_total, half)
    share = [lax.dynamic_index_in_dim(folded, mine ^ k, 0, False) for k in range(members)]
    e_all = share[:1] + [swap(share[k], "rcv", rcv_total, k) for k in range(1, members)]

    own_counts = lax.dynamic_slice_in_dim(reference_counts, mine * cols, cols).astype(jnp.float32)
    least = jnp.minimum(
        own_counts.reshape(jj_total, jp_total).T[:, :, None], group_counts[None, None, :]
    )
    inverse = (1.0 / least).reshape(jp_total, jj_total * irec)
    inverse = jnp.concatenate([inverse, inverse], axis=1)

    tables = lag_tables(k_total // (2 * S), lag_total)
    eye = jnp.eye(half, dtype=bf16)
    vmem = pl.BlockSpec(memory_space=pltpu.VMEM)
    w_part, r_part = pl.pallas_call(
        pair_kernel,
        out_shape=(
            jax.ShapeDtypeStruct((rcv_total, cols, k_own + LANES), jnp.int16),
            jax.ShapeDtypeStruct((ref_total, irec, k_quarter), jnp.float32),
        ),
        in_specs=[pl.BlockSpec(memory_space=pltpu.SMEM)] + [vmem] * (8 + members),
        out_specs=[vmem] * 2,
        scratch_shapes=[
            pltpu.VMEM((jp_total * k_total // (2 * S), LANES), jnp.float32),
            pltpu.VMEM((2, irec, k_total), bf16),
            pltpu.VMEM((k_total // LANES, LANES), jnp.float32),
        ],
        compiler_params=pltpu.CompilerParams(vmem_limit_bytes=48 * 1024 * 1024),
    )(quarter.reshape(1).astype(jnp.int32), v_all, u_all, inverse, eye, *tables, *e_all)

    got = lax.all_to_all(w_part, "rcv", split_axis=0, concat_axis=0, tiled=True)
    reference_grad = pl.pallas_call(
        join_kernel,
        out_shape=jax.ShapeDtypeStruct((k_own, col_total), jnp.float32),
        in_specs=[vmem] * 2,
        out_specs=vmem,
        compiler_params=pltpu.CompilerParams(vmem_limit_bytes=32 * 1024 * 1024),
    )(got, reference_counts.reshape(1, col_total))

    parts = [
        lax.dynamic_index_in_dim(r_part, quarter ^ k, 0, False) for k in range(ref_total)
    ]
    r_sum = parts[0]
    for k in range(1, ref_total):
        r_sum = r_sum + swap(parts[k], "ref", ref_total, k)
    parts = [r_sum[k * row_total : (k + 1) * row_total] for k in range(members)]
    r_sum = parts[0]
    for k in range(1, members):
        r_sum = r_sum + swap(parts[k], "rcv", rcv_total, k)
    receiver_grad = jnp.where(seg_quarter[None, :] < receiver_counts[:, None], r_sum, 0.0)
    return (receiver_grad, reference_grad)


def solution(mesh):
    return jax.shard_map(
        functools.partial(shards, rcv_total=mesh.shape["rcv"], ref_total=mesh.shape["ref"]),
        mesh=mesh,
        in_specs=(
            P("rcv", "ref"),
            P("rcv", "ref"),
            P("rcv"),
            P("ref"),
            P("ref"),
            P(None, "rcv", "ref"),
            P("rcv", "ref", None),
        ),
        out_specs=(P("rcv", "ref"), P("rcv", "ref")),
        check_vma=False,
    )
```

```python
import functools
import math

import jax
import jax.numpy as jnp
import numpy as np
from jax import lax
from jax.experimental import pallas as pl
from jax.experimental.pallas import tpu as pltpu
from jax.sharding import PartitionSpec as P

L = 512
S = 16
F = 256

env_floor = 0.05
misfit_scale = 0.03125
GROUP = 4
LANES = 128
FB = LANES // (2 * S)
WIDTH = 8
CHUNKS = 2
MOST_SWAPS = 8
FIXED = 32000.0


def lag_tables(freq_total, lag_total):
    half = lag_total // 2
    freq_ids = np.arange(freq_total)[:, None]
    phase = 2.0 * np.pi * (freq_ids * np.arange(half)[None, :] % lag_total) / lag_total
    cosine = np.cos(phase) / math.sqrt(freq_total)
    sine = np.sin(phase) / math.sqrt(freq_total)
    back = [np.concatenate([cosine[p::2], sine[p::2]], axis=1) for p in (0, 1)]
    ahead = [np.concatenate([cosine[p::2].T, sine[p::2].T], axis=1) for p in (0, 1)]
    return [jnp.asarray(t.astype(np.float32)).astype(jnp.bfloat16) for t in ahead + back]


def nt(a, b):
    return lax.dot_general(a, b, (((1,), (1,)), ((), ())), preferred_element_type=jnp.float32)


def nn(a, b):
    return jnp.dot(a, b, preferred_element_type=jnp.float32)


def tn(a, b):
    return lax.dot_general(a, b, (((0,), (0,)), ((), ())), preferred_element_type=jnp.float32)


def prepare_kernel(spectra_ref, counts_ref, rspectra_ref, rcounts_ref, eye_ref, u_ref, *v_refs):
    k_own, col_total = spectra_ref.shape
    chunk_total = len(v_refs)
    rcv_total, cols, _ = v_refs[0].shape
    members = col_total // (cols * chunk_total)
    width = min(k_own, 2 * LANES)
    counts = counts_ref[...]
    for begin in range(0, k_own, width):
        seg_ids = lax.broadcasted_iota(jnp.int32, (width, col_total), 0) % S
        part = spectra_ref[begin : begin + width, :].astype(jnp.float32)
        part = jnp.where(seg_ids < counts, part, 0.0).astype(jnp.bfloat16)
        turned = nt(eye_ref[...], part).astype(jnp.bfloat16)
        for c in range(chunk_total):
            for m in range(members):
                first = (m * chunk_total + c) * cols
                rows = turned[first : first + cols]
                for dest in range(m, rcv_total, members):
                    v_refs[c][dest, :, begin : begin + width] = rows
    rows, quarter = rspectra_ref.shape
    seg_ids = lax.broadcasted_iota(jnp.int32, (rows, quarter), 1) % S
    part = rspectra_ref[...].astype(jnp.float32)
    part = jnp.where(seg_ids < rcounts_ref[...], part, 0.0)
    u_ref[:, :quarter] = part.astype(jnp.bfloat16)
    u_ref[:, quarter:] = jnp.broadcast_to(rcounts_ref[...], (rows, LANES)).astype(
        jnp.float32
    ).astype(jnp.bfloat16)


def fold_kernel(c_ref, observed_ref, window_ref, order_ref, *rest):
    *out_refs, line_ref = rest
    row_total, col_total, lag_total = observed_ref.shape
    half = lag_total // 2
    cols = out_refs[0].shape[0]
    members = col_total // (cols * CHUNKS)
    window = jnp.concatenate([window_ref[0], window_ref[1]], axis=0).astype(jnp.float32).T
    station = lax.broadcasted_iota(jnp.int32, (col_total, col_total), 0) + c_ref[1]
    pick = jnp.where(station == order_ref[...], 1.0, 0.0).astype(jnp.bfloat16)
    lag_ids = lax.broadcasted_iota(jnp.int32, (col_total, half), 1).astype(jnp.float32)
    lines = col_total * row_total
    for i in range(row_total):
        begin = window[:, i : i + 1]
        end = begin + window[:, row_total + i : row_total + i + 1]
        values = observed_ref[i].astype(jnp.float32)
        low = (lag_ids >= begin) & (lag_ids < end)
        high = (lag_ids + half >= begin) & (lag_ids + half < end)
        folded = jnp.where(low, values[:, :half], jnp.where(high, -values[:, half:], 0.0))
        moved = nn(pick, folded.astype(jnp.bfloat16))
        for h in range(half // LANES):
            line_ref[pl.ds(h * lines + i, col_total, stride=row_total), :] = moved[
                :, h * LANES : (h + 1) * LANES
            ]
    mine = c_ref[0]
    for c in range(CHUNKS):
        for k in range(members):
            first = ((mine ^ k) * CHUNKS + c) * (cols * row_total)
            for h in range(half // LANES):
                begin = pl.multiple_of(h * lines + first, cols * row_total)
                rows = line_ref[pl.ds(begin, cols * row_total), :]
                out_refs[c * members + k][:, :, h * LANES : (h + 1) * LANES] = rows.reshape(
                    cols, row_total, LANES
                ).astype(jnp.bfloat16)


def pair_kernel(n_v, n_e, n_r, *refs):
    refs = list(refs)

    def take(n):
        taken = refs[:n]
        del refs[:n]
        return taken

    (c_ref, invn_ref, eye_ref, ye_ref, yo_ref, ze_ref, zo_ref) = take(7)
    v_from, e_from, u_from = take(n_v), take(n_e), take(n_r)
    r_from = take(n_r) if len(refs) > n_r + 8 else []
    (w_ref,) = take(1)
    r_to = take(n_r)
    x_ref, urow_ref, code_ref, v_ref, e_ref, r_ref, sems = refs

    src_total, col_total, k_own = v_ref.shape
    ref_total, irec, k_quarter = r_ref.shape
    jj_total = LANES // (2 * irec)
    jp_total = col_total // jj_total
    k_total = src_total * k_own
    half_f = k_total // (4 * S)
    freq_total = 2 * half_f
    blocks = k_total // LANES
    own_blocks = k_own // LANES
    quarter_blocks = k_quarter // LANES

    me = c_ref[2]
    quarter_me = c_ref[3]
    v_copies, u_copies, e_copies, r_copies = [], [], [], []

    def fetch(copies, src, dst):
        slot = sum(map(len, (v_copies, u_copies, e_copies, r_copies)))
        copy = pltpu.make_async_copy(src, dst, sems.at[slot])
        copy.start()
        copies.append(copy)

    for k, ref in enumerate(u_from):
        begin = pl.multiple_of((quarter_me ^ k) * k_quarter, k_quarter)
        fetch(u_copies, ref, urow_ref.at[0, :, pl.ds(begin, k_quarter)])
    for k, ref in enumerate(v_from):
        fetch(v_copies, ref, v_ref if n_v == 1 else v_ref.at[me ^ k])
    for k, ref in enumerate(e_from):
        fetch(e_copies, ref, e_ref.at[k])
    for k, ref in enumerate(r_from):
        fetch(r_copies, ref, r_ref.at[quarter_me ^ k])

    group_ids = lax.broadcasted_iota(jnp.int32, (jp_total, LANES), 1) // (2 * S)
    first_part = lax.broadcasted_iota(jnp.int32, (irec, LANES), 1) % (2 * S) < S

    def lanes_of(fb, per):
        return fb // per, pl.multiple_of(fb % per * LANES, LANES)

    def v_block(fb):
        src, off = lanes_of(fb, own_blocks)
        parts = [
            v_ref[src, jj * jp_total : (jj + 1) * jp_total, pl.ds(off, LANES)]
            for jj in range(jj_total)
        ]
        zero = jnp.zeros((jp_total, LANES), jnp.bfloat16)
        rows = [
            jnp.concatenate([jnp.where(group_ids == f, part, zero) for part in parts], axis=1)
            for f in range(FB)
        ]
        return jnp.concatenate(rows, axis=0)

    def u_block(parts):
        zero = jnp.zeros((irec, LANES), jnp.bfloat16)
        return jnp.concatenate(
            [
                jnp.concatenate([part if k == jj else zero for k in range(jj_total)], axis=1)
                for part in parts
                for jj in range(jj_total)
            ],
            axis=0,
        )

    def place(fb, f):
        return pl.ds((f % 2) * half_f + fb * (FB // 2) + f // 2, jp_total, stride=freq_total)

    def forward(fb, _):
        lanes = pl.ds(pl.multiple_of(fb * LANES, LANES), LANES)
        part = urow_ref[0, :, lanes]
        wide = part.astype(jnp.float32)
        crossed = jnp.where(first_part, pltpu.roll(wide, LANES - S, 1), -pltpu.roll(wide, S, 1))
        crossed = crossed.astype(jnp.bfloat16)
        urow_ref[1, :, lanes] = crossed
        out = nt(v_block(fb), u_block([part, crossed]))
        scale = invn_ref[...]
        for f in range(FB):
            x_ref[place(fb, f), :] = out[f * jp_total : (f + 1) * jp_total] * scale
        return 0

    for copy in u_copies + v_copies:
        copy.wait()
    lax.fori_loop(0, blocks, forward, 0, unroll=16)

    lane_ids = lax.broadcasted_iota(jnp.int32, (1, LANES), 1)
    sign = jnp.where(lane_ids < LANES // 2, -1.0, 1.0).astype(jnp.float32)

    def pairs(step, _):
        cols = [step * WIDTH + k for k in range(WIDTH)]
        rhs_e, rhs_o, obs = [], [], []
        for jp in cols:
            x = x_ref[pl.ds(pl.multiple_of(jp * freq_total, freq_total), freq_total), :]
            x = x.astype(jnp.bfloat16).astype(jnp.float32)
            turned = pltpu.roll(x, LANES // 2, 1) * sign
            rhs_e.append(jnp.concatenate([x[:half_f], turned[:half_f]], axis=0))
            rhs_o.append(jnp.concatenate([x[half_f:], turned[half_f:]], axis=0))
            rows = [
                e_ref[k, jj * jp_total + jp].astype(jnp.float32)
                for jj in range(jj_total)
                for k in range(n_e)
            ]
            obs.append(jnp.concatenate(rows * 2, axis=0))
        rhs_e = jnp.concatenate(rhs_e, axis=1).astype(jnp.bfloat16)
        rhs_o = jnp.concatenate(rhs_o, axis=1).astype(jnp.bfloat16)
        even = nn(ye_ref[...], rhs_e)
        odd = nn(yo_ref[...], rhs_o)
        seen = nt(eye_ref[...], jnp.concatenate(obs, axis=0).astype(jnp.bfloat16))
        g_e, g_o = [], []
        for k in range(WIDTH):
            lanes = slice(k * LANES, (k + 1) * LANES)
            e, d0, d1 = seen[:, lanes], even[:, lanes], odd[:, lanes]
            high = e < 0.0
            d = d0 + jnp.where(high, d1, -d1)
            power = d * d
            power = power + pltpu.roll(power, LANES // 2, 1) + env_floor
            g = d * (1.0 - jnp.abs(e) * lax.rsqrt(power)) * misfit_scale
            g = jnp.where(e == 0.0, 0.0, g)
            turned = -pltpu.roll(g, LANES // 2, 1) * sign
            g_e.append(jnp.concatenate([g, turned], axis=0))
            g_o.append(
                jnp.concatenate([jnp.where(high, g, -g), jnp.where(high, turned, -turned)], axis=0)
            )
        z_e = nn(ze_ref[...], jnp.concatenate(g_e, axis=1).astype(jnp.bfloat16))
        z_o = nn(zo_ref[...], jnp.concatenate(g_o, axis=1).astype(jnp.bfloat16))
        for k, jp in enumerate(cols):
            lanes = slice(k * LANES, (k + 1) * LANES)
            scale = invn_ref[pl.ds(jp, 1), :]
            base = pl.multiple_of(jp * freq_total, freq_total)
            x_ref[pl.ds(base, half_f), :] = z_e[:, lanes] * scale
            x_ref[pl.ds(base + half_f, half_f), :] = z_o[:, lanes] * scale
        return 0

    for copy in e_copies:
        copy.wait()
    lax.fori_loop(0, jp_total // WIDTH, pairs, 0)

    def backward(fb, _):
        z = jnp.concatenate([x_ref[place(fb, f), :] for f in range(FB)], axis=0)
        z = z.astype(jnp.bfloat16)
        lanes = pl.ds(pl.multiple_of(fb * LANES, LANES), LANES)
        w = nn(z, u_block([urow_ref[q, :, lanes] for q in range(2)]))
        totals = []
        for jj in range(jj_total):
            lanes = slice(jj * LANES, (jj + 1) * LANES)
            total = w[:jp_total, lanes]
            for f in range(1, FB):
                total = jnp.where(group_ids == f, w[f * jp_total : (f + 1) * jp_total, lanes], total)
            totals.append(total)
        total = jnp.concatenate(totals, axis=0)
        largest = jnp.max(jnp.abs(total), axis=0, keepdims=True)
        power = jnp.ceil(jnp.log2(jnp.maximum(largest, 1e-30)))
        code_ref[pl.ds(fb, 1), :] = power
        fixed = jnp.round(total * (jnp.exp2(-power) * FIXED)).astype(jnp.int32)
        src, off = lanes_of(fb, own_blocks)
        w_ref[src, :, pl.ds(off, LANES)] = fixed.astype(jnp.int16)
        r = tn(z, v_block(fb))
        sums = []
        for q in range(2):
            total = None
            for jj in range(jj_total):
                begin = (q * jj_total + jj) * irec
                part = r[begin : begin + irec, jj * LANES : (jj + 1) * LANES]
                total = part if total is None else total + part
            sums.append(total)
        crossed = jnp.where(
            first_part, -pltpu.roll(sums[1], LANES - S, 1), pltpu.roll(sums[1], S, 1)
        )
        quarter, off = lanes_of(fb, quarter_blocks)
        lanes = pl.ds(off, LANES)
        total = sums[0] + crossed
        r_ref[quarter, :, lanes] = r_ref[quarter, :, lanes] + total if r_from else total
        return 0

    for copy in r_copies:
        copy.wait()
    lax.fori_loop(0, blocks, backward, 0, unroll=16)
    outs = [
        pltpu.make_async_copy(r_ref.at[quarter_me ^ k], ref, sems.at[k])
        for k, ref in enumerate(r_to)
    ]
    for copy in outs:
        copy.start()

    for src in range(src_total):
        codes = code_ref[src * own_blocks : (src + 1) * own_blocks, :]
        codes = jnp.concatenate(
            [codes, jnp.zeros((col_total - own_blocks, LANES), jnp.float32)], axis=0
        )
        w_ref[src, :, k_own:] = codes.astype(jnp.int32).astype(jnp.int16)
    for copy in outs:
        copy.wait()


def join_kernel(count_ref, *refs):
    *got_refs, out_ref = refs
    src_total, cols, _ = got_refs[0].shape
    k_own, col_total = out_ref.shape
    members = col_total // (cols * len(got_refs))
    seg_ids = lax.broadcasted_iota(jnp.int32, (LANES, col_total), 0) % S
    inside = seg_ids < count_ref[...]
    scales = [
        [
            jnp.exp2(ref[src, :16, k_own:].astype(jnp.int32).astype(jnp.float32)) * (1.0 / FIXED)
            for src in range(src_total)
        ]
        for ref in got_refs
    ]
    for b in range(k_own // LANES):
        rows = []
        for m in range(members):
            for ref, scale in zip(got_refs, scales):
                total = None
                for src in range(m, src_total, members):
                    part = ref[src, :, b * LANES : (b + 1) * LANES]
                    part = part.astype(jnp.int32).astype(jnp.float32) * scale[src][b : b + 1]
                    total = part if total is None else total + part
                rows.append(total)
        whole = jnp.concatenate(rows, axis=0).T
        out_ref[b * LANES : (b + 1) * LANES, :] = jnp.where(inside, whole, 0.0)


def swap(x, axis, total, k):
    return lax.ppermute(x, axis, [(r, r ^ k) for r in range(total)])


def shards(
    receiver_spectra,
    reference_spectra,
    receiver_counts,
    reference_counts,
    column_station,
    lag_window,
    observed,
    *,
    rcv_total,
    ref_total,
):
    row_total, k_quarter = receiver_spectra.shape
    k_own, col_total = reference_spectra.shape
    k_total = k_own * rcv_total
    lag_total = observed.shape[2]
    half = lag_total // 2
    members = math.gcd(GROUP, rcv_total)
    irec = row_total * members
    cols = col_total // (members * CHUNKS)
    jj_total = LANES // (2 * irec)
    jp_total = cols // jj_total
    bf16 = jnp.bfloat16
    place = lax.axis_index("rcv")
    mine = place % members
    quarter = lax.axis_index("ref")
    vmem = pl.BlockSpec(memory_space=pltpu.VMEM)
    smem = pl.BlockSpec(memory_space=pltpu.SMEM)
    hbm = pl.BlockSpec(memory_space=pl.ANY)
    scalars = jnp.stack([mine, quarter * col_total, place, quarter]).astype(jnp.int32)

    def params(mib):
        return pltpu.CompilerParams(vmem_limit_bytes=mib * 1024 * 1024)

    def cost(us):
        return pl.CostEstimate(flops=us * 10**9, bytes_accessed=0, transcendentals=0)

    u_own, *sent = pl.pallas_call(
        prepare_kernel,
        out_shape=[jax.ShapeDtypeStruct((row_total, k_quarter + LANES), bf16)]
        + [jax.ShapeDtypeStruct((rcv_total, cols, k_own), bf16)] * CHUNKS,
        in_specs=[vmem] * 5,
        out_specs=[vmem] * (1 + CHUNKS),
        compiler_params=params(24),
    )(
        reference_spectra,
        reference_counts.reshape(1, col_total),
        receiver_spectra,
        receiver_counts.reshape(row_total, 1),
        jnp.eye(col_total, dtype=bf16),
    )

    def spread(x):
        if rcv_total > MOST_SWAPS:
            return [lax.all_to_all(x, "rcv", split_axis=0, concat_axis=0, tiled=True)]
        parts = [lax.dynamic_index_in_dim(x, place ^ k, 0, False) for k in range(rcv_total)]
        return parts[:1] + [swap(parts[k], "rcv", rcv_total, k) for k in range(1, rcv_total)]

    v_all = [spread(x) for x in sent]

    near = jnp.concatenate(
        [u_own] + [swap(u_own, "rcv", rcv_total, k) for k in range(1, members)], axis=0
    )
    group_counts = near[:, k_quarter].astype(jnp.float32)
    near = near[:, :k_quarter]
    u_all = [near] + [swap(near, "ref", ref_total, k) for k in range(1, ref_total)]

    folded = pl.pallas_call(
        fold_kernel,
        out_shape=[jax.ShapeDtypeStruct((cols, row_total, half), bf16)] * (CHUNKS * members),
        in_specs=[smem] + [vmem] * 3,
        out_specs=[vmem] * (CHUNKS * members),
        scratch_shapes=[pltpu.VMEM((half // LANES * col_total * row_total, LANES), jnp.float32)],
        compiler_params=params(32),
        cost_estimate=cost(4),
    )(scalars, observed, lag_window, column_station.reshape(1, col_total))
    e_all = [
        [
            x if k == 0 else swap(x, "rcv", rcv_total, k)
            for k, x in enumerate(folded[c * members : (c + 1) * members])
        ]
        for c in range(CHUNKS)
    ]

    tables = lag_tables(k_total // (2 * S), lag_total)
    eye = jnp.eye(half, dtype=bf16)
    own_counts = lax.dynamic_slice_in_dim(
        reference_counts, mine * (cols * CHUNKS), cols * CHUNKS
    ).astype(jnp.float32)
    r_all, got = [], []
    for c in range(CHUNKS):
        counts = own_counts[c * cols : (c + 1) * cols].reshape(jj_total, jp_total).T
        least = jnp.minimum(counts[:, :, None], group_counts[None, None, :])
        inverse = (1.0 / least).reshape(jp_total, jj_total * irec)
        inverse = jnp.concatenate([inverse, inverse], axis=1)
        operands = v_all[c] + e_all[c] + u_all + r_all
        w_part, *r_all = pl.pallas_call(
            functools.partial(pair_kernel, len(v_all[c]), members, ref_total),
            out_shape=[jax.ShapeDtypeStruct((rcv_total, cols, k_own + LANES), jnp.int16)]
            + [jax.ShapeDtypeStruct((irec, k_quarter), jnp.float32)] * ref_total,
            in_specs=[smem] + [vmem] * 6 + [hbm] * len(operands),
            out_specs=[vmem] + [hbm] * ref_total,
            scratch_shapes=[
                pltpu.VMEM((jp_total * k_total // (2 * S), LANES), jnp.float32),
                pltpu.VMEM((2, irec, k_total), bf16),
                pltpu.VMEM((k_total // LANES, LANES), jnp.float32),
                pltpu.VMEM((rcv_total, cols, k_own), bf16),
                pltpu.VMEM((members, cols, row_total, half), bf16),
                pltpu.VMEM((ref_total, irec, k_quarter), jnp.float32),
                pltpu.SemaphoreType.DMA((len(operands),)),
            ],
            compiler_params=params(48),
            cost_estimate=cost(10),
        )(scalars, inverse, eye, *tables, *operands)
        got.append(lax.all_to_all(w_part, "rcv", split_axis=0, concat_axis=0, tiled=True))

    reference_grad = pl.pallas_call(
        join_kernel,
        out_shape=jax.ShapeDtypeStruct((k_own, col_total), jnp.float32),
        in_specs=[vmem] * (1 + CHUNKS),
        out_specs=vmem,
        compiler_params=params(32),
    )(reference_counts.reshape(1, col_total), *got)

    r_sum = r_all[0]
    for k in range(1, ref_total):
        r_sum = r_sum + swap(r_all[k], "ref", ref_total, k)
    parts = [r_sum[k * row_total : (k + 1) * row_total] for k in range(members)]
    r_sum = parts[0]
    for k in range(1, members):
        r_sum = r_sum + swap(parts[k], "rcv", rcv_total, k)
    seg_quarter = jnp.arange(k_quarter, dtype=jnp.int32) % S
    receiver_grad = jnp.where(seg_quarter[None, :] < receiver_counts[:, None], r_sum, 0.0)
    return (receiver_grad, reference_grad)


def solution(mesh):
    return jax.shard_map(
        functools.partial(shards, rcv_total=mesh.shape["rcv"], ref_total=mesh.shape["ref"]),
        mesh=mesh,
        in_specs=(
            P("rcv", "ref"),
            P("rcv", "ref"),
            P("rcv"),
            P("ref"),
            P("ref"),
            P(None, "rcv", "ref"),
            P("rcv", "ref", None),
        ),
        out_specs=(P("rcv", "ref"), P("rcv", "ref")),
        check_vma=False,
    )
```

```python
import functools
import math

import jax
import jax.numpy as jnp
import numpy as np
from jax import lax
from jax.experimental import pallas as pl
from jax.experimental.pallas import tpu as pltpu
from jax.sharding import PartitionSpec as P

L = 512
S = 16
F = 256

env_floor = 0.05
misfit_scale = 0.03125
GROUP = 4
LANES = 128
FB = LANES // (2 * S)
WIDTH = 8
CHUNKS = 1
MOST_SWAPS = 1
FIXED = 32000.0


def lag_tables(freq_total, lag_total):
    half = lag_total // 2
    freq_ids = np.arange(freq_total)[:, None]
    phase = 2.0 * np.pi * (freq_ids * np.arange(half)[None, :] % lag_total) / lag_total
    cosine = np.cos(phase) / math.sqrt(freq_total)
    sine = np.sin(phase) / math.sqrt(freq_total)
    back = [np.concatenate([cosine[p::2], sine[p::2]], axis=1) for p in (0, 1)]
    ahead = [np.concatenate([cosine[p::2].T, sine[p::2].T], axis=1) for p in (0, 1)]
    return [jnp.asarray(t.astype(np.float32)).astype(jnp.bfloat16) for t in ahead + back]


def nt(a, b):
    return lax.dot_general(a, b, (((1,), (1,)), ((), ())), preferred_element_type=jnp.float32)


def nn(a, b):
    return jnp.dot(a, b, preferred_element_type=jnp.float32)


def tn(a, b):
    return lax.dot_general(a, b, (((0,), (0,)), ((), ())), preferred_element_type=jnp.float32)


def prepare_kernel(
    spectra_from, counts_ref, rspectra_ref, rcounts_ref, eye_ref, u_ref, *rest
):
    *v_to, spectra_ref, turned_ref, in_sems, out_sems = rest
    k_own, col_total = spectra_ref.shape
    chunk_total = len(v_to)
    rcv_total, cols, _ = v_to[0].shape
    members = col_total // (cols * chunk_total)
    width = min(k_own, 2 * LANES)
    copies = []
    for n, begin in enumerate(range(0, k_own, width)):
        rows = pl.ds(begin, width)
        copies.append(
            pltpu.make_async_copy(spectra_from.at[rows], spectra_ref.at[rows], in_sems.at[n])
        )
        copies[-1].start()
    rows, quarter = rspectra_ref.shape
    seg_ids = lax.broadcasted_iota(jnp.int32, (rows, quarter), 1) % S
    part = rspectra_ref[...].astype(jnp.float32)
    part = jnp.where(seg_ids < rcounts_ref[...], part, 0.0)
    u_ref[:, :quarter] = part.astype(jnp.bfloat16)
    u_ref[:, quarter:] = jnp.broadcast_to(rcounts_ref[...], (rows, LANES)).astype(
        jnp.float32
    ).astype(jnp.bfloat16)
    counts = counts_ref[...]
    seg_ids = lax.broadcasted_iota(jnp.int32, (width, col_total), 0) % S
    for n, begin in enumerate(range(0, k_own, width)):
        copies[n].wait()
        part = spectra_ref[begin : begin + width, :].astype(jnp.float32)
        part = jnp.where(seg_ids < counts, part, 0.0).astype(jnp.bfloat16)
        turned_ref[:, begin : begin + width] = nt(eye_ref[...], part).astype(jnp.bfloat16)
    copies = []
    for c in range(chunk_total):
        for dest in range(rcv_total):
            first = (dest % members * chunk_total + c) * cols
            copies.append(
                pltpu.make_async_copy(
                    turned_ref.at[pl.ds(first, cols)],
                    v_to[c].at[dest],
                    out_sems.at[c * rcv_total + dest],
                )
            )
            copies[-1].start()
    for copy in copies:
        copy.wait()


def fold_kernel(c_ref, observed_from, window_ref, order_ref, *rest):
    *out_refs, observed_ref, line_ref, sems = rest
    row_total, col_total, lag_total = observed_ref.shape
    half = lag_total // 2
    cols = out_refs[0].shape[0]
    members = col_total // (cols * CHUNKS)
    window = jnp.concatenate([window_ref[0], window_ref[1]], axis=0).astype(jnp.float32).T
    station = lax.broadcasted_iota(jnp.int32, (col_total, col_total), 0) + c_ref[1]
    pick = jnp.where(station == order_ref[...], 1.0, 0.0).astype(jnp.bfloat16)
    lag_ids = lax.broadcasted_iota(jnp.int32, (col_total, half), 1).astype(jnp.float32)
    lines = col_total * row_total
    copies = [
        pltpu.make_async_copy(observed_from.at[i], observed_ref.at[i], sems.at[i])
        for i in range(row_total)
    ]
    for copy in copies:
        copy.start()
    for i in range(row_total):
        copies[i].wait()
        begin = window[:, i : i + 1]
        end = begin + window[:, row_total + i : row_total + i + 1]
        values = observed_ref[i].astype(jnp.float32)
        low = (lag_ids >= begin) & (lag_ids < end)
        high = (lag_ids + half >= begin) & (lag_ids + half < end)
        folded = jnp.where(low, values[:, :half], jnp.where(high, -values[:, half:], 0.0))
        moved = nn(pick, folded.astype(jnp.bfloat16))
        for h in range(half // LANES):
            line_ref[pl.ds(h * lines + i, col_total, stride=row_total), :] = moved[
                :, h * LANES : (h + 1) * LANES
            ]
    mine = c_ref[0]
    for c in range(CHUNKS):
        for k in range(members):
            first = ((mine ^ k) * CHUNKS + c) * (cols * row_total)
            for h in range(half // LANES):
                begin = pl.multiple_of(h * lines + first, cols * row_total)
                rows = line_ref[pl.ds(begin, cols * row_total), :]
                out_refs[c * members + k][:, :, h * LANES : (h + 1) * LANES] = rows.reshape(
                    cols, row_total, LANES
                ).astype(jnp.bfloat16)


def pair_kernel(n_v, n_e, n_r, *refs):
    refs = list(refs)

    def take(n):
        taken = refs[:n]
        del refs[:n]
        return taken

    (c_ref, invn_ref, eye_ref, ye_ref, yo_ref, ze_ref, zo_ref) = take(7)
    v_from, e_from, u_from = take(n_v), take(n_e), take(n_r)
    r_from = take(n_r) if len(refs) > n_r + 12 else []
    (w_to,) = take(1)
    r_to = take(n_r)
    x_ref, z_ref, u_ref, turned_ref, code_ref, v_ref, e_ref, r_ref, w_ref, sems, w_sems = refs

    src_total, col_total, k_own = v_ref.shape
    ref_total, irec, k_quarter = r_ref.shape
    jj_total = LANES // (2 * irec)
    jp_total = col_total // jj_total
    k_total = src_total * k_own
    half_f = k_total // (4 * S)
    freq_total = 2 * half_f
    blocks = k_total // LANES
    own_blocks = k_own // LANES
    quarter_blocks = k_quarter // LANES

    me = c_ref[2]
    quarter_me = c_ref[3]
    v_copies, u_copies, e_copies, r_copies = [], [], [], []

    def fetch(copies, src, dst):
        slot = sum(map(len, (v_copies, u_copies, e_copies, r_copies)))
        copy = pltpu.make_async_copy(src, dst, sems.at[slot])
        copy.start()
        copies.append(copy)

    for k, ref in enumerate(u_from):
        begin = pl.multiple_of((quarter_me ^ k) * k_quarter, k_quarter)
        fetch(u_copies, ref, u_ref.at[:, pl.ds(begin, k_quarter)])
    for k, ref in enumerate(v_from):
        fetch(v_copies, ref, v_ref if n_v == 1 else v_ref.at[me ^ k])
    for k, ref in enumerate(e_from):
        fetch(e_copies, ref, e_ref.at[k])
    for k, ref in enumerate(r_from):
        fetch(r_copies, ref, r_ref.at[quarter_me ^ k])

    group_ids = lax.broadcasted_iota(jnp.int32, (jp_total, LANES), 1) // (2 * S)
    first_part = lax.broadcasted_iota(jnp.int32, (irec, LANES), 1) % (2 * S) < S

    def lanes_of(fb, per):
        return fb // per, pl.multiple_of(fb % per * LANES, LANES)

    def v_block(fb):
        src, off = lanes_of(fb, own_blocks)
        parts = [
            v_ref[src, jj * jp_total : (jj + 1) * jp_total, pl.ds(off, LANES)]
            for jj in range(jj_total)
        ]
        zero = jnp.zeros((jp_total, LANES), jnp.bfloat16)
        rows = [
            jnp.concatenate([jnp.where(group_ids == f, part, zero) for part in parts], axis=1)
            for f in range(FB)
        ]
        return jnp.concatenate(rows, axis=0)

    def u_block(parts):
        zero = jnp.zeros((irec, LANES), jnp.bfloat16)
        return jnp.concatenate(
            [
                jnp.concatenate([part if k == jj else zero for k in range(jj_total)], axis=1)
                for part in parts
                for jj in range(jj_total)
            ],
            axis=0,
        )

    def place(fb, f):
        return pl.ds((f % 2) * half_f + fb * (FB // 2) + f // 2, jp_total, stride=freq_total)

    def forward(fb, _):
        lanes = pl.ds(pl.multiple_of(fb * LANES, LANES), LANES)
        part = u_ref[:, lanes]
        wide = part.astype(jnp.float32)
        crossed = jnp.where(first_part, pltpu.roll(wide, LANES - S, 1), -pltpu.roll(wide, S, 1))
        crossed = crossed.astype(jnp.bfloat16)
        turned_ref[:, lanes] = crossed
        out = nt(v_block(fb), u_block([part, crossed]))
        scale = invn_ref[...]
        for f in range(FB):
            x_ref[place(fb, f), :] = out[f * jp_total : (f + 1) * jp_total] * scale
        return 0

    for copy in u_copies + v_copies:
        copy.wait()
    lax.fori_loop(0, blocks, forward, 0, unroll=16)

    lane_ids = lax.broadcasted_iota(jnp.int32, (1, LANES), 1)
    sign = jnp.where(lane_ids < LANES // 2, -1.0, 1.0).astype(jnp.float32)

    def pairs(step, _):
        cols = [step * WIDTH + k for k in range(WIDTH)]
        rhs_e, rhs_o, obs = [], [], []
        for jp in cols:
            x = x_ref[pl.ds(pl.multiple_of(jp * freq_total, freq_total), freq_total), :]
            x = x.astype(jnp.bfloat16).astype(jnp.float32)
            turned = pltpu.roll(x, LANES // 2, 1) * sign
            rhs_e.append(jnp.concatenate([x[:half_f], turned[:half_f]], axis=0))
            rhs_o.append(jnp.concatenate([x[half_f:], turned[half_f:]], axis=0))
            rows = [
                e_ref[k, jj * jp_total + jp].astype(jnp.float32)
                for jj in range(jj_total)
                for k in range(n_e)
            ]
            obs.append(jnp.concatenate(rows * 2, axis=0))
        rhs_e = jnp.concatenate(rhs_e, axis=1).astype(jnp.bfloat16)
        rhs_o = jnp.concatenate(rhs_o, axis=1).astype(jnp.bfloat16)
        even = nn(ye_ref[...], rhs_e)
        odd = nn(yo_ref[...], rhs_o)
        seen = nt(eye_ref[...], jnp.concatenate(obs, axis=0).astype(jnp.bfloat16))
        g_e, g_o = [], []
        for k in range(WIDTH):
            lanes = slice(k * LANES, (k + 1) * LANES)
            e, d0, d1 = seen[:, lanes], even[:, lanes], odd[:, lanes]
            high = e < 0.0
            d = d0 + jnp.where(high, d1, -d1)
            power = d * d
            power = power + pltpu.roll(power, LANES // 2, 1) + env_floor
            g = d * (1.0 - jnp.abs(e) * lax.rsqrt(power)) * misfit_scale
            g = jnp.where(e == 0.0, 0.0, g)
            turned = -pltpu.roll(g, LANES // 2, 1) * sign
            g_e.append(jnp.concatenate([g, turned], axis=0))
            g_o.append(
                jnp.concatenate([jnp.where(high, g, -g), jnp.where(high, turned, -turned)], axis=0)
            )
        z_e = nn(ze_ref[...], jnp.concatenate(g_e, axis=1).astype(jnp.bfloat16))
        z_o = nn(zo_ref[...], jnp.concatenate(g_o, axis=1).astype(jnp.bfloat16))
        for k, jp in enumerate(cols):
            lanes = slice(k * LANES, (k + 1) * LANES)
            scale = invn_ref[pl.ds(jp, 1), :]
            base = pl.multiple_of(jp * freq_total, freq_total)
            z_ref[pl.ds(base, half_f), :] = z_e[:, lanes] * scale
            z_ref[pl.ds(base + half_f, half_f), :] = z_o[:, lanes] * scale
        return 0

    for copy in e_copies:
        copy.wait()
    lax.fori_loop(0, jp_total // WIDTH, pairs, 0)

    def backward(fb):
        z = jnp.concatenate([z_ref[place(fb, f), :] for f in range(FB)], axis=0)
        z = z.astype(jnp.bfloat16)
        lanes = pl.ds(pl.multiple_of(fb * LANES, LANES), LANES)
        w = nn(z, u_block([u_ref[:, lanes], turned_ref[:, lanes]]))
        totals = []
        for jj in range(jj_total):
            lanes = slice(jj * LANES, (jj + 1) * LANES)
            total = w[:jp_total, lanes]
            for f in range(1, FB):
                total = jnp.where(group_ids == f, w[f * jp_total : (f + 1) * jp_total, lanes], total)
            totals.append(total)
        total = jnp.concatenate(totals, axis=0)
        largest = jnp.max(jnp.abs(total), axis=0, keepdims=True)
        power = jnp.ceil(jnp.log2(jnp.maximum(largest, 1e-30)))
        code_ref[pl.ds(fb, 1), :] = power
        fixed = jnp.round(total * (jnp.exp2(-power) * FIXED)).astype(jnp.int32)
        src, off = lanes_of(fb, own_blocks)
        w_ref[src, :, pl.ds(off, LANES)] = fixed.astype(jnp.int16)
        r = tn(z, v_block(fb))
        sums = []
        for q in range(2):
            total = None
            for jj in range(jj_total):
                begin = (q * jj_total + jj) * irec
                part = r[begin : begin + irec, jj * LANES : (jj + 1) * LANES]
                total = part if total is None else total + part
            sums.append(total)
        crossed = jnp.where(
            first_part, -pltpu.roll(sums[1], LANES - S, 1), pltpu.roll(sums[1], S, 1)
        )
        quarter, off = lanes_of(fb, quarter_blocks)
        lanes = pl.ds(off, LANES)
        total = sums[0] + crossed
        r_ref[quarter, :, lanes] = r_ref[quarter, :, lanes] + total if r_from else total

    def w_copy(src):
        return pltpu.make_async_copy(w_ref.at[src], w_to.at[src], w_sems.at[src])

    def from_owner(src, _):
        for b in range(own_blocks):
            backward(src * own_blocks + b)
        codes = code_ref[pl.ds(src * own_blocks, own_blocks), :]
        codes = jnp.concatenate(
            [codes, jnp.zeros((col_total - own_blocks, LANES), jnp.float32)], axis=0
        )
        w_ref[src, :, k_own:] = codes.astype(jnp.int32).astype(jnp.int16)
        w_copy(src).start()
        return 0

    for copy in r_copies:
        copy.wait()
    owners = src_total // ref_total
    outs = []
    for k, ref in enumerate(r_to):
        begin = (quarter_me ^ k) * owners
        lax.fori_loop(begin, begin + owners, from_owner, 0)
        outs.append(pltpu.make_async_copy(r_ref.at[quarter_me ^ k], ref, sems.at[k]))
        outs[-1].start()
    for copy in outs:
        copy.wait()
    for src in range(src_total):
        w_copy(src).wait()


def join_kernel(count_ref, *refs):
    *got_refs, out_ref = refs
    src_total, cols, _ = got_refs[0].shape
    k_own, col_total = out_ref.shape
    members = col_total // (cols * len(got_refs))
    seg_ids = lax.broadcasted_iota(jnp.int32, (LANES, col_total), 0) % S
    inside = seg_ids < count_ref[...]
    scales = [
        [
            jnp.exp2(ref[src, :16, k_own:].astype(jnp.int32).astype(jnp.float32)) * (1.0 / FIXED)
            for src in range(src_total)
        ]
        for ref in got_refs
    ]
    for b in range(k_own // LANES):
        rows = []
        for m in range(members):
            for ref, scale in zip(got_refs, scales):
                total = None
                for src in range(m, src_total, members):
                    part = ref[src, :, b * LANES : (b + 1) * LANES]
                    part = part.astype(jnp.int32).astype(jnp.float32) * scale[src][b : b + 1]
                    total = part if total is None else total + part
                rows.append(total)
        whole = jnp.concatenate(rows, axis=0).T
        out_ref[b * LANES : (b + 1) * LANES, :] = jnp.where(inside, whole, 0.0)


def swap(x, axis, total, k):
    return lax.ppermute(x, axis, [(r, r ^ k) for r in range(total)])


def shards(
    receiver_spectra,
    reference_spectra,
    receiver_counts,
    reference_counts,
    column_station,
    lag_window,
    observed,
    *,
    rcv_total,
    ref_total,
):
    row_total, k_quarter = receiver_spectra.shape
    k_own, col_total = reference_spectra.shape
    k_total = k_own * rcv_total
    lag_total = observed.shape[2]
    half = lag_total // 2
    members = math.gcd(GROUP, rcv_total)
    irec = row_total * members
    cols = col_total // (members * CHUNKS)
    jj_total = LANES // (2 * irec)
    jp_total = cols // jj_total
    bf16 = jnp.bfloat16
    place = lax.axis_index("rcv")
    mine = place % members
    quarter = lax.axis_index("ref")
    vmem = pl.BlockSpec(memory_space=pltpu.VMEM)
    smem = pl.BlockSpec(memory_space=pltpu.SMEM)
    hbm = pl.BlockSpec(memory_space=pl.ANY)
    scalars = jnp.stack([mine, quarter * col_total, place, quarter]).astype(jnp.int32)

    def params(mib):
        return pltpu.CompilerParams(vmem_limit_bytes=mib * 1024 * 1024)

    def cost(us):
        return pl.CostEstimate(flops=us * 10**9, bytes_accessed=0, transcendentals=0)

    u_own, *sent = pl.pallas_call(
        prepare_kernel,
        out_shape=[jax.ShapeDtypeStruct((row_total, k_quarter + LANES), bf16)]
        + [jax.ShapeDtypeStruct((rcv_total, cols, k_own), bf16)] * CHUNKS,
        in_specs=[hbm] + [vmem] * 4,
        out_specs=[vmem] + [hbm] * CHUNKS,
        scratch_shapes=[
            pltpu.VMEM((k_own, col_total), bf16),
            pltpu.VMEM((col_total, k_own), bf16),
            pltpu.SemaphoreType.DMA((k_own // min(k_own, 2 * LANES),)),
            pltpu.SemaphoreType.DMA((CHUNKS * rcv_total,)),
        ],
        compiler_params=params(24),
    )(
        reference_spectra,
        reference_counts.reshape(1, col_total),
        receiver_spectra,
        receiver_counts.reshape(row_total, 1),
        jnp.eye(col_total, dtype=bf16),
    )

    def spread(x):
        if rcv_total > MOST_SWAPS:
            return [lax.all_to_all(x, "rcv", split_axis=0, concat_axis=0, tiled=True)]
        parts = [lax.dynamic_index_in_dim(x, place ^ k, 0, False) for k in range(rcv_total)]
        return parts[:1] + [swap(parts[k], "rcv", rcv_total, k) for k in range(1, rcv_total)]

    v_all = [spread(x) for x in sent]

    near = jnp.concatenate(
        [u_own] + [swap(u_own, "rcv", rcv_total, k) for k in range(1, members)], axis=0
    )
    group_counts = near[:, k_quarter].astype(jnp.float32)
    near = near[:, :k_quarter]
    u_all = [near] + [swap(near, "ref", ref_total, k) for k in range(1, ref_total)]

    folded = pl.pallas_call(
        fold_kernel,
        out_shape=[jax.ShapeDtypeStruct((cols, row_total, half), bf16)] * (CHUNKS * members),
        in_specs=[smem, hbm] + [vmem] * 2,
        out_specs=[vmem] * (CHUNKS * members),
        scratch_shapes=[
            pltpu.VMEM((row_total, col_total, lag_total), bf16),
            pltpu.VMEM((half // LANES * col_total * row_total, LANES), jnp.float32),
            pltpu.SemaphoreType.DMA((row_total,)),
        ],
        compiler_params=params(32),
        cost_estimate=cost(4),
    )(scalars, observed, lag_window, column_station.reshape(1, col_total))
    e_all = [
        [
            x if k == 0 else swap(x, "rcv", rcv_total, k)
            for k, x in enumerate(folded[c * members : (c + 1) * members])
        ]
        for c in range(CHUNKS)
    ]

    tables = lag_tables(k_total // (2 * S), lag_total)
    eye = jnp.eye(half, dtype=bf16)
    own_counts = lax.dynamic_slice_in_dim(
        reference_counts, mine * (cols * CHUNKS), cols * CHUNKS
    ).astype(jnp.float32)
    r_all, got = [], []
    for c in range(CHUNKS):
        counts = own_counts[c * cols : (c + 1) * cols].reshape(jj_total, jp_total).T
        least = jnp.minimum(counts[:, :, None], group_counts[None, None, :])
        inverse = (1.0 / least).reshape(jp_total, jj_total * irec)
        inverse = jnp.concatenate([inverse, inverse], axis=1)
        operands = v_all[c] + e_all[c] + u_all + r_all
        w_part, *r_all = pl.pallas_call(
            functools.partial(pair_kernel, len(v_all[c]), members, ref_total),
            out_shape=[jax.ShapeDtypeStruct((rcv_total, cols, k_own + LANES), jnp.int16)]
            + [jax.ShapeDtypeStruct((irec, k_quarter), jnp.float32)] * ref_total,
            in_specs=[smem] + [vmem] * 6 + [hbm] * len(operands),
            out_specs=[hbm] * (1 + ref_total),
            scratch_shapes=[
                pltpu.VMEM((jp_total * k_total // (2 * S), LANES), jnp.float32),
                pltpu.VMEM((jp_total * k_total // (2 * S), LANES), jnp.float32),
                pltpu.VMEM((irec, k_total), bf16),
                pltpu.VMEM((irec, k_total), bf16),
                pltpu.VMEM((k_total // LANES, LANES), jnp.float32),
                pltpu.VMEM((rcv_total, cols, k_own), bf16),
                pltpu.VMEM((members, cols, row_total, half), bf16),
                pltpu.VMEM((ref_total, irec, k_quarter), jnp.float32),
                pltpu.VMEM((rcv_total, cols, k_own + LANES), jnp.int16),
                pltpu.SemaphoreType.DMA((len(operands),)),
                pltpu.SemaphoreType.DMA((rcv_total,)),
            ],
            compiler_params=params(48),
            cost_estimate=cost(10),
        )(scalars, inverse, eye, *tables, *operands)
        got.append(lax.all_to_all(w_part, "rcv", split_axis=0, concat_axis=0, tiled=True))

    reference_grad = pl.pallas_call(
        join_kernel,
        out_shape=jax.ShapeDtypeStruct((k_own, col_total), jnp.float32),
        in_specs=[vmem] * (1 + CHUNKS),
        out_specs=vmem,
        compiler_params=params(32),
    )(reference_counts.reshape(1, col_total), *got)

    r_sum = r_all[0]
    for k in range(1, ref_total):
        r_sum = r_sum + swap(r_all[k], "ref", ref_total, k)
    parts = [r_sum[k * row_total : (k + 1) * row_total] for k in range(members)]
    r_sum = parts[0]
    for k in range(1, members):
        r_sum = r_sum + swap(parts[k], "rcv", rcv_total, k)
    seg_quarter = jnp.arange(k_quarter, dtype=jnp.int32) % S
    receiver_grad = jnp.where(seg_quarter[None, :] < receiver_counts[:, None], r_sum, 0.0)
    return (receiver_grad, reference_grad)


def solution(mesh):
    return jax.shard_map(
        functools.partial(shards, rcv_total=mesh.shape["rcv"], ref_total=mesh.shape["ref"]),
        mesh=mesh,
        in_specs=(
            P("rcv", "ref"),
            P("rcv", "ref"),
            P("rcv"),
            P("ref"),
            P("ref"),
            P(None, "rcv", "ref"),
            P("rcv", "ref", None),
        ),
        out_specs=(P("rcv", "ref"), P("rcv", "ref")),
        check_vma=False,
    )
```

```python
import functools
import math

import jax
import jax.numpy as jnp
import numpy as np
from jax import lax
from jax.experimental import pallas as pl
from jax.experimental.pallas import tpu as pltpu
from jax.sharding import PartitionSpec as P

L = 512
S = 16
F = 256

env_floor = 0.05
misfit_scale = 0.03125
GROUP = 4
LANES = 128
FB = LANES // (2 * S)
WIDTH = 8
FIXED = 32000.0


def lag_tables(freq_total, lag_total):
    half = lag_total // 2
    freq_ids = np.arange(freq_total)[:, None]
    phase = 2.0 * np.pi * (freq_ids * np.arange(half)[None, :] % lag_total) / lag_total
    cosine = np.cos(phase) / math.sqrt(freq_total)
    sine = np.sin(phase) / math.sqrt(freq_total)
    back = [np.concatenate([cosine[p::2], sine[p::2]], axis=1) for p in (0, 1)]
    ahead = [np.concatenate([cosine[p::2].T, sine[p::2].T], axis=1) for p in (0, 1)]
    back = [np.concatenate([t[:, :half], t[:, half:]], axis=0) for t in back]
    whole = np.concatenate(ahead + back, axis=0)
    return jnp.asarray(whole.astype(np.float32)).astype(jnp.bfloat16)


def nt(a, b):
    return lax.dot_general(a, b, (((1,), (1,)), ((), ())), preferred_element_type=jnp.float32)


def nn(a, b):
    return jnp.dot(a, b, preferred_element_type=jnp.float32)


def tn(a, b):
    return lax.dot_general(a, b, (((0,), (0,)), ((), ())), preferred_element_type=jnp.float32)


def eye_of(size):
    rows = lax.broadcasted_iota(jnp.int32, (size, size), 0)
    lanes = lax.broadcasted_iota(jnp.int32, (size, size), 1)
    return jnp.where(rows == lanes, 1.0, 0.0).astype(jnp.bfloat16)


def turn_kernel(spectra_from, counts_from, v_to, spectra_ref, counts_ref, turned_ref, sems):
    k_own, col_total = spectra_ref.shape
    rcv_total, cols, _ = v_to.shape
    members = col_total // cols
    width = min(k_own, 2 * LANES)
    copies = [pltpu.make_async_copy(counts_from, counts_ref, sems.at[0])]
    for n, begin in enumerate(range(0, k_own, width)):
        rows = pl.ds(begin, width)
        copies.append(
            pltpu.make_async_copy(spectra_from.at[rows], spectra_ref.at[rows], sems.at[1 + n])
        )
    for copy in copies:
        copy.start()
    eye = eye_of(col_total)
    seg_ids = lax.broadcasted_iota(jnp.int32, (width, col_total), 0) % S
    copies[0].wait()
    inside = seg_ids < counts_ref[...]
    for n, begin in enumerate(range(0, k_own, width)):
        copies[1 + n].wait()
        part = spectra_ref[begin : begin + width, :].astype(jnp.float32)
        part = jnp.where(inside, part, 0.0).astype(jnp.bfloat16)
        turned_ref[:, begin : begin + width] = nt(eye, part).astype(jnp.bfloat16)
    copies = [
        pltpu.make_async_copy(
            turned_ref.at[pl.ds(dest % members * cols, cols)], v_to.at[dest], sems.at[dest]
        )
        for dest in range(rcv_total)
    ]
    for copy in copies:
        copy.start()
    for copy in copies:
        copy.wait()


def fold_kernel(c_ref, rcounts_ref, observed_from, rspectra_from, window_from, order_from, *rest):
    *out_to, observed_ref, rspectra_ref, window_ref, order_ref, line_ref, out_ref, sems, out_sems = (
        rest
    )
    row_total, col_total, lag_total = observed_ref.shape
    half = lag_total // 2
    members = len(out_to)
    cols = col_total // members
    lines = col_total * row_total
    quarter = rspectra_ref.shape[1]
    copies = [
        pltpu.make_async_copy(src, dst, sems.at[row_total + n])
        for n, (src, dst) in enumerate(
            [(window_from, window_ref), (order_from, order_ref), (rspectra_from, rspectra_ref)]
        )
    ] + [
        pltpu.make_async_copy(observed_from.at[i], observed_ref.at[i], sems.at[i])
        for i in range(row_total)
    ]
    for copy in copies:
        copy.start()
    for copy in copies[:3]:
        copy.wait()
    window = jnp.concatenate([window_ref[0], window_ref[1]], axis=0).astype(jnp.float32).T
    station = lax.broadcasted_iota(jnp.int32, (col_total, col_total), 0) + c_ref[1]
    pick = jnp.where(station == order_ref[...], 1.0, 0.0).astype(jnp.bfloat16)
    lag_ids = lax.broadcasted_iota(jnp.int32, (col_total, half), 1).astype(jnp.float32)
    for i in range(row_total):
        copies[3 + i].wait()
        begin = window[:, i : i + 1]
        end = begin + window[:, row_total + i : row_total + i + 1]
        values = observed_ref[i].astype(jnp.float32)
        low = (lag_ids >= begin) & (lag_ids < end)
        high = (lag_ids + half >= begin) & (lag_ids + half < end)
        folded = jnp.where(low, values[:, :half], jnp.where(high, -values[:, half:], 0.0))
        moved = nn(pick, folded.astype(jnp.bfloat16))
        for h in range(half // LANES):
            line_ref[pl.ds(h * lines + i, col_total, stride=row_total), :] = moved[
                :, h * LANES : (h + 1) * LANES
            ]
    row_ids = lax.broadcasted_iota(jnp.int32, (row_total, half), 0)
    counts = jnp.zeros((row_total, half), jnp.int32)
    for i in range(row_total):
        counts = jnp.where(row_ids == i, rcounts_ref[i], counts)
    seg_ids = lax.broadcasted_iota(jnp.int32, (row_total, half), 1) % S
    pieces = quarter // half
    for k in range(members):
        for n in range(pieces):
            part = rspectra_ref[:, n * half : (n + 1) * half].astype(jnp.float32)
            out_ref[k, cols + n] = jnp.where(seg_ids < counts, part, 0.0).astype(jnp.bfloat16)
        out_ref[k, cols + pieces] = counts.astype(jnp.float32).astype(jnp.bfloat16)
    mine = c_ref[0]
    copies = []
    for k in range(members):
        first = (mine ^ k) * (cols * row_total)
        for h in range(half // LANES):
            begin = pl.multiple_of(h * lines + first, cols * row_total)
            rows = line_ref[pl.ds(begin, cols * row_total), :]
            out_ref[k, :cols, :, h * LANES : (h + 1) * LANES] = rows.reshape(
                cols, row_total, LANES
            ).astype(jnp.bfloat16)
        copies.append(pltpu.make_async_copy(out_ref.at[k], out_to[k], out_sems.at[k]))
        copies[-1].start()
    for copy in copies:
        copy.wait()


def near_kernel(*refs):
    *parts, out_ref, sems = refs
    extra = out_ref.shape[1]
    copies = []
    for k, ref in enumerate(parts):
        rows = ref.at[pl.ds(ref.shape[0] - extra, extra)]
        copies.append(pltpu.make_async_copy(rows, out_ref.at[k], sems.at[k]))
        copies[-1].start()
    for copy in copies:
        copy.wait()


def pair_kernel(n_e, n_r, c_ref, invn_ref, table_ref, v_from, *refs):
    refs = list(refs)
    e_from, u_from = refs[:n_e], refs[n_e : n_e + n_r]
    w_to, *r_to = refs[n_e + n_r : n_e + 2 * n_r + 1]
    (
        x_ref, z_ref, plain_ref, turned_ref, code_ref, u_ref, v_ref, e_ref, r_ref, w_ref,
        sems, w_sems,
    ) = refs[n_e + 2 * n_r + 1 :]

    src_total, col_total, k_own = v_ref.shape
    ref_total, irec, k_quarter = r_ref.shape
    jj_total = LANES // (2 * irec)
    jp_total = col_total // jj_total
    k_total = src_total * k_own
    half_f = k_total // (4 * S)
    freq_total = 2 * half_f
    blocks = k_total // LANES
    own_blocks = k_own // LANES
    quarter_blocks = k_quarter // LANES

    quarter_me = c_ref[3]
    early = [pltpu.make_async_copy(v_from, v_ref, sems.at[0])]
    for k, ref in enumerate(u_from):
        early.append(pltpu.make_async_copy(ref, u_ref.at[quarter_me ^ k], sems.at[1 + k]))
    late = [
        pltpu.make_async_copy(ref.at[pl.ds(0, col_total)], e_ref.at[k], sems.at[1 + n_r + k])
        for k, ref in enumerate(e_from)
    ]
    for copy in early + late:
        copy.start()
    half = e_ref.shape[-1]
    eye = eye_of(half)
    table_y = [table_ref[p * half : (p + 1) * half, :] for p in range(2)]
    table_z = []
    for p in range(2):
        begin = 2 * half + p * 2 * half_f
        parts = [table_ref[begin + n * half_f : begin + (n + 1) * half_f, :] for n in range(2)]
        table_z.append(jnp.concatenate(parts, axis=1))

    group_ids = lax.broadcasted_iota(jnp.int32, (jp_total, LANES), 1) // (2 * S)
    first_part = lax.broadcasted_iota(jnp.int32, (irec, LANES), 1) % (2 * S) < S

    def lanes_of(fb, per):
        return fb // per, pl.multiple_of(fb % per * LANES, LANES)

    def v_block(fb):
        src, off = lanes_of(fb, own_blocks)
        parts = [
            v_ref[src, jj * jp_total : (jj + 1) * jp_total, pl.ds(off, LANES)]
            for jj in range(jj_total)
        ]
        zero = jnp.zeros((jp_total, LANES), jnp.bfloat16)
        rows = [
            jnp.concatenate([jnp.where(group_ids == f, part, zero) for part in parts], axis=1)
            for f in range(FB)
        ]
        return jnp.concatenate(rows, axis=0)

    def u_block(parts):
        zero = jnp.zeros((irec, LANES), jnp.bfloat16)
        return jnp.concatenate(
            [
                jnp.concatenate([part if k == jj else zero for k in range(jj_total)], axis=1)
                for part in parts
                for jj in range(jj_total)
            ],
            axis=0,
        )

    def place(fb, f):
        return pl.ds((f % 2) * half_f + fb * (FB // 2) + f // 2, jp_total, stride=freq_total)

    def forward(fb, _):
        lanes = pl.ds(pl.multiple_of(fb * LANES, LANES), LANES)
        quarter, off = lanes_of(fb, quarter_blocks)
        piece, off = off // half, pl.multiple_of(off % half, LANES)
        wide = u_ref[quarter, :, piece, :, pl.ds(off, LANES)].astype(jnp.float32)
        wide = wide.reshape(irec, LANES)
        part = wide.astype(jnp.bfloat16)
        plain_ref[:, lanes] = part
        crossed = jnp.where(first_part, pltpu.roll(wide, LANES - S, 1), -pltpu.roll(wide, S, 1))
        crossed = crossed.astype(jnp.bfloat16)
        turned_ref[:, lanes] = crossed
        out = nt(v_block(fb), u_block([part, crossed]))
        scale = invn_ref[...]
        for f in range(FB):
            x_ref[place(fb, f), :] = out[f * jp_total : (f + 1) * jp_total] * scale
        return 0

    for copy in early:
        copy.wait()
    lax.fori_loop(0, blocks, forward, 0, unroll=16)

    lane_ids = lax.broadcasted_iota(jnp.int32, (1, LANES), 1)
    sign = jnp.where(lane_ids < LANES // 2, -1.0, 1.0).astype(jnp.float32)

    sign = sign.astype(jnp.bfloat16)

    def pairs(step, _):
        cols = [step * WIDTH + k for k in range(WIDTH)]
        rhs_e, rhs_o, obs = [], [], []
        for jp in cols:
            x = x_ref[pl.ds(pl.multiple_of(jp * freq_total, freq_total), freq_total), :]
            plain = x.astype(jnp.bfloat16)
            turned = pltpu.roll(x, LANES // 2, 1).astype(jnp.bfloat16) * sign
            rhs_e.append(jnp.concatenate([plain[:half_f], turned[:half_f]], axis=0))
            rhs_o.append(jnp.concatenate([plain[half_f:], turned[half_f:]], axis=0))
            rows = [
                e_ref[:, jj * jp_total + jp].astype(jnp.float32).reshape(irec, half)
                for jj in range(jj_total)
            ]
            rows = jnp.concatenate(rows, axis=0).astype(jnp.bfloat16)
            obs += [rows, rows]
        even = nn(table_y[0], jnp.concatenate(rhs_e, axis=1))
        odd = nn(table_y[1], jnp.concatenate(rhs_o, axis=1))
        seen = nt(eye, jnp.concatenate(obs, axis=0))
        g_e, g_o = [], []
        for k in range(WIDTH):
            lanes = slice(k * LANES, (k + 1) * LANES)
            e, d0, d1 = seen[:, lanes], even[:, lanes], odd[:, lanes]
            d = jnp.where(e < 0.0, d0 + d1, d0 - d1)
            power = d * d
            power = power + (pltpu.roll(power, LANES // 2, 1) + env_floor)
            g = d * (1.0 - jnp.abs(e) * lax.rsqrt(power))
            side = jnp.where(e < 0.0, 1.0, jnp.where(e > 0.0, -1.0, 0.0)).astype(jnp.bfloat16)
            turned = pltpu.roll(g, LANES // 2, 1).astype(jnp.bfloat16)
            g_side = g.astype(jnp.bfloat16) * side
            t_side = turned * (side * -sign)
            g_e.append(jnp.concatenate([g_side * side, t_side * side], axis=0))
            g_o.append(jnp.concatenate([g_side, t_side], axis=0))
        z_e = nn(table_z[0], jnp.concatenate(g_e, axis=1))
        z_o = nn(table_z[1], jnp.concatenate(g_o, axis=1))
        for k, jp in enumerate(cols):
            lanes = slice(k * LANES, (k + 1) * LANES)
            scale = invn_ref[pl.ds(jp, 1), :] * misfit_scale
            base = pl.multiple_of(jp * freq_total, freq_total)
            z_ref[pl.ds(base, half_f), :] = z_e[:, lanes] * scale
            z_ref[pl.ds(base + half_f, half_f), :] = z_o[:, lanes] * scale
        return 0

    for copy in late:
        copy.wait()
    lax.fori_loop(0, jp_total // WIDTH, pairs, 0)

    def backward(fb):
        z = jnp.concatenate([z_ref[place(fb, f), :] for f in range(FB)], axis=0)
        z = z.astype(jnp.bfloat16)
        lanes = pl.ds(pl.multiple_of(fb * LANES, LANES), LANES)
        w = nn(z, u_block([plain_ref[:, lanes], turned_ref[:, lanes]]))
        totals = []
        for jj in range(jj_total):
            lanes = slice(jj * LANES, (jj + 1) * LANES)
            total = w[:jp_total, lanes]
            for f in range(1, FB):
                total = jnp.where(group_ids == f, w[f * jp_total : (f + 1) * jp_total, lanes], total)
            totals.append(total)
        total = jnp.concatenate(totals, axis=0)
        largest = jnp.max(jnp.abs(total), axis=0, keepdims=True)
        power = jnp.ceil(jnp.log2(jnp.maximum(largest, 1e-30)))
        code_ref[pl.ds(fb, 1), :] = power
        fixed = jnp.round(total * (jnp.exp2(-power) * FIXED)).astype(jnp.int32)
        src, off = lanes_of(fb, own_blocks)
        w_ref[src, :, pl.ds(off, LANES)] = fixed.astype(jnp.int16)
        r = tn(z, v_block(fb))
        sums = []
        for q in range(2):
            total = None
            for jj in range(jj_total):
                begin = (q * jj_total + jj) * irec
                part = r[begin : begin + irec, jj * LANES : (jj + 1) * LANES]
                total = part if total is None else total + part
            sums.append(total)
        crossed = jnp.where(
            first_part, -pltpu.roll(sums[1], LANES - S, 1), pltpu.roll(sums[1], S, 1)
        )
        quarter, off = lanes_of(fb, quarter_blocks)
        lanes = pl.ds(off, LANES)
        total = sums[0] + crossed
        r_ref[quarter, :, lanes] = total

    def w_copy(src):
        return pltpu.make_async_copy(w_ref.at[src], w_to.at[src], w_sems.at[src])

    def from_owner(src, _):
        for b in range(own_blocks):
            backward(src * own_blocks + b)
        codes = code_ref[pl.ds(src * own_blocks, own_blocks), :]
        codes = jnp.concatenate(
            [codes, jnp.zeros((col_total - own_blocks, LANES), jnp.float32)], axis=0
        )
        w_ref[src, :, k_own:] = codes.astype(jnp.int32).astype(jnp.int16)
        w_copy(src).start()
        return 0

    owners = src_total // ref_total
    outs = []
    for k, ref in enumerate(r_to):
        begin = (quarter_me ^ k) * owners
        lax.fori_loop(begin, begin + owners, from_owner, 0)
        outs.append(pltpu.make_async_copy(r_ref.at[quarter_me ^ k], ref, sems.at[k]))
        outs[-1].start()
    for copy in outs:
        copy.wait()
    for src in range(src_total):
        w_copy(src).wait()


def join_kernel(count_ref, got_ref, out_ref):
    src_total, cols, _ = got_ref.shape
    k_own, col_total = out_ref.shape
    members = col_total // cols
    seg_ids = lax.broadcasted_iota(jnp.int32, (LANES, col_total), 0) % S
    inside = seg_ids < count_ref[...]
    scales = [
        jnp.exp2(got_ref[src, :16, k_own:].astype(jnp.int32).astype(jnp.float32)) * (1.0 / FIXED)
        for src in range(src_total)
    ]
    for b in range(k_own // LANES):
        rows = []
        for m in range(members):
            total = None
            for src in range(m, src_total, members):
                part = got_ref[src, :, b * LANES : (b + 1) * LANES]
                part = part.astype(jnp.int32).astype(jnp.float32) * scales[src][b : b + 1]
                total = part if total is None else total + part
            rows.append(total)
        whole = jnp.concatenate(rows, axis=0).T
        out_ref[b * LANES : (b + 1) * LANES, :] = jnp.where(inside, whole, 0.0)


def swap(x, axis, total, k):
    return lax.ppermute(x, axis, [(r, r ^ k) for r in range(total)])


def shards(
    receiver_spectra,
    reference_spectra,
    receiver_counts,
    reference_counts,
    column_station,
    lag_window,
    observed,
    *,
    rcv_total,
    ref_total,
):
    row_total, k_quarter = receiver_spectra.shape
    k_own, col_total = reference_spectra.shape
    k_total = k_own * rcv_total
    lag_total = observed.shape[2]
    half = lag_total // 2
    members = math.gcd(GROUP, rcv_total)
    irec = row_total * members
    cols = col_total // members
    jj_total = LANES // (2 * irec)
    jp_total = cols // jj_total
    extra = k_quarter // half + 1
    bf16 = jnp.bfloat16
    place = lax.axis_index("rcv")
    mine = place % members
    quarter = lax.axis_index("ref")
    vmem = pl.BlockSpec(memory_space=pltpu.VMEM)
    smem = pl.BlockSpec(memory_space=pltpu.SMEM)
    hbm = pl.BlockSpec(memory_space=pl.ANY)
    scalars = jnp.stack([mine, quarter * col_total, place, quarter]).astype(jnp.int32)
    params = pltpu.CompilerParams(vmem_limit_bytes=32 * 1024 * 1024)
    free = pl.CostEstimate(flops=0, bytes_accessed=0, transcendentals=0)

    sent = pl.pallas_call(
        turn_kernel,
        out_shape=jax.ShapeDtypeStruct((rcv_total, cols, k_own), bf16),
        in_specs=[hbm] * 2,
        out_specs=hbm,
        scratch_shapes=[
            pltpu.VMEM((k_own, col_total), bf16),
            pltpu.VMEM((1, col_total), jnp.int32),
            pltpu.VMEM((col_total, k_own), bf16),
            pltpu.SemaphoreType.DMA((max(rcv_total, 1 + k_own // min(k_own, 2 * LANES)),)),
        ],
        compiler_params=params,
        cost_estimate=free,
    )(reference_spectra, reference_counts.reshape(1, col_total))
    v_all = lax.all_to_all(sent, "rcv", split_axis=0, concat_axis=0, tiled=True)

    _, observed = lax.optimization_barrier((sent, observed))
    shape = (cols + extra, row_total, half)
    folded = pl.pallas_call(
        fold_kernel,
        out_shape=[jax.ShapeDtypeStruct(shape, bf16)] * members,
        in_specs=[smem] * 2 + [hbm] * 4,
        out_specs=[hbm] * members,
        scratch_shapes=[
            pltpu.VMEM(observed.shape, bf16),
            pltpu.VMEM(receiver_spectra.shape, bf16),
            pltpu.VMEM(lag_window.shape, jnp.int32),
            pltpu.VMEM((1, col_total), jnp.int32),
            pltpu.VMEM((half // LANES * col_total * row_total, LANES), jnp.float32),
            pltpu.VMEM((members,) + shape, bf16),
            pltpu.SemaphoreType.DMA((row_total + 3,)),
            pltpu.SemaphoreType.DMA((members,)),
        ],
        compiler_params=params,
        cost_estimate=free,
    )(
        scalars,
        receiver_counts,
        observed,
        receiver_spectra,
        lag_window,
        column_station.reshape(1, col_total),
    )
    e_all = [folded[0]] + [swap(folded[k], "rcv", rcv_total, k) for k in range(1, members)]

    near = pl.pallas_call(
        near_kernel,
        out_shape=jax.ShapeDtypeStruct((members, extra, row_total, half), bf16),
        in_specs=[hbm] * members,
        out_specs=hbm,
        scratch_shapes=[pltpu.SemaphoreType.DMA((members,))],
        compiler_params=params,
        cost_estimate=free,
    )(*e_all)
    u_all = [near] + [swap(near, "ref", ref_total, k) for k in range(1, ref_total)]

    group_counts = near[:, extra - 1, :, 0].reshape(irec).astype(jnp.float32)
    own_counts = lax.dynamic_slice_in_dim(reference_counts, mine * cols, cols).astype(jnp.float32)
    counts = own_counts.reshape(jj_total, jp_total).T
    least = jnp.minimum(counts[:, :, None], group_counts[None, None, :])
    inverse = (1.0 / least).reshape(jp_total, jj_total * irec)
    inverse = jnp.concatenate([inverse, inverse], axis=1)

    table = lag_tables(k_total // (2 * S), lag_total)
    lines = jp_total * k_total // (2 * S)
    w_part, *r_all = pl.pallas_call(
        functools.partial(pair_kernel, members, ref_total),
        out_shape=[jax.ShapeDtypeStruct((rcv_total, cols, k_own + LANES), jnp.int16)]
        + [jax.ShapeDtypeStruct((irec, k_quarter), jnp.float32)] * ref_total,
        in_specs=[smem] + [vmem] * 2 + [hbm] * (1 + members + ref_total),
        out_specs=[hbm] * (1 + ref_total),
        scratch_shapes=[
            pltpu.VMEM((lines, LANES), jnp.float32),
            pltpu.VMEM((lines, LANES), jnp.float32),
            pltpu.VMEM((irec, k_total), bf16),
            pltpu.VMEM((irec, k_total), bf16),
            pltpu.VMEM((k_total // LANES, LANES), jnp.float32),
            pltpu.VMEM((ref_total,) + near.shape, bf16),
            pltpu.VMEM((rcv_total, cols, k_own), bf16),
            pltpu.VMEM((members, cols, row_total, half), bf16),
            pltpu.VMEM((ref_total, irec, k_quarter), jnp.float32),
            pltpu.VMEM((rcv_total, cols, k_own + LANES), jnp.int16),
            pltpu.SemaphoreType.DMA((1 + members + ref_total,)),
            pltpu.SemaphoreType.DMA((rcv_total,)),
        ],
        compiler_params=params,
        cost_estimate=free,
    )(scalars, inverse, table, v_all, *e_all, *u_all)

    got = lax.all_to_all(w_part, "rcv", split_axis=0, concat_axis=0, tiled=True)
    reference_grad = pl.pallas_call(
        join_kernel,
        out_shape=jax.ShapeDtypeStruct((k_own, col_total), jnp.float32),
        in_specs=[vmem] * 2,
        out_specs=vmem,
        compiler_params=params,
        cost_estimate=free,
    )(reference_counts.reshape(1, col_total), got)

    r_sum = r_all[0]
    for k in range(1, ref_total):
        r_sum = r_sum + swap(r_all[k], "ref", ref_total, k)
    parts = [r_sum[k * row_total : (k + 1) * row_total] for k in range(members)]
    r_sum = parts[0]
    for k in range(1, members):
        r_sum = r_sum + swap(parts[k], "rcv", rcv_total, k)
    seg_quarter = jnp.arange(k_quarter, dtype=jnp.int32) % S
    receiver_grad = jnp.where(seg_quarter[None, :] < receiver_counts[:, None], r_sum, 0.0)
    return (receiver_grad, reference_grad)


def solution(mesh):
    return jax.shard_map(
        functools.partial(shards, rcv_total=mesh.shape["rcv"], ref_total=mesh.shape["ref"]),
        mesh=mesh,
        in_specs=(
            P("rcv", "ref"),
            P("rcv", "ref"),
            P("rcv"),
            P("ref"),
            P("ref"),
            P(None, "rcv", "ref"),
            P("rcv", "ref", None),
        ),
        out_specs=(P("rcv", "ref"), P("rcv", "ref")),
        check_vma=False,
    )
```

```python
import functools
import math

import jax
import jax.numpy as jnp
import numpy as np
from jax import lax
from jax.experimental import pallas as pl
from jax.experimental.pallas import tpu as pltpu
from jax.sharding import PartitionSpec as P

L = 512
S = 16
F = 256

env_floor = 0.05
misfit_scale = 0.03125
GROUP = 4
LANES = 128
FB = LANES // (2 * S)
WIDTH = 16
CHUNKS = 2
FIXED = 32000.0


def lag_tables(freq_total, lag_total):
    half = lag_total // 2
    freq_ids = np.arange(freq_total)[:, None]
    phase = 2.0 * np.pi * (freq_ids * np.arange(half)[None, :] % lag_total) / lag_total
    cosine = np.cos(phase) / math.sqrt(freq_total)
    sine = np.sin(phase) / math.sqrt(freq_total)
    back = [np.concatenate([cosine[p::2], sine[p::2]], axis=1) for p in (0, 1)]
    ahead = [np.concatenate([cosine[p::2].T, sine[p::2].T], axis=1) for p in (0, 1)]
    back = [np.concatenate([t[:, :half], t[:, half:]], axis=0) for t in back]
    whole = np.concatenate(ahead + back, axis=0)
    return jnp.asarray(whole.astype(np.float32)).astype(jnp.bfloat16)


def nt(a, b):
    return lax.dot_general(a, b, (((1,), (1,)), ((), ())), preferred_element_type=jnp.float32)


def nn(a, b):
    return jnp.dot(a, b, preferred_element_type=jnp.float32)


def tn(a, b):
    return lax.dot_general(a, b, (((0,), (0,)), ((), ())), preferred_element_type=jnp.float32)


def eye_of(size):
    rows = lax.broadcasted_iota(jnp.int32, (size, size), 0)
    lanes = lax.broadcasted_iota(jnp.int32, (size, size), 1)
    return jnp.where(rows == lanes, 1.0, 0.0).astype(jnp.bfloat16)


def turn_kernel(rcounts_ref, spectra_from, counts_from, rspectra_from, *refs):
    u_to, *v_to = refs[: 1 + CHUNKS]
    spectra_ref, counts_ref, rspectra_ref, turned_ref, u_ref, sems, out_sems = refs[1 + CHUNKS :]
    k_own, col_total = spectra_ref.shape
    rcv_total, cols, _ = v_to[0].shape
    members = col_total // (cols * CHUNKS)
    width = min(k_own, 2 * LANES)
    copies = [
        pltpu.make_async_copy(counts_from, counts_ref, sems.at[0]),
        pltpu.make_async_copy(rspectra_from, rspectra_ref, sems.at[1]),
    ]
    for n, begin in enumerate(range(0, k_own, width)):
        rows = pl.ds(begin, width)
        copies.append(
            pltpu.make_async_copy(spectra_from.at[rows], spectra_ref.at[rows], sems.at[2 + n])
        )
    for copy in copies:
        copy.start()
    eye = eye_of(col_total)
    seg_ids = lax.broadcasted_iota(jnp.int32, (width, col_total), 0) % S
    copies[0].wait()
    inside = seg_ids < counts_ref[...]
    for n, begin in enumerate(range(0, k_own, width)):
        copies[2 + n].wait()
        part = spectra_ref[begin : begin + width, :].astype(jnp.float32)
        part = jnp.where(inside, part, 0.0).astype(jnp.bfloat16)
        turned_ref[:, begin : begin + width] = nt(eye, part).astype(jnp.bfloat16)
    outs = []
    for c in range(CHUNKS):
        for dest in range(rcv_total):
            first = (dest % members * CHUNKS + c) * cols
            outs.append(
                pltpu.make_async_copy(
                    turned_ref.at[pl.ds(first, cols)],
                    v_to[c].at[dest],
                    out_sems.at[c * rcv_total + dest],
                )
            )
            outs[-1].start()
    copies[1].wait()
    pieces, rows, half = u_ref.shape
    row_ids = lax.broadcasted_iota(jnp.int32, (rows, half), 0)
    counts = jnp.zeros((rows, half), jnp.int32)
    for i in range(rows):
        counts = jnp.where(row_ids == i, rcounts_ref[i], counts)
    seg_ids = lax.broadcasted_iota(jnp.int32, (rows, half), 1) % S
    for n in range(pieces - 1):
        part = rspectra_ref[:, n * half : (n + 1) * half].astype(jnp.float32)
        u_ref[n] = jnp.where(seg_ids < counts, part, 0.0).astype(jnp.bfloat16)
    u_ref[pieces - 1] = counts.astype(jnp.float32).astype(jnp.bfloat16)
    outs.append(pltpu.make_async_copy(u_ref, u_to, out_sems.at[CHUNKS * rcv_total]))
    outs[-1].start()
    for copy in outs:
        copy.wait()


def fold_kernel(c_ref, observed_from, window_from, order_from, *rest):
    *out_to, observed_ref, window_ref, order_ref, line_ref, out_ref, sems, out_sems = rest
    row_total, col_total, lag_total = observed_ref.shape
    half = lag_total // 2
    members = len(out_to) // CHUNKS
    cols = col_total // len(out_to)
    lines = col_total * row_total
    copies = [
        pltpu.make_async_copy(window_from, window_ref, sems.at[row_total]),
        pltpu.make_async_copy(order_from, order_ref, sems.at[row_total + 1]),
    ] + [
        pltpu.make_async_copy(observed_from.at[i], observed_ref.at[i], sems.at[i])
        for i in range(row_total)
    ]
    for copy in copies:
        copy.start()
    for copy in copies[:2]:
        copy.wait()
    window = jnp.concatenate([window_ref[0], window_ref[1]], axis=0).astype(jnp.float32).T
    station = lax.broadcasted_iota(jnp.int32, (col_total, col_total), 0) + c_ref[1]
    pick = jnp.where(station == order_ref[...], 1.0, 0.0).astype(jnp.bfloat16)
    lag_ids = lax.broadcasted_iota(jnp.int32, (col_total, half), 1).astype(jnp.float32)
    for i in range(row_total):
        copies[2 + i].wait()
        begin = window[:, i : i + 1]
        end = begin + window[:, row_total + i : row_total + i + 1]
        values = observed_ref[i].astype(jnp.float32)
        low = (lag_ids >= begin) & (lag_ids < end)
        high = (lag_ids + half >= begin) & (lag_ids + half < end)
        folded = jnp.where(low, values[:, :half], jnp.where(high, -values[:, half:], 0.0))
        moved = nn(pick, folded.astype(jnp.bfloat16))
        for h in range(half // LANES):
            line_ref[pl.ds(h * lines + i, col_total, stride=row_total), :] = moved[
                :, h * LANES : (h + 1) * LANES
            ]
    mine = c_ref[0]
    copies = []
    for c in range(CHUNKS):
        for k in range(members):
            n = c * members + k
            first = ((mine ^ k) * CHUNKS + c) * (cols * row_total)
            for h in range(half // LANES):
                begin = pl.multiple_of(h * lines + first, cols * row_total)
                rows = line_ref[pl.ds(begin, cols * row_total), :]
                out_ref[n, :, :, h * LANES : (h + 1) * LANES] = rows.reshape(
                    cols, row_total, LANES
                ).astype(jnp.bfloat16)
            copies.append(pltpu.make_async_copy(out_ref.at[n], out_to[n], out_sems.at[n]))
            copies[-1].start()
    for copy in copies:
        copy.wait()


def near_kernel(*refs):
    *parts, out_ref, sems = refs
    copies = [
        pltpu.make_async_copy(ref, out_ref.at[k], sems.at[k]) for k, ref in enumerate(parts)
    ]
    for copy in copies:
        copy.start()
    for copy in copies:
        copy.wait()


def pair_kernel(n_e, n_r, n_in, c_ref, invn_ref, table_ref, v_from, *refs):
    refs = list(refs)
    e_from, u_from = refs[:n_e], refs[n_e : n_e + n_r]
    r_from = refs[n_e + n_r : n_e + n_r + n_in]
    w_to, *r_to = refs[n_e + n_r + n_in : n_e + 2 * n_r + n_in + 1]
    (
        x_ref, z_ref, plain_ref, turned_ref, code_ref, u_ref, v_ref, e_ref, r_ref, w_ref,
        sems, w_sems,
    ) = refs[n_e + 2 * n_r + n_in + 1 :]

    src_total, col_total, k_own = v_ref.shape
    ref_total, irec, k_quarter = r_ref.shape
    jj_total = LANES // (2 * irec)
    jp_total = col_total // jj_total
    k_total = src_total * k_own
    half_f = k_total // (4 * S)
    freq_total = 2 * half_f
    blocks = k_total // LANES
    own_blocks = k_own // LANES
    quarter_blocks = k_quarter // LANES

    quarter_me = c_ref[3]
    early = [pltpu.make_async_copy(v_from, v_ref, sems.at[0])]
    for k, ref in enumerate(u_from):
        early.append(pltpu.make_async_copy(ref, u_ref.at[quarter_me ^ k], sems.at[1 + k]))
    late = [
        pltpu.make_async_copy(ref, e_ref.at[k], sems.at[1 + n_r + k])
        for k, ref in enumerate(e_from)
    ]
    last = [
        pltpu.make_async_copy(ref, r_ref.at[quarter_me ^ k], sems.at[1 + n_r + n_e + k])
        for k, ref in enumerate(r_from)
    ]
    for copy in early + late + last:
        copy.start()
    half = e_ref.shape[-1]
    eye = eye_of(half)
    table_y = [table_ref[p * half : (p + 1) * half, :] for p in range(2)]
    table_z = []
    for p in range(2):
        begin = 2 * half + p * 2 * half_f
        parts = [table_ref[begin + n * half_f : begin + (n + 1) * half_f, :] for n in range(2)]
        table_z.append(jnp.concatenate(parts, axis=1))

    group_ids = lax.broadcasted_iota(jnp.int32, (jp_total, LANES), 1) // (2 * S)
    first_part = lax.broadcasted_iota(jnp.int32, (irec, LANES), 1) % (2 * S) < S

    def lanes_of(fb, per):
        return fb // per, pl.multiple_of(fb % per * LANES, LANES)

    def v_block(fb):
        src, off = lanes_of(fb, own_blocks)
        parts = [
            v_ref[src, jj * jp_total : (jj + 1) * jp_total, pl.ds(off, LANES)]
            for jj in range(jj_total)
        ]
        zero = jnp.zeros((jp_total, LANES), jnp.bfloat16)
        rows = [
            jnp.concatenate([jnp.where(group_ids == f, part, zero) for part in parts], axis=1)
            for f in range(FB)
        ]
        return jnp.concatenate(rows, axis=0)

    def u_block(parts):
        zero = jnp.zeros((irec, LANES), jnp.bfloat16)
        return jnp.concatenate(
            [
                jnp.concatenate([part if k == jj else zero for k in range(jj_total)], axis=1)
                for part in parts
                for jj in range(jj_total)
            ],
            axis=0,
        )

    def place(fb, f):
        return pl.ds((f % 2) * half_f + fb * (FB // 2) + f // 2, jp_total, stride=freq_total)

    def forward(fb, _):
        lanes = pl.ds(pl.multiple_of(fb * LANES, LANES), LANES)
        quarter, off = lanes_of(fb, quarter_blocks)
        piece, off = off // half, pl.multiple_of(off % half, LANES)
        wide = u_ref[quarter, :, piece, :, pl.ds(off, LANES)].astype(jnp.float32)
        wide = wide.reshape(irec, LANES)
        part = wide.astype(jnp.bfloat16)
        plain_ref[:, lanes] = part
        crossed = jnp.where(first_part, pltpu.roll(wide, LANES - S, 1), -pltpu.roll(wide, S, 1))
        crossed = crossed.astype(jnp.bfloat16)
        turned_ref[:, lanes] = crossed
        out = nt(v_block(fb), u_block([part, crossed]))
        scale = invn_ref[...]
        for f in range(FB):
            x_ref[place(fb, f), :] = out[f * jp_total : (f + 1) * jp_total] * scale
        return 0

    for copy in early:
        copy.wait()
    lax.fori_loop(0, blocks, forward, 0, unroll=64)

    lane_ids = lax.broadcasted_iota(jnp.int32, (1, LANES), 1)
    sign = jnp.where(lane_ids < LANES // 2, -1.0, 1.0).astype(jnp.float32)

    sign = sign.astype(jnp.bfloat16)

    def pairs(step, _):
        cols = [step * WIDTH + k for k in range(WIDTH)]
        rhs_e, rhs_o, obs = [], [], []
        for jp in cols:
            x = x_ref[pl.ds(pl.multiple_of(jp * freq_total, freq_total), freq_total), :]
            plain = x.astype(jnp.bfloat16)
            turned = pltpu.roll(x, LANES // 2, 1).astype(jnp.bfloat16) * sign
            rhs_e.append(jnp.concatenate([plain[:half_f], turned[:half_f]], axis=0))
            rhs_o.append(jnp.concatenate([plain[half_f:], turned[half_f:]], axis=0))
            rows = [
                e_ref[:, jj * jp_total + jp].astype(jnp.float32).reshape(irec, half)
                for jj in range(jj_total)
            ]
            rows = jnp.concatenate(rows, axis=0).astype(jnp.bfloat16)
            obs += [rows, rows]
        even = nn(table_y[0], jnp.concatenate(rhs_e, axis=1))
        odd = nn(table_y[1], jnp.concatenate(rhs_o, axis=1))
        seen = nt(eye, jnp.concatenate(obs, axis=0))
        g_e, g_o = [], []
        for k in range(WIDTH):
            lanes = slice(k * LANES, (k + 1) * LANES)
            e, d0, d1 = seen[:, lanes], even[:, lanes], odd[:, lanes]
            d = jnp.where(e < 0.0, d0 + d1, d0 - d1)
            power = d * d
            power = power + (pltpu.roll(power, LANES // 2, 1) + env_floor)
            g = d * (1.0 - jnp.abs(e) * lax.rsqrt(power))
            side = jnp.where(e < 0.0, 1.0, jnp.where(e > 0.0, -1.0, 0.0)).astype(jnp.bfloat16)
            turned = pltpu.roll(g, LANES // 2, 1).astype(jnp.bfloat16)
            g_side = g.astype(jnp.bfloat16) * side
            t_side = turned * (side * -sign)
            g_e.append(jnp.concatenate([g_side * side, t_side * side], axis=0))
            g_o.append(jnp.concatenate([g_side, t_side], axis=0))
        z_e = nn(table_z[0], jnp.concatenate(g_e, axis=1))
        z_o = nn(table_z[1], jnp.concatenate(g_o, axis=1))
        for k, jp in enumerate(cols):
            lanes = slice(k * LANES, (k + 1) * LANES)
            scale = invn_ref[pl.ds(jp, 1), :] * misfit_scale
            base = pl.multiple_of(jp * freq_total, freq_total)
            z_ref[pl.ds(base, half_f), :] = z_e[:, lanes] * scale
            z_ref[pl.ds(base + half_f, half_f), :] = z_o[:, lanes] * scale
        return 0

    for copy in late:
        copy.wait()
    lax.fori_loop(0, jp_total // WIDTH, pairs, 0, unroll=2)

    def backward(fb):
        z = jnp.concatenate([z_ref[place(fb, f), :] for f in range(FB)], axis=0)
        z = z.astype(jnp.bfloat16)
        lanes = pl.ds(pl.multiple_of(fb * LANES, LANES), LANES)
        w = nn(z, u_block([plain_ref[:, lanes], turned_ref[:, lanes]]))
        totals = []
        for jj in range(jj_total):
            lanes = slice(jj * LANES, (jj + 1) * LANES)
            total = w[:jp_total, lanes]
            for f in range(1, FB):
                total = jnp.where(group_ids == f, w[f * jp_total : (f + 1) * jp_total, lanes], total)
            totals.append(total)
        total = jnp.concatenate(totals, axis=0)
        largest = jnp.max(jnp.abs(total), axis=0, keepdims=True)
        power = jnp.ceil(jnp.log2(jnp.maximum(largest, 1e-30)))
        code_ref[pl.ds(fb, 1), :] = power
        fixed = jnp.round(total * (jnp.exp2(-power) * FIXED)).astype(jnp.int32)
        src, off = lanes_of(fb, own_blocks)
        w_ref[src, :, pl.ds(off, LANES)] = fixed.astype(jnp.int16)
        r = tn(z, v_block(fb))
        sums = []
        for q in range(2):
            total = None
            for jj in range(jj_total):
                begin = (q * jj_total + jj) * irec
                part = r[begin : begin + irec, jj * LANES : (jj + 1) * LANES]
                total = part if total is None else total + part
            sums.append(total)
        crossed = jnp.where(
            first_part, -pltpu.roll(sums[1], LANES - S, 1), pltpu.roll(sums[1], S, 1)
        )
        quarter, off = lanes_of(fb, quarter_blocks)
        lanes = pl.ds(off, LANES)
        total = sums[0] + crossed
        r_ref[quarter, :, lanes] = r_ref[quarter, :, lanes] + total if r_from else total

    def w_copy(src):
        return pltpu.make_async_copy(w_ref.at[src], w_to.at[src], w_sems.at[src])

    def from_owner(src, _):
        for b in range(own_blocks):
            backward(src * own_blocks + b)
        codes = code_ref[pl.ds(src * own_blocks, own_blocks), :]
        codes = jnp.concatenate(
            [codes, jnp.zeros((col_total - own_blocks, LANES), jnp.float32)], axis=0
        )
        w_ref[src, :, k_own:] = codes.astype(jnp.int32).astype(jnp.int16)
        w_copy(src).start()
        return 0

    for copy in last:
        copy.wait()
    lax.fori_loop(0, src_total, from_owner, 0, unroll=4)
    outs = [
        pltpu.make_async_copy(r_ref.at[quarter_me ^ k], ref, sems.at[k])
        for k, ref in enumerate(r_to)
    ]
    for copy in outs:
        copy.start()
    for copy in outs:
        copy.wait()
    for src in range(src_total):
        w_copy(src).wait()


def join_kernel(count_ref, *refs):
    *got_refs, out_ref = refs
    src_total, cols, _ = got_refs[0].shape
    k_own, col_total = out_ref.shape
    members = col_total // (cols * len(got_refs))
    seg_ids = lax.broadcasted_iota(jnp.int32, (LANES, col_total), 0) % S
    inside = seg_ids < count_ref[...]
    scales = [
        [
            jnp.exp2(ref[src, :16, k_own:].astype(jnp.int32).astype(jnp.float32)) * (1.0 / FIXED)
            for src in range(src_total)
        ]
        for ref in got_refs
    ]
    for b in range(k_own // LANES):
        rows = []
        for m in range(members):
            for ref, scale in zip(got_refs, scales):
                total = None
                for src in range(m, src_total, members):
                    part = ref[src, :, b * LANES : (b + 1) * LANES]
                    part = part.astype(jnp.int32).astype(jnp.float32) * scale[src][b : b + 1]
                    total = part if total is None else total + part
                rows.append(total)
        whole = jnp.concatenate(rows, axis=0).T
        out_ref[b * LANES : (b + 1) * LANES, :] = jnp.where(inside, whole, 0.0)


def swap(x, axis, total, k):
    return lax.ppermute(x, axis, [(r, r ^ k) for r in range(total)])


def shards(
    receiver_spectra,
    reference_spectra,
    receiver_counts,
    reference_counts,
    column_station,
    lag_window,
    observed,
    *,
    rcv_total,
    ref_total,
):
    row_total, k_quarter = receiver_spectra.shape
    k_own, col_total = reference_spectra.shape
    k_total = k_own * rcv_total
    lag_total = observed.shape[2]
    half = lag_total // 2
    members = math.gcd(GROUP, rcv_total)
    irec = row_total * members
    cols = col_total // (members * CHUNKS)
    jj_total = LANES // (2 * irec)
    jp_total = cols // jj_total
    extra = k_quarter // half + 1
    bf16 = jnp.bfloat16
    place = lax.axis_index("rcv")
    mine = place % members
    quarter = lax.axis_index("ref")
    vmem = pl.BlockSpec(memory_space=pltpu.VMEM)
    smem = pl.BlockSpec(memory_space=pltpu.SMEM)
    hbm = pl.BlockSpec(memory_space=pl.ANY)
    scalars = jnp.stack([mine, quarter * col_total, place, quarter]).astype(jnp.int32)

    def params(mib):
        return pltpu.CompilerParams(vmem_limit_bytes=mib * 1024 * 1024)

    def cost(us):
        return pl.CostEstimate(flops=us * 10**9, bytes_accessed=0, transcendentals=0)

    def after(x, *others):
        return lax.optimization_barrier((x,) + others)[0]

    u_own, *sent = pl.pallas_call(
        turn_kernel,
        out_shape=[jax.ShapeDtypeStruct((extra, row_total, half), bf16)]
        + [jax.ShapeDtypeStruct((rcv_total, cols, k_own), bf16)] * CHUNKS,
        in_specs=[smem] + [hbm] * 3,
        out_specs=[hbm] * (1 + CHUNKS),
        scratch_shapes=[
            pltpu.VMEM((k_own, col_total), bf16),
            pltpu.VMEM((1, col_total), jnp.int32),
            pltpu.VMEM(receiver_spectra.shape, bf16),
            pltpu.VMEM((col_total, k_own), bf16),
            pltpu.VMEM((extra, row_total, half), bf16),
            pltpu.SemaphoreType.DMA((2 + k_own // min(k_own, 2 * LANES),)),
            pltpu.SemaphoreType.DMA((CHUNKS * rcv_total + 1,)),
        ],
        compiler_params=params(62),
        cost_estimate=cost(0),
    )(receiver_counts, reference_spectra, reference_counts.reshape(1, col_total), receiver_spectra)
    v_all = []
    for x in sent:
        x = after(x, *v_all[-1:])
        v_all.append(lax.all_to_all(x, "rcv", split_axis=0, concat_axis=0, tiled=True))

    shape = (cols, row_total, half)
    folded = pl.pallas_call(
        fold_kernel,
        out_shape=[jax.ShapeDtypeStruct(shape, bf16)] * (CHUNKS * members),
        in_specs=[smem] + [hbm] * 3,
        out_specs=[hbm] * (CHUNKS * members),
        scratch_shapes=[
            pltpu.VMEM(observed.shape, bf16),
            pltpu.VMEM(lag_window.shape, jnp.int32),
            pltpu.VMEM((1, col_total), jnp.int32),
            pltpu.VMEM((half // LANES * col_total * row_total, LANES), jnp.float32),
            pltpu.VMEM((CHUNKS * members,) + shape, bf16),
            pltpu.SemaphoreType.DMA((row_total + 2,)),
            pltpu.SemaphoreType.DMA((CHUNKS * members,)),
        ],
        compiler_params=params(32),
        cost_estimate=cost(0),
    )(scalars, after(observed, u_own), lag_window, column_station.reshape(1, col_total))
    e_all = [
        [
            x if k == 0 else swap(x, "rcv", rcv_total, k)
            for k, x in enumerate(folded[c * members : (c + 1) * members])
        ]
        for c in range(CHUNKS)
    ]

    near = pl.pallas_call(
        near_kernel,
        out_shape=jax.ShapeDtypeStruct((members, extra, row_total, half), bf16),
        in_specs=[hbm] * members,
        out_specs=hbm,
        scratch_shapes=[pltpu.SemaphoreType.DMA((members,))],
        compiler_params=params(16),
        cost_estimate=cost(0),
    )(u_own, *[swap(u_own, "rcv", rcv_total, k) for k in range(1, members)])
    u_all = [near] + [swap(near, "ref", ref_total, k) for k in range(1, ref_total)]
    group_counts = near[:, extra - 1, :, 0].reshape(irec).astype(jnp.float32)
    own_counts = lax.dynamic_slice_in_dim(
        reference_counts, mine * (cols * CHUNKS), cols * CHUNKS
    ).astype(jnp.float32)

    table = lag_tables(k_total // (2 * S), lag_total)
    lines = jp_total * k_total // (2 * S)
    r_all, got = [], []
    for c in range(CHUNKS):
        counts = own_counts[c * cols : (c + 1) * cols].reshape(jj_total, jp_total).T
        least = jnp.minimum(counts[:, :, None], group_counts[None, None, :])
        inverse = (1.0 / least).reshape(jp_total, jj_total * irec)
        inverse = jnp.concatenate([inverse, inverse], axis=1)
        operands = [v_all[c], *e_all[c], *u_all, *r_all]
        w_part, *r_all = pl.pallas_call(
            functools.partial(pair_kernel, members, ref_total, len(r_all)),
            out_shape=[jax.ShapeDtypeStruct((rcv_total, cols, k_own + LANES), jnp.int16)]
            + [jax.ShapeDtypeStruct((irec, k_quarter), jnp.float32)] * ref_total,
            in_specs=[smem] + [vmem] * 2 + [hbm] * len(operands),
            out_specs=[hbm] * (1 + ref_total),
            scratch_shapes=[
                pltpu.VMEM((lines, LANES), jnp.float32),
                pltpu.VMEM((lines, LANES), jnp.float32),
                pltpu.VMEM((irec, k_total), bf16),
                pltpu.VMEM((irec, k_total), bf16),
                pltpu.VMEM((k_total // LANES, LANES), jnp.float32),
                pltpu.VMEM((ref_total,) + near.shape, bf16),
                pltpu.VMEM((rcv_total, cols, k_own), bf16),
                pltpu.VMEM((members, cols, row_total, half), bf16),
                pltpu.VMEM((ref_total, irec, k_quarter), jnp.float32),
                pltpu.VMEM((rcv_total, cols, k_own + LANES), jnp.int16),
                pltpu.SemaphoreType.DMA((len(operands),)),
                pltpu.SemaphoreType.DMA((rcv_total,)),
            ],
            compiler_params=params(32),
            cost_estimate=cost(10),
        )(scalars, inverse, table, *operands)
        w_part = after(w_part, *got[-1:])
        got.append(lax.all_to_all(w_part, "rcv", split_axis=0, concat_axis=0, tiled=True))

    reference_grad = pl.pallas_call(
        join_kernel,
        out_shape=jax.ShapeDtypeStruct((k_own, col_total), jnp.float32),
        in_specs=[vmem] * (1 + CHUNKS),
        out_specs=vmem,
        compiler_params=params(32),
        cost_estimate=cost(1),
    )(reference_counts.reshape(1, col_total), *got)

    r_sum = r_all[0]
    for k in range(1, ref_total):
        r_sum = r_sum + swap(r_all[k], "ref", ref_total, k)
    parts = [r_sum[k * row_total : (k + 1) * row_total] for k in range(members)]
    r_sum = parts[0]
    for k in range(1, members):
        r_sum = r_sum + swap(parts[k], "rcv", rcv_total, k)
    seg_quarter = jnp.arange(k_quarter, dtype=jnp.int32) % S
    receiver_grad = jnp.where(seg_quarter[None, :] < receiver_counts[:, None], r_sum, 0.0)
    return (receiver_grad, reference_grad)


def solution(mesh):
    return jax.shard_map(
        functools.partial(shards, rcv_total=mesh.shape["rcv"], ref_total=mesh.shape["ref"]),
        mesh=mesh,
        in_specs=(
            P("rcv", "ref"),
            P("rcv", "ref"),
            P("rcv"),
            P("ref"),
            P("ref"),
            P(None, "rcv", "ref"),
            P("rcv", "ref", None),
        ),
        out_specs=(P("rcv", "ref"), P("rcv", "ref")),
        check_vma=False,
    )
```

```python
import functools
import math

import jax
import jax.numpy as jnp
import numpy as np
from jax import lax
from jax.experimental import pallas as pl
from jax.experimental.pallas import tpu as pltpu
from jax.sharding import PartitionSpec as P

L = 512
S = 16
F = 256

env_floor = 0.05
misfit_scale = 0.03125
GROUP = 4
LANES = 128
FB = LANES // (2 * S)
WIDTH = 16
CHUNKS = 2
FIXED = 32000.0


def lag_tables(freq_total, lag_total):
    half = lag_total // 2
    freq_ids = np.arange(freq_total)[:, None]
    phase = 2.0 * np.pi * (freq_ids * np.arange(half)[None, :] % lag_total) / lag_total
    cosine = np.cos(phase) / math.sqrt(freq_total)
    sine = np.sin(phase) / math.sqrt(freq_total)
    back = [np.concatenate([cosine[p::2], sine[p::2]], axis=1) for p in (0, 1)]
    ahead = [np.concatenate([cosine[p::2].T, sine[p::2].T], axis=1) for p in (0, 1)]
    back = [np.concatenate([t[:, :half], t[:, half:]], axis=0) for t in back]
    whole = np.concatenate(ahead + back, axis=0)
    return jnp.asarray(whole.astype(np.float32)).astype(jnp.bfloat16)


def nt(a, b):
    return lax.dot_general(a, b, (((1,), (1,)), ((), ())), preferred_element_type=jnp.float32)


def nn(a, b):
    return jnp.dot(a, b, preferred_element_type=jnp.float32)


def tn(a, b):
    return lax.dot_general(a, b, (((0,), (0,)), ((), ())), preferred_element_type=jnp.float32)


def eye_of(size):
    rows = lax.broadcasted_iota(jnp.int32, (size, size), 0)
    lanes = lax.broadcasted_iota(jnp.int32, (size, size), 1)
    return jnp.where(rows == lanes, 1.0, 0.0).astype(jnp.bfloat16)


def prepare_kernel(c_ref, rcounts_ref, *refs):
    spectra_from, counts_from, rspectra_from, observed_from, window_from, order_from = refs[:6]
    v_to, e_to = refs[6 : 6 + CHUNKS], refs[6 + CHUNKS : -11]
    (
        spectra_ref, counts_ref, rspectra_ref, observed_ref, window_ref, order_ref,
        turned_ref, line_ref, out_ref, sems, out_sems,
    ) = refs[-11:]
    k_own, col_total = spectra_ref.shape
    rcv_total, chunk, _ = v_to[0].shape
    row_total, _, lag_total = observed_ref.shape
    half = lag_total // 2
    members = len(e_to)
    cols = col_total // members
    width = min(k_own, 2 * LANES)
    n_in, n_out = 0, 0

    def fetch(src, dst):
        nonlocal n_in
        copy = pltpu.make_async_copy(src, dst, sems.at[n_in])
        copy.start()
        n_in += 1
        return copy

    def send(src, dst):
        nonlocal n_out
        copy = pltpu.make_async_copy(src, dst, out_sems.at[n_out])
        copy.start()
        n_out += 1
        return copy

    small = [
        fetch(counts_from, counts_ref),
        fetch(window_from, window_ref),
        fetch(order_from, order_ref),
        fetch(rspectra_from, rspectra_ref),
    ]
    spectra = []
    for begin in range(0, k_own, width):
        rows = pl.ds(begin, width)
        spectra.append(fetch(spectra_from.at[rows], spectra_ref.at[rows]))
    seen = [fetch(observed_from.at[i], observed_ref.at[i]) for i in range(row_total)]

    eye = eye_of(col_total)
    seg_ids = lax.broadcasted_iota(jnp.int32, (width, col_total), 0) % S
    for copy in small:
        copy.wait()
    inside = seg_ids < counts_ref[...]
    for n, begin in enumerate(range(0, k_own, width)):
        spectra[n].wait()
        part = spectra_ref[begin : begin + width, :].astype(jnp.float32)
        part = jnp.where(inside, part, 0.0).astype(jnp.bfloat16)
        turned_ref[:, begin : begin + width] = nt(eye, part).astype(jnp.bfloat16)
    outs = []
    for c in range(CHUNKS):
        for dest in range(rcv_total):
            first = dest % members * cols + c * chunk
            outs.append(send(turned_ref.at[pl.ds(first, chunk)], v_to[c].at[dest]))

    window = jnp.concatenate([window_ref[0], window_ref[1]], axis=0).astype(jnp.float32).T
    station = lax.broadcasted_iota(jnp.int32, (col_total, col_total), 0) + c_ref[1]
    pick = jnp.where(station == order_ref[...], 1.0, 0.0).astype(jnp.bfloat16)
    lag_ids = lax.broadcasted_iota(jnp.int32, (col_total, half), 1).astype(jnp.float32)
    lines = col_total * row_total
    for i in range(row_total):
        seen[i].wait()
        begin = window[:, i : i + 1]
        end = begin + window[:, row_total + i : row_total + i + 1]
        values = observed_ref[i].astype(jnp.float32)
        low = (lag_ids >= begin) & (lag_ids < end)
        high = (lag_ids + half >= begin) & (lag_ids + half < end)
        folded = jnp.where(low, values[:, :half], jnp.where(high, -values[:, half:], 0.0))
        moved = nn(pick, folded.astype(jnp.bfloat16))
        for h in range(half // LANES):
            line_ref[pl.ds(h * lines + i, col_total, stride=row_total), :] = moved[
                :, h * LANES : (h + 1) * LANES
            ]
    row_ids = lax.broadcasted_iota(jnp.int32, (row_total, half), 0)
    counts = jnp.zeros((row_total, half), jnp.int32)
    for i in range(row_total):
        counts = jnp.where(row_ids == i, rcounts_ref[i], counts)
    seg_ids = lax.broadcasted_iota(jnp.int32, (row_total, half), 1) % S
    pieces = rspectra_ref.shape[1] // half
    extra = []
    for n in range(pieces):
        part = rspectra_ref[:, n * half : (n + 1) * half].astype(jnp.float32)
        extra.append(jnp.where(seg_ids < counts, part, 0.0).astype(jnp.bfloat16))
    extra.append(counts.astype(jnp.float32).astype(jnp.bfloat16))
    for k in range(members):
        for n, part in enumerate(extra):
            out_ref[k, cols + n] = part
        first = (c_ref[0] ^ k) * (cols * row_total)
        for h in range(half // LANES):
            begin = pl.multiple_of(h * lines + first, cols * row_total)
            rows = line_ref[pl.ds(begin, cols * row_total), :]
            out_ref[k, :cols, :, h * LANES : (h + 1) * LANES] = rows.reshape(
                cols, row_total, LANES
            ).astype(jnp.bfloat16)
        outs.append(send(out_ref.at[k], e_to[k]))
    for copy in outs:
        copy.wait()


def near_kernel(*refs):
    *parts, out_ref, sems = refs
    extra = out_ref.shape[1]
    copies = []
    for k, ref in enumerate(parts):
        rows = ref.at[pl.ds(ref.shape[0] - extra, extra)]
        copies.append(pltpu.make_async_copy(rows, out_ref.at[k], sems.at[k]))
        copies[-1].start()
    for copy in copies:
        copy.wait()


def pair_kernel(chunk, n_e, n_r, n_in, n_out, c_ref, invn_ref, table_ref, v_from, *refs):
    refs = list(refs)
    e_from, u_from = refs[:n_e], refs[n_e : n_e + n_r]
    r_from = refs[n_e + n_r : n_e + n_r + n_in]
    w_to, *r_to = refs[n_e + n_r + n_in : n_e + n_r + n_in + n_out + 1]
    (
        x_ref, z_ref, plain_ref, turned_ref, code_ref, u_ref, v_ref, e_ref, r_ref, w_ref,
        sems, w_sems,
    ) = refs[n_e + n_r + n_in + n_out + 1 :]

    src_total, col_total, k_own = v_ref.shape
    ref_total, irec, k_quarter = r_ref.shape
    jj_total = LANES // (2 * irec)
    jp_total = col_total // jj_total
    k_total = src_total * k_own
    half_f = k_total // (4 * S)
    freq_total = 2 * half_f
    blocks = k_total // LANES
    own_blocks = k_own // LANES
    quarter_blocks = k_quarter // LANES

    quarter_me = c_ref[3]
    early = [pltpu.make_async_copy(v_from, v_ref, sems.at[0])]
    for k, ref in enumerate(u_from):
        early.append(pltpu.make_async_copy(ref, u_ref.at[quarter_me ^ k], sems.at[1 + k]))
    late = [
        pltpu.make_async_copy(
            ref.at[pl.ds(chunk * col_total, col_total)], e_ref.at[k], sems.at[1 + n_r + k]
        )
        for k, ref in enumerate(e_from)
    ]
    last = [
        pltpu.make_async_copy(ref, r_ref, sems.at[1 + n_r + n_e]) for ref in r_from
    ]
    for copy in early + late + last:
        copy.start()
    half = e_ref.shape[-1]
    eye = eye_of(half)
    table_y = [table_ref[p * half : (p + 1) * half, :] for p in range(2)]
    table_z = []
    for p in range(2):
        begin = 2 * half + p * 2 * half_f
        parts = [table_ref[begin + n * half_f : begin + (n + 1) * half_f, :] for n in range(2)]
        table_z.append(jnp.concatenate(parts, axis=1))

    group_ids = lax.broadcasted_iota(jnp.int32, (jp_total, LANES), 1) // (2 * S)
    first_part = lax.broadcasted_iota(jnp.int32, (irec, LANES), 1) % (2 * S) < S

    def lanes_of(fb, per):
        return fb // per, pl.multiple_of(fb % per * LANES, LANES)

    def v_block(fb):
        src, off = lanes_of(fb, own_blocks)
        parts = [
            v_ref[src, jj * jp_total : (jj + 1) * jp_total, pl.ds(off, LANES)]
            for jj in range(jj_total)
        ]
        zero = jnp.zeros((jp_total, LANES), jnp.bfloat16)
        rows = [
            jnp.concatenate([jnp.where(group_ids == f, part, zero) for part in parts], axis=1)
            for f in range(FB)
        ]
        return jnp.concatenate(rows, axis=0)

    def u_block(parts):
        zero = jnp.zeros((irec, LANES), jnp.bfloat16)
        return jnp.concatenate(
            [
                jnp.concatenate([part if k == jj else zero for k in range(jj_total)], axis=1)
                for part in parts
                for jj in range(jj_total)
            ],
            axis=0,
        )

    def place(fb, f):
        return pl.ds((f % 2) * half_f + fb * (FB // 2) + f // 2, jp_total, stride=freq_total)

    def forward(fb, _):
        lanes = pl.ds(pl.multiple_of(fb * LANES, LANES), LANES)
        quarter, off = lanes_of(fb, quarter_blocks)
        piece, off = off // half, pl.multiple_of(off % half, LANES)
        wide = u_ref[quarter, :, piece, :, pl.ds(off, LANES)].astype(jnp.float32)
        wide = wide.reshape(irec, LANES)
        part = wide.astype(jnp.bfloat16)
        plain_ref[:, lanes] = part
        crossed = jnp.where(first_part, pltpu.roll(wide, LANES - S, 1), -pltpu.roll(wide, S, 1))
        crossed = crossed.astype(jnp.bfloat16)
        turned_ref[:, lanes] = crossed
        out = nt(v_block(fb), u_block([part, crossed]))
        scale = invn_ref[...]
        for f in range(FB):
            x_ref[place(fb, f), :] = out[f * jp_total : (f + 1) * jp_total] * scale
        return 0

    for copy in early:
        copy.wait()
    lax.fori_loop(0, blocks, forward, 0, unroll=64)

    lane_ids = lax.broadcasted_iota(jnp.int32, (1, LANES), 1)
    sign = jnp.where(lane_ids < LANES // 2, -1.0, 1.0).astype(jnp.float32)

    sign = sign.astype(jnp.bfloat16)

    def pairs(step, _):
        cols = [step * WIDTH + k for k in range(WIDTH)]
        rhs_e, rhs_o, obs = [], [], []
        for jp in cols:
            x = x_ref[pl.ds(pl.multiple_of(jp * freq_total, freq_total), freq_total), :]
            plain = x.astype(jnp.bfloat16)
            turned = pltpu.roll(x, LANES // 2, 1).astype(jnp.bfloat16) * sign
            rhs_e.append(jnp.concatenate([plain[:half_f], turned[:half_f]], axis=0))
            rhs_o.append(jnp.concatenate([plain[half_f:], turned[half_f:]], axis=0))
            rows = [
                e_ref[:, jj * jp_total + jp].astype(jnp.float32).reshape(irec, half)
                for jj in range(jj_total)
            ]
            rows = jnp.concatenate(rows, axis=0).astype(jnp.bfloat16)
            obs += [rows, rows]
        even = nn(table_y[0], jnp.concatenate(rhs_e, axis=1))
        odd = nn(table_y[1], jnp.concatenate(rhs_o, axis=1))
        seen = nt(eye, jnp.concatenate(obs, axis=0))
        g_e, g_o = [], []
        for k in range(WIDTH):
            lanes = slice(k * LANES, (k + 1) * LANES)
            e, d0, d1 = seen[:, lanes], even[:, lanes], odd[:, lanes]
            d = jnp.where(e < 0.0, d0 + d1, d0 - d1)
            power = d * d
            power = power + (pltpu.roll(power, LANES // 2, 1) + env_floor)
            g = d * (1.0 - jnp.abs(e) * lax.rsqrt(power))
            side = jnp.where(e < 0.0, 1.0, jnp.where(e > 0.0, -1.0, 0.0)).astype(jnp.bfloat16)
            turned = pltpu.roll(g, LANES // 2, 1).astype(jnp.bfloat16)
            g_side = g.astype(jnp.bfloat16) * side
            t_side = turned * (side * -sign)
            g_e.append(jnp.concatenate([g_side * side, t_side * side], axis=0))
            g_o.append(jnp.concatenate([g_side, t_side], axis=0))
        z_e = nn(table_z[0], jnp.concatenate(g_e, axis=1))
        z_o = nn(table_z[1], jnp.concatenate(g_o, axis=1))
        for k, jp in enumerate(cols):
            lanes = slice(k * LANES, (k + 1) * LANES)
            scale = invn_ref[pl.ds(jp, 1), :] * misfit_scale
            base = pl.multiple_of(jp * freq_total, freq_total)
            z_ref[pl.ds(base, half_f), :] = z_e[:, lanes] * scale
            z_ref[pl.ds(base + half_f, half_f), :] = z_o[:, lanes] * scale
        return 0

    for copy in late:
        copy.wait()
    lax.fori_loop(0, jp_total // WIDTH, pairs, 0, unroll=2)

    def backward(fb):
        z = jnp.concatenate([z_ref[place(fb, f), :] for f in range(FB)], axis=0)
        z = z.astype(jnp.bfloat16)
        lanes = pl.ds(pl.multiple_of(fb * LANES, LANES), LANES)
        w = nn(z, u_block([plain_ref[:, lanes], turned_ref[:, lanes]]))
        totals = []
        for jj in range(jj_total):
            lanes = slice(jj * LANES, (jj + 1) * LANES)
            total = w[:jp_total, lanes]
            for f in range(1, FB):
                total = jnp.where(group_ids == f, w[f * jp_total : (f + 1) * jp_total, lanes], total)
            totals.append(total)
        total = jnp.concatenate(totals, axis=0)
        largest = jnp.max(jnp.abs(total), axis=0, keepdims=True)
        power = jnp.ceil(jnp.log2(jnp.maximum(largest, 1e-30)))
        code_ref[pl.ds(fb, 1), :] = power
        fixed = jnp.round(total * (jnp.exp2(-power) * FIXED)).astype(jnp.int32)
        src, off = lanes_of(fb, own_blocks)
        w_ref[src, :, pl.ds(off, LANES)] = fixed.astype(jnp.int16)
        r = tn(z, v_block(fb))
        sums = []
        for q in range(2):
            total = None
            for jj in range(jj_total):
                begin = (q * jj_total + jj) * irec
                part = r[begin : begin + irec, jj * LANES : (jj + 1) * LANES]
                total = part if total is None else total + part
            sums.append(total)
        crossed = jnp.where(
            first_part, -pltpu.roll(sums[1], LANES - S, 1), pltpu.roll(sums[1], S, 1)
        )
        quarter, off = lanes_of(fb, quarter_blocks)
        lanes = pl.ds(off, LANES)
        total = sums[0] + crossed
        r_ref[quarter, :, lanes] = r_ref[quarter, :, lanes] + total if r_from else total

    def w_copy(src):
        return pltpu.make_async_copy(w_ref.at[src], w_to.at[src], w_sems.at[src])

    def from_owner(src, _):
        for b in range(own_blocks):
            backward(src * own_blocks + b)
        codes = code_ref[pl.ds(src * own_blocks, own_blocks), :]
        codes = jnp.concatenate(
            [codes, jnp.zeros((col_total - own_blocks, LANES), jnp.float32)], axis=0
        )
        w_ref[src, :, k_own:] = codes.astype(jnp.int32).astype(jnp.int16)
        w_copy(src).start()
        return 0

    for copy in last:
        copy.wait()
    lax.fori_loop(0, src_total, from_owner, 0, unroll=4)
    outs = [
        pltpu.make_async_copy(r_ref if n_out == 1 else r_ref.at[quarter_me ^ k], ref, sems.at[k])
        for k, ref in enumerate(r_to)
    ]
    for copy in outs:
        copy.start()
    for copy in outs:
        copy.wait()
    for src in range(src_total):
        w_copy(src).wait()


def join_kernel(count_ref, *refs):
    *got_refs, out_ref = refs
    src_total, cols, _ = got_refs[0].shape
    k_own, col_total = out_ref.shape
    members = col_total // (cols * len(got_refs))
    seg_ids = lax.broadcasted_iota(jnp.int32, (LANES, col_total), 0) % S
    inside = seg_ids < count_ref[...]
    scales = [
        [
            jnp.exp2(ref[src, :16, k_own:].astype(jnp.int32).astype(jnp.float32)) * (1.0 / FIXED)
            for src in range(src_total)
        ]
        for ref in got_refs
    ]
    for b in range(k_own // LANES):
        rows = []
        for m in range(members):
            for ref, scale in zip(got_refs, scales):
                total = None
                for src in range(m, src_total, members):
                    part = ref[src, :, b * LANES : (b + 1) * LANES]
                    part = part.astype(jnp.int32).astype(jnp.float32) * scale[src][b : b + 1]
                    total = part if total is None else total + part
                rows.append(total)
        whole = jnp.concatenate(rows, axis=0).T
        out_ref[b * LANES : (b + 1) * LANES, :] = jnp.where(inside, whole, 0.0)


def swap(x, axis, total, k):
    return lax.ppermute(x, axis, [(r, r ^ k) for r in range(total)])


def shards(
    receiver_spectra,
    reference_spectra,
    receiver_counts,
    reference_counts,
    column_station,
    lag_window,
    observed,
    *,
    rcv_total,
    ref_total,
):
    row_total, k_quarter = receiver_spectra.shape
    k_own, col_total = reference_spectra.shape
    k_total = k_own * rcv_total
    lag_total = observed.shape[2]
    half = lag_total // 2
    members = math.gcd(GROUP, rcv_total)
    irec = row_total * members
    cols = col_total // (members * CHUNKS)
    jj_total = LANES // (2 * irec)
    jp_total = cols // jj_total
    extra = k_quarter // half + 1
    bf16 = jnp.bfloat16
    place = lax.axis_index("rcv")
    mine = place % members
    quarter = lax.axis_index("ref")
    vmem = pl.BlockSpec(memory_space=pltpu.VMEM)
    smem = pl.BlockSpec(memory_space=pltpu.SMEM)
    hbm = pl.BlockSpec(memory_space=pl.ANY)
    scalars = jnp.stack([mine, quarter * col_total, place, quarter]).astype(jnp.int32)

    def params(mib):
        return pltpu.CompilerParams(vmem_limit_bytes=mib * 1024 * 1024)

    def cost(us):
        return pl.CostEstimate(flops=us * 10**9, bytes_accessed=0, transcendentals=0)

    def after(x, *others):
        return lax.optimization_barrier((x,) + others)[0]

    shape = (cols * CHUNKS + extra, row_total, half)
    prepared = pl.pallas_call(
        prepare_kernel,
        out_shape=[jax.ShapeDtypeStruct((rcv_total, cols, k_own), bf16)] * CHUNKS
        + [jax.ShapeDtypeStruct(shape, bf16)] * members,
        in_specs=[smem] * 2 + [hbm] * 6,
        out_specs=[hbm] * (CHUNKS + members),
        scratch_shapes=[
            pltpu.VMEM((k_own, col_total), bf16),
            pltpu.VMEM((1, col_total), jnp.int32),
            pltpu.VMEM(receiver_spectra.shape, bf16),
            pltpu.VMEM(observed.shape, bf16),
            pltpu.VMEM(lag_window.shape, jnp.int32),
            pltpu.VMEM((1, col_total), jnp.int32),
            pltpu.VMEM((col_total, k_own), bf16),
            pltpu.VMEM((half // LANES * col_total * row_total, LANES), jnp.float32),
            pltpu.VMEM((members,) + shape, bf16),
            pltpu.SemaphoreType.DMA((4 + k_own // min(k_own, 2 * LANES) + row_total,)),
            pltpu.SemaphoreType.DMA((CHUNKS * rcv_total + members,)),
        ],
        compiler_params=params(62),
        cost_estimate=cost(0),
    )(
        scalars,
        receiver_counts,
        reference_spectra,
        reference_counts.reshape(1, col_total),
        receiver_spectra,
        observed,
        lag_window,
        column_station.reshape(1, col_total),
    )
    sent, folded = prepared[:CHUNKS], prepared[CHUNKS:]
    v_all = []
    for x in sent:
        x = after(x, *v_all[-1:])
        v_all.append(lax.all_to_all(x, "rcv", split_axis=0, concat_axis=0, tiled=True))
    e_all = [folded[0]] + [swap(folded[k], "rcv", rcv_total, k) for k in range(1, members)]

    near = pl.pallas_call(
        near_kernel,
        out_shape=jax.ShapeDtypeStruct((members, extra, row_total, half), bf16),
        in_specs=[hbm] * members,
        out_specs=hbm,
        scratch_shapes=[pltpu.SemaphoreType.DMA((members,))],
        compiler_params=params(16),
        cost_estimate=cost(0),
    )(*e_all)
    u_all = [near] + [swap(near, "ref", ref_total, k) for k in range(1, ref_total)]
    group_counts = near[:, extra - 1, :, 0].reshape(irec).astype(jnp.float32)
    own_counts = lax.dynamic_slice_in_dim(
        reference_counts, mine * (cols * CHUNKS), cols * CHUNKS
    ).astype(jnp.float32)

    table = lag_tables(k_total // (2 * S), lag_total)
    lines = jp_total * k_total // (2 * S)
    r_all, got = [], []
    for c in range(CHUNKS):
        counts = own_counts[c * cols : (c + 1) * cols].reshape(jj_total, jp_total).T
        least = jnp.minimum(counts[:, :, None], group_counts[None, None, :])
        inverse = (1.0 / least).reshape(jp_total, jj_total * irec)
        inverse = jnp.concatenate([inverse, inverse], axis=1)
        operands = [v_all[c], *e_all, *u_all, *r_all]
        if c < CHUNKS - 1:
            r_shapes = [jax.ShapeDtypeStruct((ref_total, irec, k_quarter), jnp.float32)]
        else:
            r_shapes = [jax.ShapeDtypeStruct((irec, k_quarter), jnp.float32)] * ref_total
        w_part, *r_all = pl.pallas_call(
            functools.partial(pair_kernel, c, members, ref_total, len(r_all), len(r_shapes)),
            out_shape=[jax.ShapeDtypeStruct((rcv_total, cols, k_own + LANES), jnp.int16)]
            + r_shapes,
            in_specs=[smem] + [vmem] * 2 + [hbm] * len(operands),
            out_specs=[hbm] * (1 + len(r_shapes)),
            scratch_shapes=[
                pltpu.VMEM((lines, LANES), jnp.float32),
                pltpu.VMEM((lines, LANES), jnp.float32),
                pltpu.VMEM((irec, k_total), bf16),
                pltpu.VMEM((irec, k_total), bf16),
                pltpu.VMEM((k_total // LANES, LANES), jnp.float32),
                pltpu.VMEM((ref_total,) + near.shape, bf16),
                pltpu.VMEM((rcv_total, cols, k_own), bf16),
                pltpu.VMEM((members, cols, row_total, half), bf16),
                pltpu.VMEM((ref_total, irec, k_quarter), jnp.float32),
                pltpu.VMEM((rcv_total, cols, k_own + LANES), jnp.int16),
                pltpu.SemaphoreType.DMA((len(operands),)),
                pltpu.SemaphoreType.DMA((rcv_total,)),
            ],
            compiler_params=params(32),
            cost_estimate=cost(10),
        )(scalars, inverse, table, *operands)
        w_part = after(w_part, *got[-1:])
        got.append(lax.all_to_all(w_part, "rcv", split_axis=0, concat_axis=0, tiled=True))

    reference_grad = pl.pallas_call(
        join_kernel,
        out_shape=jax.ShapeDtypeStruct((k_own, col_total), jnp.float32),
        in_specs=[vmem] * (1 + CHUNKS),
        out_specs=vmem,
        compiler_params=params(32),
        cost_estimate=cost(1),
    )(reference_counts.reshape(1, col_total), *got)

    r_sum = r_all[0]
    for k in range(1, ref_total):
        r_sum = r_sum + swap(r_all[k], "ref", ref_total, k)
    parts = [r_sum[k * row_total : (k + 1) * row_total] for k in range(members)]
    r_sum = parts[0]
    for k in range(1, members):
        r_sum = r_sum + swap(parts[k], "rcv", rcv_total, k)
    seg_quarter = jnp.arange(k_quarter, dtype=jnp.int32) % S
    receiver_grad = jnp.where(seg_quarter[None, :] < receiver_counts[:, None], r_sum, 0.0)
    return (receiver_grad, reference_grad)


def solution(mesh):
    return jax.shard_map(
        functools.partial(shards, rcv_total=mesh.shape["rcv"], ref_total=mesh.shape["ref"]),
        mesh=mesh,
        in_specs=(
            P("rcv", "ref"),
            P("rcv", "ref"),
            P("rcv"),
            P("ref"),
            P("ref"),
            P(None, "rcv", "ref"),
            P("rcv", "ref", None),
        ),
        out_specs=(P("rcv", "ref"), P("rcv", "ref")),
        check_vma=False,
    )
```

```python
import functools
import math

import jax
import jax.numpy as jnp
import numpy as np
from jax import lax
from jax.experimental import pallas as pl
from jax.experimental.pallas import tpu as pltpu
from jax.sharding import PartitionSpec as P

L = 512
S = 16
F = 256

env_floor = 0.05
misfit_scale = 0.03125
GROUP = 4
LANES = 128
FB = LANES // (2 * S)
WIDTH = 16
FIXED = 32000.0
PAD = 8
CODES = 16


def lag_tables(freq_total, lag_total):
    half = lag_total // 2
    freq_ids = np.arange(freq_total)[:, None]
    phase = 2.0 * np.pi * (freq_ids * np.arange(half)[None, :] % lag_total) / lag_total
    cosine = np.cos(phase) / math.sqrt(freq_total)
    sine = np.sin(phase) / math.sqrt(freq_total)
    back = [np.concatenate([cosine[p::2], sine[p::2]], axis=1) for p in (0, 1)]
    ahead = [np.concatenate([cosine[p::2].T, sine[p::2].T], axis=1) for p in (0, 1)]
    back = [np.concatenate([t[:, :half], t[:, half:]], axis=0) for t in back]
    whole = np.concatenate(ahead + back, axis=0)
    return jnp.asarray(whole.astype(np.float32)).astype(jnp.bfloat16)


def nt(a, b):
    return lax.dot_general(a, b, (((1,), (1,)), ((), ())), preferred_element_type=jnp.float32)


def nn(a, b):
    return jnp.dot(a, b, preferred_element_type=jnp.float32)


def tn(a, b):
    return lax.dot_general(a, b, (((0,), (0,)), ((), ())), preferred_element_type=jnp.float32)


def eye_of(size):
    rows = lax.broadcasted_iota(jnp.int32, (size, size), 0)
    lanes = lax.broadcasted_iota(jnp.int32, (size, size), 1)
    return jnp.where(rows == lanes, 1.0, 0.0).astype(jnp.bfloat16)


def turn_kernel(spectra_from, counts_from, v_to, spectra_ref, counts_ref, turned_ref, sems):
    k_own, col_total = spectra_ref.shape
    rcv_total, cols, _ = v_to.shape
    members = col_total // cols
    width = min(k_own, 2 * LANES)
    copies = [pltpu.make_async_copy(counts_from, counts_ref, sems.at[0])]
    for n, begin in enumerate(range(0, k_own, width)):
        rows = pl.ds(begin, width)
        copies.append(
            pltpu.make_async_copy(spectra_from.at[rows], spectra_ref.at[rows], sems.at[1 + n])
        )
    for copy in copies:
        copy.start()
    eye = eye_of(col_total)
    seg_ids = lax.broadcasted_iota(jnp.int32, (width, col_total), 0) % S
    copies[0].wait()
    inside = seg_ids < counts_ref[...]
    for n, begin in enumerate(range(0, k_own, width)):
        copies[1 + n].wait()
        part = spectra_ref[begin : begin + width, :].astype(jnp.float32)
        part = jnp.where(inside, part, 0.0).astype(jnp.bfloat16)
        turned_ref[:, begin : begin + width] = nt(eye, part).astype(jnp.bfloat16)
    copies = [
        pltpu.make_async_copy(
            turned_ref.at[pl.ds(dest % members * cols, cols)], v_to.at[dest], sems.at[dest]
        )
        for dest in range(rcv_total)
    ]
    for copy in copies:
        copy.start()
    for copy in copies:
        copy.wait()


def fold_kernel(c_ref, rcounts_ref, observed_from, rspectra_from, window_from, order_from, *rest):
    u_to, *out_to = rest[:-9]
    (
        observed_ref, rspectra_ref, window_ref, order_ref, line_ref, out_ref, u_ref, sems, out_sems,
    ) = rest[-9:]
    row_total, col_total, lag_total = observed_ref.shape
    half = lag_total // 2
    members = len(out_to)
    cols = col_total // members
    lines = col_total * row_total
    quarter = rspectra_ref.shape[1]
    copies = [
        pltpu.make_async_copy(src, dst, sems.at[row_total + n])
        for n, (src, dst) in enumerate(
            [(window_from, window_ref), (order_from, order_ref), (rspectra_from, rspectra_ref)]
        )
    ] + [
        pltpu.make_async_copy(observed_from.at[i], observed_ref.at[i], sems.at[i])
        for i in range(row_total)
    ]
    for copy in copies:
        copy.start()
    for copy in copies[:3]:
        copy.wait()
    row_ids = lax.broadcasted_iota(jnp.int32, (row_total, half), 0)
    counts = jnp.zeros((row_total, half), jnp.int32)
    for i in range(row_total):
        counts = jnp.where(row_ids == i, rcounts_ref[i], counts)
    seg_ids = lax.broadcasted_iota(jnp.int32, (row_total, half), 1) % S
    pieces = quarter // half
    for n in range(pieces):
        part = rspectra_ref[:, n * half : (n + 1) * half].astype(jnp.float32)
        u_ref[n] = jnp.where(seg_ids < counts, part, 0.0).astype(jnp.bfloat16)
    u_ref[pieces] = counts.astype(jnp.float32).astype(jnp.bfloat16)
    u_copy = pltpu.make_async_copy(u_ref, u_to, out_sems.at[members])
    u_copy.start()
    window = jnp.concatenate([window_ref[0], window_ref[1]], axis=0).astype(jnp.float32).T
    station = lax.broadcasted_iota(jnp.int32, (col_total, col_total), 0) + c_ref[1]
    pick = jnp.where(station == order_ref[...], 1.0, 0.0).astype(jnp.bfloat16)
    lag_ids = lax.broadcasted_iota(jnp.int32, (col_total, half), 1).astype(jnp.float32)
    for i in range(row_total):
        copies[3 + i].wait()
        begin = window[:, i : i + 1]
        end = begin + window[:, row_total + i : row_total + i + 1]
        values = observed_ref[i].astype(jnp.float32)
        low = (lag_ids >= begin) & (lag_ids < end)
        high = (lag_ids + half >= begin) & (lag_ids + half < end)
        folded = jnp.where(low, values[:, :half], jnp.where(high, -values[:, half:], 0.0))
        moved = nn(pick, folded.astype(jnp.bfloat16))
        for h in range(half // LANES):
            line_ref[pl.ds(h * lines + i, col_total, stride=row_total), :] = moved[
                :, h * LANES : (h + 1) * LANES
            ]
    mine = c_ref[0]
    copies = []
    for k in range(members):
        first = (mine ^ k) * (cols * row_total)
        for h in range(half // LANES):
            begin = pl.multiple_of(h * lines + first, cols * row_total)
            rows = line_ref[pl.ds(begin, cols * row_total), :]
            out_ref[k, :, :, h * LANES : (h + 1) * LANES] = rows.reshape(
                cols, row_total, LANES
            ).astype(jnp.bfloat16)
        copies.append(pltpu.make_async_copy(out_ref.at[k], out_to[k], out_sems.at[k]))
        copies[-1].start()
    for copy in copies + [u_copy]:
        copy.wait()


def near_kernel(*refs):
    *parts, out_ref, sems = refs
    copies = [
        pltpu.make_async_copy(ref, out_ref.at[k], sems.at[k]) for k, ref in enumerate(parts)
    ]
    for copy in copies:
        copy.start()
    for copy in copies:
        copy.wait()


def pair_kernel(n_e, n_r, c_ref, invn_ref, table_ref, v_from, *refs):
    refs = list(refs)
    e_from, u_from = refs[:n_e], refs[n_e : n_e + n_r]
    w_to, *r_to = refs[n_e + n_r : n_e + 2 * n_r + 1]
    (
        x_ref, z_ref, plain_ref, turned_ref, code_ref, u_ref, v_ref, e_ref, r_ref, w_ref,
        sems, w_sems,
    ) = refs[n_e + 2 * n_r + 1 :]

    src_total, col_total, k_own = v_ref.shape
    ref_total, irec, k_quarter = r_ref.shape
    jj_total = LANES // (2 * irec)
    jp_total = col_total // jj_total
    k_total = src_total * k_own
    half_f = k_total // (4 * S)
    freq_total = 2 * half_f
    pitch = freq_total + PAD
    blocks = k_total // LANES
    own_blocks = k_own // LANES
    quarter_blocks = k_quarter // LANES

    quarter_me = c_ref[3]
    early = [pltpu.make_async_copy(v_from, v_ref, sems.at[0])]
    for k, ref in enumerate(u_from):
        early.append(pltpu.make_async_copy(ref, u_ref.at[quarter_me ^ k], sems.at[1 + k]))
    late = [
        pltpu.make_async_copy(ref, e_ref.at[k], sems.at[1 + n_r + k])
        for k, ref in enumerate(e_from)
    ]
    for copy in early + late:
        copy.start()
    half = e_ref.shape[-1]
    eye = eye_of(half)
    table_y = [table_ref[p * half : (p + 1) * half, :] for p in range(2)]
    table_z = []
    for p in range(2):
        begin = 2 * half + p * 2 * half_f
        parts = [table_ref[begin + n * half_f : begin + (n + 1) * half_f, :] for n in range(2)]
        table_z.append(jnp.concatenate(parts, axis=1))

    group_ids = lax.broadcasted_iota(jnp.int32, (jp_total, LANES), 1) // (2 * S)
    first_part = lax.broadcasted_iota(jnp.int32, (irec, LANES), 1) % (2 * S) < S

    def lanes_of(fb, per):
        return fb // per, pl.multiple_of(fb % per * LANES, LANES)

    def v_block(fb):
        src, off = lanes_of(fb, own_blocks)
        parts = [
            v_ref[src, jj * jp_total : (jj + 1) * jp_total, pl.ds(off, LANES)]
            for jj in range(jj_total)
        ]
        zero = jnp.zeros((jp_total, LANES), jnp.bfloat16)
        rows = [
            jnp.concatenate([jnp.where(group_ids == f, part, zero) for part in parts], axis=1)
            for f in range(FB)
        ]
        return jnp.concatenate(rows, axis=0)

    def u_block(parts):
        zero = jnp.zeros((irec, LANES), jnp.bfloat16)
        return jnp.concatenate(
            [
                jnp.concatenate([part if k == jj else zero for k in range(jj_total)], axis=1)
                for part in parts
                for jj in range(jj_total)
            ],
            axis=0,
        )

    def place(fb, f):
        return pl.ds((f % 2) * half_f + fb * (FB // 2) + f // 2, jp_total, stride=pitch)

    def forward(fb, _):
        lanes = pl.ds(pl.multiple_of(fb * LANES, LANES), LANES)
        quarter, off = lanes_of(fb, quarter_blocks)
        piece, off = off // half, pl.multiple_of(off % half, LANES)
        wide = u_ref[quarter, :, piece, :, pl.ds(off, LANES)].astype(jnp.float32)
        wide = wide.reshape(irec, LANES)
        part = wide.astype(jnp.bfloat16)
        plain_ref[:, lanes] = part
        crossed = jnp.where(first_part, pltpu.roll(wide, LANES - S, 1), -pltpu.roll(wide, S, 1))
        crossed = crossed.astype(jnp.bfloat16)
        turned_ref[:, lanes] = crossed
        out = nt(v_block(fb), u_block([part, crossed]))
        scale = invn_ref[...]
        for f in range(FB):
            x_ref[place(fb, f), :] = out[f * jp_total : (f + 1) * jp_total] * scale
        return 0

    for copy in early:
        copy.wait()
    lax.fori_loop(0, blocks, forward, 0, unroll=64)

    lane_ids = lax.broadcasted_iota(jnp.int32, (1, LANES), 1)
    sign = jnp.where(lane_ids < LANES // 2, -1.0, 1.0).astype(jnp.float32)

    sign = sign.astype(jnp.bfloat16)

    def pairs(step, _):
        cols = [step * WIDTH + k for k in range(WIDTH)]
        rhs_e, rhs_o, obs = [], [], []
        for jp in cols:
            x = x_ref[pl.ds(pl.multiple_of(jp * pitch, PAD), freq_total), :]
            plain = x.astype(jnp.bfloat16)
            turned = pltpu.roll(x, LANES // 2, 1).astype(jnp.bfloat16) * sign
            rhs_e.append(jnp.concatenate([plain[:half_f], turned[:half_f]], axis=0))
            rhs_o.append(jnp.concatenate([plain[half_f:], turned[half_f:]], axis=0))
            rows = [
                e_ref[:, jj * jp_total + jp].astype(jnp.float32).reshape(irec, half)
                for jj in range(jj_total)
            ]
            rows = jnp.concatenate(rows, axis=0).astype(jnp.bfloat16)
            obs += [rows, rows]
        even = nn(table_y[0], jnp.concatenate(rhs_e, axis=1))
        odd = nn(table_y[1], jnp.concatenate(rhs_o, axis=1))
        seen = nt(eye, jnp.concatenate(obs, axis=0))
        g_e, g_o = [], []
        for k in range(WIDTH):
            lanes = slice(k * LANES, (k + 1) * LANES)
            e, d0, d1 = seen[:, lanes], even[:, lanes], odd[:, lanes]
            d = jnp.where(e < 0.0, d0 + d1, d0 - d1)
            power = d * d
            power = power + (pltpu.roll(power, LANES // 2, 1) + env_floor)
            g = d * (1.0 - jnp.abs(e) * lax.rsqrt(power))
            side = jnp.where(e < 0.0, 1.0, jnp.where(e > 0.0, -1.0, 0.0)).astype(jnp.bfloat16)
            turned = pltpu.roll(g, LANES // 2, 1).astype(jnp.bfloat16)
            g_side = g.astype(jnp.bfloat16) * side
            t_side = turned * (side * -sign)
            g_e.append(jnp.concatenate([g_side * side, t_side * side], axis=0))
            g_o.append(jnp.concatenate([g_side, t_side], axis=0))
        z_e = nn(table_z[0], jnp.concatenate(g_e, axis=1))
        z_o = nn(table_z[1], jnp.concatenate(g_o, axis=1))
        for k, jp in enumerate(cols):
            lanes = slice(k * LANES, (k + 1) * LANES)
            scale = invn_ref[pl.ds(jp, 1), :] * misfit_scale
            base = pl.multiple_of(jp * pitch, PAD)
            z_ref[pl.ds(base, half_f), :] = z_e[:, lanes] * scale
            z_ref[pl.ds(base + half_f, half_f), :] = z_o[:, lanes] * scale
        return 0

    for copy in late:
        copy.wait()
    lax.fori_loop(0, jp_total // WIDTH, pairs, 0, unroll=2)

    def backward(src, b):
        fb = src * own_blocks + b
        z = jnp.concatenate([z_ref[place(fb, f), :] for f in range(FB)], axis=0)
        z = z.astype(jnp.bfloat16)
        lanes = pl.ds(pl.multiple_of(fb * LANES, LANES), LANES)
        w = nn(z, u_block([plain_ref[:, lanes], turned_ref[:, lanes]]))
        totals = []
        for jj in range(jj_total):
            lanes = slice(jj * LANES, (jj + 1) * LANES)
            total = w[:jp_total, lanes]
            for f in range(1, FB):
                total = jnp.where(group_ids == f, w[f * jp_total : (f + 1) * jp_total, lanes], total)
            totals.append(total)
        total = jnp.concatenate(totals, axis=0)
        largest = jnp.max(jnp.abs(total), axis=0, keepdims=True)
        power = jnp.ceil(jnp.log2(jnp.maximum(largest, 1e-30)))
        code_ref[pl.ds(fb, 1), :] = power
        fixed = jnp.round(total * (jnp.exp2(-power) * FIXED)).astype(jnp.int32)
        w_ref[src, b * col_total : (b + 1) * col_total, :] = fixed.astype(jnp.int16)
        r = tn(z, v_block(fb))
        sums = []
        for q in range(2):
            total = None
            for jj in range(jj_total):
                begin = (q * jj_total + jj) * irec
                part = r[begin : begin + irec, jj * LANES : (jj + 1) * LANES]
                total = part if total is None else total + part
            sums.append(total)
        crossed = jnp.where(
            first_part, -pltpu.roll(sums[1], LANES - S, 1), pltpu.roll(sums[1], S, 1)
        )
        quarter, off = lanes_of(fb, quarter_blocks)
        lanes = pl.ds(off, LANES)
        total = sums[0] + crossed
        r_ref[quarter, :, lanes] = total

    def w_copy(src):
        return pltpu.make_async_copy(w_ref.at[src], w_to.at[src], w_sems.at[src])

    def from_owner(src, _):
        for b in range(own_blocks):
            backward(src, b)
        codes = code_ref[pl.ds(src * own_blocks, own_blocks), :]
        codes = jnp.concatenate(
            [codes, jnp.zeros((CODES - own_blocks, LANES), jnp.float32)], axis=0
        )
        w_ref[src, own_blocks * col_total :, :] = codes.astype(jnp.int32).astype(jnp.int16)
        w_copy(src).start()
        return 0

    lax.fori_loop(0, src_total, from_owner, 0, unroll=4)
    outs = [
        pltpu.make_async_copy(r_ref.at[quarter_me ^ k], ref, sems.at[k])
        for k, ref in enumerate(r_to)
    ]
    for copy in outs:
        copy.start()
    for copy in outs:
        copy.wait()
    for src in range(src_total):
        w_copy(src).wait()


def join_kernel(count_ref, got_ref, out_ref):
    src_total, rows_total, _ = got_ref.shape
    k_own, col_total = out_ref.shape
    own_blocks = k_own // LANES
    cols = (rows_total - CODES) // own_blocks
    members = col_total // cols
    seg_ids = lax.broadcasted_iota(jnp.int32, (LANES, col_total), 0) % S
    inside = seg_ids < count_ref[...]
    scales = []
    for src in range(src_total):
        codes = got_ref[src, own_blocks * cols :, :].astype(jnp.int32).astype(jnp.float32)
        scales.append(jnp.exp2(codes) * (1.0 / FIXED))
    for b in range(own_blocks):
        rows = []
        for m in range(members):
            total = None
            for src in range(m, src_total, members):
                part = got_ref[src, b * cols : (b + 1) * cols, :]
                part = part.astype(jnp.int32).astype(jnp.float32) * scales[src][b : b + 1]
                total = part if total is None else total + part
            rows.append(total)
        whole = jnp.concatenate(rows, axis=0).T
        out_ref[b * LANES : (b + 1) * LANES, :] = jnp.where(inside, whole, 0.0)


def swap(x, axis, total, k):
    return lax.ppermute(x, axis, [(r, r ^ k) for r in range(total)])


def shards(
    receiver_spectra,
    reference_spectra,
    receiver_counts,
    reference_counts,
    column_station,
    lag_window,
    observed,
    *,
    rcv_total,
    ref_total,
):
    row_total, k_quarter = receiver_spectra.shape
    k_own, col_total = reference_spectra.shape
    k_total = k_own * rcv_total
    lag_total = observed.shape[2]
    half = lag_total // 2
    members = math.gcd(GROUP, rcv_total)
    irec = row_total * members
    cols = col_total // members
    jj_total = LANES // (2 * irec)
    jp_total = cols // jj_total
    extra = k_quarter // half + 1
    bf16 = jnp.bfloat16
    place = lax.axis_index("rcv")
    mine = place % members
    quarter = lax.axis_index("ref")
    vmem = pl.BlockSpec(memory_space=pltpu.VMEM)
    smem = pl.BlockSpec(memory_space=pltpu.SMEM)
    hbm = pl.BlockSpec(memory_space=pl.ANY)
    scalars = jnp.stack([mine, quarter * col_total, place, quarter]).astype(jnp.int32)
    def params(mib):
        return pltpu.CompilerParams(vmem_limit_bytes=mib * 1024 * 1024)

    free = pl.CostEstimate(flops=0, bytes_accessed=0, transcendentals=0)

    sent = pl.pallas_call(
        turn_kernel,
        out_shape=jax.ShapeDtypeStruct((rcv_total, cols, k_own), bf16),
        in_specs=[hbm] * 2,
        out_specs=hbm,
        scratch_shapes=[
            pltpu.VMEM((k_own, col_total), bf16),
            pltpu.VMEM((1, col_total), jnp.int32),
            pltpu.VMEM((col_total, k_own), bf16),
            pltpu.SemaphoreType.DMA((max(rcv_total, 1 + k_own // min(k_own, 2 * LANES)),)),
        ],
        compiler_params=params(62),
        cost_estimate=free,
    )(reference_spectra, reference_counts.reshape(1, col_total))
    v_all = lax.all_to_all(sent, "rcv", split_axis=0, concat_axis=0, tiled=True)

    _, observed = lax.optimization_barrier((sent, observed))
    shape = (cols, row_total, half)
    u_own, *folded = pl.pallas_call(
        fold_kernel,
        out_shape=[jax.ShapeDtypeStruct((extra, row_total, half), bf16)]
        + [jax.ShapeDtypeStruct(shape, bf16)] * members,
        in_specs=[smem] * 2 + [hbm] * 4,
        out_specs=[hbm] * (1 + members),
        scratch_shapes=[
            pltpu.VMEM(observed.shape, bf16),
            pltpu.VMEM(receiver_spectra.shape, bf16),
            pltpu.VMEM(lag_window.shape, jnp.int32),
            pltpu.VMEM((1, col_total), jnp.int32),
            pltpu.VMEM((half // LANES * col_total * row_total, LANES), jnp.float32),
            pltpu.VMEM((members,) + shape, bf16),
            pltpu.VMEM((extra, row_total, half), bf16),
            pltpu.SemaphoreType.DMA((row_total + 3,)),
            pltpu.SemaphoreType.DMA((members + 1,)),
        ],
        compiler_params=params(32),
        cost_estimate=free,
    )(
        scalars,
        receiver_counts,
        observed,
        receiver_spectra,
        lag_window,
        column_station.reshape(1, col_total),
    )
    e_all = [folded[0]] + [swap(folded[k], "rcv", rcv_total, k) for k in range(1, members)]

    near = pl.pallas_call(
        near_kernel,
        out_shape=jax.ShapeDtypeStruct((members, extra, row_total, half), bf16),
        in_specs=[hbm] * members,
        out_specs=hbm,
        scratch_shapes=[pltpu.SemaphoreType.DMA((members,))],
        compiler_params=params(16),
        cost_estimate=free,
    )(u_own, *[swap(u_own, "rcv", rcv_total, k) for k in range(1, members)])
    u_all = [near] + [swap(near, "ref", ref_total, k) for k in range(1, ref_total)]

    group_counts = near[:, extra - 1, :, 0].reshape(irec).astype(jnp.float32)
    own_counts = lax.dynamic_slice_in_dim(reference_counts, mine * cols, cols).astype(jnp.float32)
    counts = own_counts.reshape(jj_total, jp_total).T
    least = jnp.minimum(counts[:, :, None], group_counts[None, None, :])
    inverse = (1.0 / least).reshape(jp_total, jj_total * irec)
    inverse = jnp.concatenate([inverse, inverse], axis=1)

    table = lag_tables(k_total // (2 * S), lag_total)
    w_rows = k_own // LANES * cols + CODES
    lines = jp_total * (k_total // (2 * S) + PAD)
    w_part, *r_all = pl.pallas_call(
        functools.partial(pair_kernel, members, ref_total),
        out_shape=[jax.ShapeDtypeStruct((rcv_total, w_rows, LANES), jnp.int16)]
        + [jax.ShapeDtypeStruct((irec, k_quarter), jnp.float32)] * ref_total,
        in_specs=[smem] + [vmem] * 2 + [hbm] * (1 + members + ref_total),
        out_specs=[hbm] * (1 + ref_total),
        scratch_shapes=[
            pltpu.VMEM((lines, LANES), jnp.float32),
            pltpu.VMEM((lines, LANES), jnp.float32),
            pltpu.VMEM((irec, k_total), bf16),
            pltpu.VMEM((irec, k_total), bf16),
            pltpu.VMEM((k_total // LANES, LANES), jnp.float32),
            pltpu.VMEM((ref_total,) + near.shape, bf16),
            pltpu.VMEM((rcv_total, cols, k_own), bf16),
            pltpu.VMEM((members, cols, row_total, half), bf16),
            pltpu.VMEM((ref_total, irec, k_quarter), jnp.float32),
            pltpu.VMEM((rcv_total, w_rows, LANES), jnp.int16),
            pltpu.SemaphoreType.DMA((1 + members + ref_total,)),
            pltpu.SemaphoreType.DMA((rcv_total,)),
        ],
        compiler_params=params(32),
        cost_estimate=free,
    )(scalars, inverse, table, v_all, *e_all, *u_all)

    got = lax.all_to_all(w_part, "rcv", split_axis=0, concat_axis=0, tiled=True)
    reference_grad = pl.pallas_call(
        join_kernel,
        out_shape=jax.ShapeDtypeStruct((k_own, col_total), jnp.float32),
        in_specs=[vmem] * 2,
        out_specs=vmem,
        compiler_params=params(32),
        cost_estimate=free,
    )(reference_counts.reshape(1, col_total), got)

    r_sum = r_all[0]
    for k in range(1, ref_total):
        r_sum = r_sum + swap(r_all[k], "ref", ref_total, k)
    parts = [r_sum[k * row_total : (k + 1) * row_total] for k in range(members)]
    r_sum = parts[0]
    for k in range(1, members):
        r_sum = r_sum + swap(parts[k], "rcv", rcv_total, k)
    seg_quarter = jnp.arange(k_quarter, dtype=jnp.int32) % S
    receiver_grad = jnp.where(seg_quarter[None, :] < receiver_counts[:, None], r_sum, 0.0)
    return (receiver_grad, reference_grad)


def solution(mesh):
    return jax.shard_map(
        functools.partial(shards, rcv_total=mesh.shape["rcv"], ref_total=mesh.shape["ref"]),
        mesh=mesh,
        in_specs=(
            P("rcv", "ref"),
            P("rcv", "ref"),
            P("rcv"),
            P("ref"),
            P("ref"),
            P(None, "rcv", "ref"),
            P("rcv", "ref", None),
        ),
        out_specs=(P("rcv", "ref"), P("rcv", "ref")),
        check_vma=False,
    )
```

```python
import functools
import math

import jax
import jax.numpy as jnp
import numpy as np
from jax import lax
from jax.experimental import pallas as pl
from jax.experimental.pallas import tpu as pltpu
from jax.sharding import PartitionSpec as P

L = 512
S = 16
F = 256

env_floor = 0.05
misfit_scale = 0.03125
GROUP = 4
LANES = 128
FB = LANES // (2 * S)
WIDTH = 16
FIXED = 32000.0
PAD = 8
CODES = 16


def lag_tables(freq_total, lag_total):
    half = lag_total // 2
    freq_ids = np.arange(freq_total)[:, None]
    phase = 2.0 * np.pi * (freq_ids * np.arange(half)[None, :] % lag_total) / lag_total
    cosine = np.cos(phase) / math.sqrt(freq_total)
    sine = np.sin(phase) / math.sqrt(freq_total)
    back = [np.concatenate([cosine[p::2], sine[p::2]], axis=1) for p in (0, 1)]
    ahead = [np.concatenate([cosine[p::2].T, sine[p::2].T], axis=1) for p in (0, 1)]
    back = [np.concatenate([t[:, :half], t[:, half:]], axis=0) for t in back]
    whole = np.concatenate(ahead + back, axis=0)
    return jnp.asarray(whole.astype(np.float32)).astype(jnp.bfloat16)


def nt(a, b):
    return lax.dot_general(a, b, (((1,), (1,)), ((), ())), preferred_element_type=jnp.float32)


def nn(a, b):
    return jnp.dot(a, b, preferred_element_type=jnp.float32)


def tn(a, b):
    return lax.dot_general(a, b, (((0,), (0,)), ((), ())), preferred_element_type=jnp.float32)


def eye_of(size):
    rows = lax.broadcasted_iota(jnp.int32, (size, size), 0)
    lanes = lax.broadcasted_iota(jnp.int32, (size, size), 1)
    return jnp.where(rows == lanes, 1.0, 0.0).astype(jnp.bfloat16)


def turn_kernel(spectra_from, counts_from, v_to, spectra_ref, counts_ref, turned_ref, sems):
    k_own, col_total = spectra_ref.shape
    rcv_total, cols, _ = v_to.shape
    members = col_total // cols
    width = min(k_own, 2 * LANES)
    copies = [pltpu.make_async_copy(counts_from, counts_ref, sems.at[0])]
    for n, begin in enumerate(range(0, k_own, width)):
        rows = pl.ds(begin, width)
        copies.append(
            pltpu.make_async_copy(spectra_from.at[rows], spectra_ref.at[rows], sems.at[1 + n])
        )
    for copy in copies:
        copy.start()
    eye = eye_of(col_total)
    seg_ids = lax.broadcasted_iota(jnp.int32, (width, col_total), 0) % S
    copies[0].wait()
    inside = seg_ids < counts_ref[...]
    for n, begin in enumerate(range(0, k_own, width)):
        copies[1 + n].wait()
        part = spectra_ref[begin : begin + width, :].astype(jnp.float32)
        part = jnp.where(inside, part, 0.0).astype(jnp.bfloat16)
        turned_ref[:, begin : begin + width] = nt(eye, part).astype(jnp.bfloat16)
    copies = [
        pltpu.make_async_copy(
            turned_ref.at[pl.ds(dest % members * cols, cols)], v_to.at[dest], sems.at[dest]
        )
        for dest in range(rcv_total)
    ]
    for copy in copies:
        copy.start()
    for copy in copies:
        copy.wait()


def fold_kernel(c_ref, rcounts_ref, observed_from, rspectra_from, window_from, order_from, *rest):
    u_to, *out_to = rest[:-9]
    (
        observed_ref, rspectra_ref, window_ref, order_ref, line_ref, out_ref, u_ref, sems, out_sems,
    ) = rest[-9:]
    row_total, col_total, lag_total = observed_ref.shape
    half = lag_total // 2
    members = len(out_to)
    cols = col_total // members
    lines = col_total * row_total
    quarter = rspectra_ref.shape[1]
    copies = [
        pltpu.make_async_copy(src, dst, sems.at[row_total + n])
        for n, (src, dst) in enumerate(
            [(window_from, window_ref), (order_from, order_ref), (rspectra_from, rspectra_ref)]
        )
    ] + [
        pltpu.make_async_copy(observed_from.at[i], observed_ref.at[i], sems.at[i])
        for i in range(row_total)
    ]
    for copy in copies:
        copy.start()
    for copy in copies[:3]:
        copy.wait()
    row_ids = lax.broadcasted_iota(jnp.int32, (row_total, half), 0)
    counts = jnp.zeros((row_total, half), jnp.int32)
    for i in range(row_total):
        counts = jnp.where(row_ids == i, rcounts_ref[i], counts)
    seg_ids = lax.broadcasted_iota(jnp.int32, (row_total, half), 1) % S
    pieces = quarter // half
    for n in range(pieces):
        part = rspectra_ref[:, n * half : (n + 1) * half].astype(jnp.float32)
        u_ref[n] = jnp.where(seg_ids < counts, part, 0.0).astype(jnp.bfloat16)
    u_ref[pieces] = counts.astype(jnp.float32).astype(jnp.bfloat16)
    u_copy = pltpu.make_async_copy(u_ref, u_to, out_sems.at[members])
    u_copy.start()
    window = jnp.concatenate([window_ref[0], window_ref[1]], axis=0).astype(jnp.float32).T
    station = lax.broadcasted_iota(jnp.int32, (col_total, col_total), 0) + c_ref[1]
    pick = jnp.where(station == order_ref[...], 1.0, 0.0).astype(jnp.bfloat16)
    lag_ids = lax.broadcasted_iota(jnp.int32, (col_total, half), 1).astype(jnp.float32)
    for i in range(row_total):
        copies[3 + i].wait()
        begin = window[:, i : i + 1]
        end = begin + window[:, row_total + i : row_total + i + 1]
        values = observed_ref[i].astype(jnp.float32)
        low = (lag_ids >= begin) & (lag_ids < end)
        high = (lag_ids + half >= begin) & (lag_ids + half < end)
        folded = jnp.where(low, values[:, :half], jnp.where(high, -values[:, half:], 0.0))
        moved = nn(pick, folded.astype(jnp.bfloat16))
        for h in range(half // LANES):
            line_ref[pl.ds(h * lines + i, col_total, stride=row_total), :] = moved[
                :, h * LANES : (h + 1) * LANES
            ]
    mine = c_ref[0]
    copies = []
    for k in range(members):
        first = (mine ^ k) * (cols * row_total)
        for h in range(half // LANES):
            begin = pl.multiple_of(h * lines + first, cols * row_total)
            rows = line_ref[pl.ds(begin, cols * row_total), :]
            out_ref[k, :, :, h * LANES : (h + 1) * LANES] = rows.reshape(
                cols, row_total, LANES
            ).astype(jnp.bfloat16)
        copies.append(pltpu.make_async_copy(out_ref.at[k], out_to[k], out_sems.at[k]))
        copies[-1].start()
    for copy in copies + [u_copy]:
        copy.wait()


def near_kernel(*refs):
    *parts, out_ref, sems = refs
    copies = [
        pltpu.make_async_copy(ref, out_ref.at[k], sems.at[k]) for k, ref in enumerate(parts)
    ]
    for copy in copies:
        copy.start()
    for copy in copies:
        copy.wait()


def pair_kernel(n_e, n_r, c_ref, invn_ref, v_from, table_from, *refs):
    refs = list(refs)
    e_from, u_from = refs[:n_e], refs[n_e : n_e + n_r]
    w_to, *r_to = refs[n_e + n_r : n_e + 2 * n_r + 1]
    (
        x_ref, z_ref, plain_ref, turned_ref, code_ref, u_ref, v_ref, e_ref, r_ref, w_ref,
        table_ref, sems, w_sems,
    ) = refs[n_e + 2 * n_r + 1 :]

    src_total, col_total, k_own = v_ref.shape
    ref_total, irec, k_quarter = r_ref.shape
    jj_total = LANES // (2 * irec)
    jp_total = col_total // jj_total
    k_total = src_total * k_own
    half_f = k_total // (4 * S)
    freq_total = 2 * half_f
    pitch = freq_total + PAD
    blocks = k_total // LANES
    own_blocks = k_own // LANES
    quarter_blocks = k_quarter // LANES

    quarter_me = c_ref[3]
    early = [pltpu.make_async_copy(v_from, v_ref, sems.at[0])]
    for k, ref in enumerate(u_from):
        early.append(pltpu.make_async_copy(ref, u_ref.at[quarter_me ^ k], sems.at[1 + k]))
    late = [
        pltpu.make_async_copy(ref, e_ref.at[k], sems.at[1 + n_r + k])
        for k, ref in enumerate(e_from)
    ]
    late.append(pltpu.make_async_copy(table_from, table_ref, sems.at[1 + n_r + n_e]))
    for copy in early + late:
        copy.start()
    half = e_ref.shape[-1]
    eye = eye_of(half)
    group_ids = lax.broadcasted_iota(jnp.int32, (jp_total, LANES), 1) // (2 * S)
    first_part = lax.broadcasted_iota(jnp.int32, (irec, LANES), 1) % (2 * S) < S

    def lanes_of(fb, per):
        return fb // per, pl.multiple_of(fb % per * LANES, LANES)

    def v_block(fb):
        src, off = lanes_of(fb, own_blocks)
        parts = [
            v_ref[src, jj * jp_total : (jj + 1) * jp_total, pl.ds(off, LANES)]
            for jj in range(jj_total)
        ]
        zero = jnp.zeros((jp_total, LANES), jnp.bfloat16)
        rows = [
            jnp.concatenate([jnp.where(group_ids == f, part, zero) for part in parts], axis=1)
            for f in range(FB)
        ]
        return jnp.concatenate(rows, axis=0)

    def u_block(parts):
        zero = jnp.zeros((irec, LANES), jnp.bfloat16)
        return jnp.concatenate(
            [
                jnp.concatenate([part if k == jj else zero for k in range(jj_total)], axis=1)
                for part in parts
                for jj in range(jj_total)
            ],
            axis=0,
        )

    def place(fb, f):
        return pl.ds((f % 2) * half_f + fb * (FB // 2) + f // 2, jp_total, stride=pitch)

    def forward(fb, _):
        lanes = pl.ds(pl.multiple_of(fb * LANES, LANES), LANES)
        quarter, off = lanes_of(fb, quarter_blocks)
        piece, off = off // half, pl.multiple_of(off % half, LANES)
        wide = u_ref[quarter, :, piece, :, pl.ds(off, LANES)].astype(jnp.float32)
        wide = wide.reshape(irec, LANES)
        part = wide.astype(jnp.bfloat16)
        plain_ref[:, lanes] = part
        crossed = jnp.where(first_part, pltpu.roll(wide, LANES - S, 1), -pltpu.roll(wide, S, 1))
        crossed = crossed.astype(jnp.bfloat16)
        turned_ref[:, lanes] = crossed
        out = nt(v_block(fb), u_block([part, crossed]))
        scale = invn_ref[...]
        for f in range(FB):
            x_ref[place(fb, f), :] = out[f * jp_total : (f + 1) * jp_total] * scale
        return 0

    for copy in early:
        copy.wait()
    lax.fori_loop(0, blocks, forward, 0, unroll=64)

    lane_ids = lax.broadcasted_iota(jnp.int32, (1, LANES), 1)
    sign = jnp.where(lane_ids < LANES // 2, -1.0, 1.0).astype(jnp.float32)

    sign = sign.astype(jnp.bfloat16)

    def pairs(step, _):
        cols = [step * WIDTH + k for k in range(WIDTH)]
        rhs_e, rhs_o, obs = [], [], []
        for jp in cols:
            x = x_ref[pl.ds(pl.multiple_of(jp * pitch, PAD), freq_total), :]
            plain = x.astype(jnp.bfloat16)
            turned = pltpu.roll(x, LANES // 2, 1).astype(jnp.bfloat16) * sign
            rhs_e.append(jnp.concatenate([plain[:half_f], turned[:half_f]], axis=0))
            rhs_o.append(jnp.concatenate([plain[half_f:], turned[half_f:]], axis=0))
            rows = [
                e_ref[:, jj * jp_total + jp].astype(jnp.float32).reshape(irec, half)
                for jj in range(jj_total)
            ]
            rows = jnp.concatenate(rows, axis=0).astype(jnp.bfloat16)
            obs += [rows, rows]
        even = nn(table_y[0], jnp.concatenate(rhs_e, axis=1))
        odd = nn(table_y[1], jnp.concatenate(rhs_o, axis=1))
        seen = nt(eye, jnp.concatenate(obs, axis=0))
        g_e, g_o = [], []
        for k in range(WIDTH):
            lanes = slice(k * LANES, (k + 1) * LANES)
            e, d0, d1 = seen[:, lanes], even[:, lanes], odd[:, lanes]
            d = jnp.where(e < 0.0, d0 + d1, d0 - d1)
            power = d * d
            power = power + (pltpu.roll(power, LANES // 2, 1) + env_floor)
            g = d * (1.0 - jnp.abs(e) * lax.rsqrt(power))
            side = jnp.where(e < 0.0, 1.0, jnp.where(e > 0.0, -1.0, 0.0)).astype(jnp.bfloat16)
            turned = pltpu.roll(g, LANES // 2, 1).astype(jnp.bfloat16)
            g_side = g.astype(jnp.bfloat16) * side
            t_side = turned * (side * -sign)
            g_e.append(jnp.concatenate([g_side * side, t_side * side], axis=0))
            g_o.append(jnp.concatenate([g_side, t_side], axis=0))
        z_e = nn(table_z[0], jnp.concatenate(g_e, axis=1))
        z_o = nn(table_z[1], jnp.concatenate(g_o, axis=1))
        for k, jp in enumerate(cols):
            lanes = slice(k * LANES, (k + 1) * LANES)
            scale = invn_ref[pl.ds(jp, 1), :] * misfit_scale
            base = pl.multiple_of(jp * pitch, PAD)
            z_ref[pl.ds(base, half_f), :] = z_e[:, lanes] * scale
            z_ref[pl.ds(base + half_f, half_f), :] = z_o[:, lanes] * scale
        return 0

    for copy in late:
        copy.wait()
    table_y = [table_ref[p * half : (p + 1) * half, :] for p in range(2)]
    table_z = []
    for p in range(2):
        begin = 2 * half + p * 2 * half_f
        parts = [table_ref[begin + n * half_f : begin + (n + 1) * half_f, :] for n in range(2)]
        table_z.append(jnp.concatenate(parts, axis=1))
    lax.fori_loop(0, jp_total // WIDTH, pairs, 0, unroll=2)

    def backward(src, b):
        fb = src * own_blocks + b
        z = jnp.concatenate([z_ref[place(fb, f), :] for f in range(FB)], axis=0)
        z = z.astype(jnp.bfloat16)
        lanes = pl.ds(pl.multiple_of(fb * LANES, LANES), LANES)
        w = nn(z, u_block([plain_ref[:, lanes], turned_ref[:, lanes]]))
        totals = []
        for jj in range(jj_total):
            lanes = slice(jj * LANES, (jj + 1) * LANES)
            total = w[:jp_total, lanes]
            for f in range(1, FB):
                total = jnp.where(group_ids == f, w[f * jp_total : (f + 1) * jp_total, lanes], total)
            totals.append(total)
        total = jnp.concatenate(totals, axis=0)
        largest = jnp.max(jnp.abs(total), axis=0, keepdims=True)
        power = jnp.ceil(jnp.log2(jnp.maximum(largest, 1e-30)))
        code_ref[pl.ds(fb, 1), :] = power
        fixed = jnp.round(total * (jnp.exp2(-power) * FIXED)).astype(jnp.int32)
        w_ref[src, b * col_total : (b + 1) * col_total, :] = fixed.astype(jnp.int16)
        r = tn(z, v_block(fb))
        sums = []
        for q in range(2):
            total = None
            for jj in range(jj_total):
                begin = (q * jj_total + jj) * irec
                part = r[begin : begin + irec, jj * LANES : (jj + 1) * LANES]
                total = part if total is None else total + part
            sums.append(total)
        crossed = jnp.where(
            first_part, -pltpu.roll(sums[1], LANES - S, 1), pltpu.roll(sums[1], S, 1)
        )
        quarter, off = lanes_of(fb, quarter_blocks)
        lanes = pl.ds(off, LANES)
        total = sums[0] + crossed
        r_ref[quarter, :, lanes] = total

    def w_copy(src):
        return pltpu.make_async_copy(w_ref.at[src], w_to.at[src], w_sems.at[src])

    def from_owner(src, _):
        for b in range(own_blocks):
            backward(src, b)
        codes = code_ref[pl.ds(src * own_blocks, own_blocks), :]
        codes = jnp.concatenate(
            [codes, jnp.zeros((CODES - own_blocks, LANES), jnp.float32)], axis=0
        )
        w_ref[src, own_blocks * col_total :, :] = codes.astype(jnp.int32).astype(jnp.int16)
        w_copy(src).start()
        return 0

    lax.fori_loop(0, src_total, from_owner, 0, unroll=4)
    outs = [
        pltpu.make_async_copy(r_ref.at[quarter_me ^ k], ref, sems.at[k])
        for k, ref in enumerate(r_to)
    ]
    for copy in outs:
        copy.start()
    for copy in outs:
        copy.wait()
    for src in range(src_total):
        w_copy(src).wait()


def join_kernel(count_ref, got_ref, out_to, out_ref, sems):
    src_total, rows_total, _ = got_ref.shape
    k_own, col_total = out_ref.shape
    own_blocks = k_own // LANES
    cols = (rows_total - CODES) // own_blocks
    members = col_total // cols
    seg_ids = lax.broadcasted_iota(jnp.int32, (LANES, col_total), 0) % S
    inside = seg_ids < count_ref[...]
    scales = []
    for src in range(src_total):
        codes = got_ref[src, own_blocks * cols :, :].astype(jnp.int32).astype(jnp.float32)
        scales.append(jnp.exp2(codes) * (1.0 / FIXED))
    copies = []
    for b in range(own_blocks):
        rows = []
        for m in range(members):
            total = None
            for src in range(m, src_total, members):
                part = got_ref[src, b * cols : (b + 1) * cols, :]
                part = part.astype(jnp.int32).astype(jnp.float32) * scales[src][b : b + 1]
                total = part if total is None else total + part
            rows.append(total)
        whole = jnp.concatenate(rows, axis=0).T
        rows = pl.ds(b * LANES, LANES)
        out_ref[rows, :] = jnp.where(inside, whole, 0.0)
        copies.append(pltpu.make_async_copy(out_ref.at[rows], out_to.at[rows], sems.at[b]))
        copies[-1].start()
    for copy in copies:
        copy.wait()


def swap(x, axis, total, k):
    return lax.ppermute(x, axis, [(r, r ^ k) for r in range(total)])


def shards(
    receiver_spectra,
    reference_spectra,
    receiver_counts,
    reference_counts,
    column_station,
    lag_window,
    observed,
    *,
    rcv_total,
    ref_total,
):
    row_total, k_quarter = receiver_spectra.shape
    k_own, col_total = reference_spectra.shape
    k_total = k_own * rcv_total
    lag_total = observed.shape[2]
    half = lag_total // 2
    members = math.gcd(GROUP, rcv_total)
    irec = row_total * members
    cols = col_total // members
    jj_total = LANES // (2 * irec)
    jp_total = cols // jj_total
    extra = k_quarter // half + 1
    bf16 = jnp.bfloat16
    place = lax.axis_index("rcv")
    mine = place % members
    quarter = lax.axis_index("ref")
    vmem = pl.BlockSpec(memory_space=pltpu.VMEM)
    smem = pl.BlockSpec(memory_space=pltpu.SMEM)
    hbm = pl.BlockSpec(memory_space=pl.ANY)
    scalars = jnp.stack([mine, quarter * col_total, place, quarter]).astype(jnp.int32)
    def params(mib):
        return pltpu.CompilerParams(vmem_limit_bytes=mib * 1024 * 1024)

    free = pl.CostEstimate(flops=0, bytes_accessed=0, transcendentals=0)

    sent = pl.pallas_call(
        turn_kernel,
        out_shape=jax.ShapeDtypeStruct((rcv_total, cols, k_own), bf16),
        in_specs=[hbm] * 2,
        out_specs=hbm,
        scratch_shapes=[
            pltpu.VMEM((k_own, col_total), bf16),
            pltpu.VMEM((1, col_total), jnp.int32),
            pltpu.VMEM((col_total, k_own), bf16),
            pltpu.SemaphoreType.DMA((max(rcv_total, 1 + k_own // min(k_own, 2 * LANES)),)),
        ],
        compiler_params=params(62),
        cost_estimate=free,
    )(reference_spectra, reference_counts.reshape(1, col_total))
    v_all = lax.all_to_all(sent, "rcv", split_axis=0, concat_axis=0, tiled=True)

    _, observed = lax.optimization_barrier((sent, observed))
    shape = (cols, row_total, half)
    u_own, *folded = pl.pallas_call(
        fold_kernel,
        out_shape=[jax.ShapeDtypeStruct((extra, row_total, half), bf16)]
        + [jax.ShapeDtypeStruct(shape, bf16)] * members,
        in_specs=[smem] * 2 + [hbm] * 4,
        out_specs=[hbm] * (1 + members),
        scratch_shapes=[
            pltpu.VMEM(observed.shape, bf16),
            pltpu.VMEM(receiver_spectra.shape, bf16),
            pltpu.VMEM(lag_window.shape, jnp.int32),
            pltpu.VMEM((1, col_total), jnp.int32),
            pltpu.VMEM((half // LANES * col_total * row_total, LANES), jnp.float32),
            pltpu.VMEM((members,) + shape, bf16),
            pltpu.VMEM((extra, row_total, half), bf16),
            pltpu.SemaphoreType.DMA((row_total + 3,)),
            pltpu.SemaphoreType.DMA((members + 1,)),
        ],
        compiler_params=params(32),
        cost_estimate=free,
    )(
        scalars,
        receiver_counts,
        observed,
        receiver_spectra,
        lag_window,
        column_station.reshape(1, col_total),
    )
    e_all = [folded[0]] + [swap(folded[k], "rcv", rcv_total, k) for k in range(1, members)]

    near = pl.pallas_call(
        near_kernel,
        out_shape=jax.ShapeDtypeStruct((members, extra, row_total, half), bf16),
        in_specs=[hbm] * members,
        out_specs=hbm,
        scratch_shapes=[pltpu.SemaphoreType.DMA((members,))],
        compiler_params=params(16),
        cost_estimate=free,
    )(u_own, *[swap(u_own, "rcv", rcv_total, k) for k in range(1, members)])
    u_all = [near] + [swap(near, "ref", ref_total, k) for k in range(1, ref_total)]

    group_counts = near[:, extra - 1, :, 0].reshape(irec).astype(jnp.float32)
    own_counts = lax.dynamic_slice_in_dim(reference_counts, mine * cols, cols).astype(jnp.float32)
    counts = own_counts.reshape(jj_total, jp_total).T
    least = jnp.minimum(counts[:, :, None], group_counts[None, None, :])
    inverse = (1.0 / least).reshape(jp_total, jj_total * irec)
    inverse = jnp.concatenate([inverse, inverse], axis=1)

    table = lag_tables(k_total // (2 * S), lag_total)
    w_rows = k_own // LANES * cols + CODES
    lines = jp_total * (k_total // (2 * S) + PAD)
    w_part, *r_all = pl.pallas_call(
        functools.partial(pair_kernel, members, ref_total),
        out_shape=[jax.ShapeDtypeStruct((rcv_total, w_rows, LANES), jnp.int16)]
        + [jax.ShapeDtypeStruct((irec, k_quarter), jnp.float32)] * ref_total,
        in_specs=[smem, vmem] + [hbm] * (2 + members + ref_total),
        out_specs=[hbm] * (1 + ref_total),
        scratch_shapes=[
            pltpu.VMEM((lines, LANES), jnp.float32),
            pltpu.VMEM((lines, LANES), jnp.float32),
            pltpu.VMEM((irec, k_total), bf16),
            pltpu.VMEM((irec, k_total), bf16),
            pltpu.VMEM((k_total // LANES, LANES), jnp.float32),
            pltpu.VMEM((ref_total,) + near.shape, bf16),
            pltpu.VMEM((rcv_total, cols, k_own), bf16),
            pltpu.VMEM((members, cols, row_total, half), bf16),
            pltpu.VMEM((ref_total, irec, k_quarter), jnp.float32),
            pltpu.VMEM((rcv_total, w_rows, LANES), jnp.int16),
            pltpu.VMEM(table.shape, bf16),
            pltpu.SemaphoreType.DMA((2 + members + ref_total,)),
            pltpu.SemaphoreType.DMA((rcv_total,)),
        ],
        compiler_params=params(62),
        cost_estimate=free,
    )(scalars, inverse, v_all, table, *e_all, *u_all)

    got = lax.all_to_all(w_part, "rcv", split_axis=0, concat_axis=0, tiled=True)
    reference_grad = pl.pallas_call(
        join_kernel,
        out_shape=jax.ShapeDtypeStruct((k_own, col_total), jnp.float32),
        in_specs=[vmem] * 2,
        out_specs=hbm,
        scratch_shapes=[
            pltpu.VMEM((k_own, col_total), jnp.float32),
            pltpu.SemaphoreType.DMA((k_own // LANES,)),
        ],
        compiler_params=params(32),
        cost_estimate=free,
    )(reference_counts.reshape(1, col_total), got)

    r_sum = r_all[0]
    for k in range(1, ref_total):
        r_sum = r_sum + swap(r_all[k], "ref", ref_total, k)
    parts = [r_sum[k * row_total : (k + 1) * row_total] for k in range(members)]
    r_sum = parts[0]
    for k in range(1, members):
        r_sum = r_sum + swap(parts[k], "rcv", rcv_total, k)
    seg_quarter = jnp.arange(k_quarter, dtype=jnp.int32) % S
    receiver_grad = jnp.where(seg_quarter[None, :] < receiver_counts[:, None], r_sum, 0.0)
    return (receiver_grad, reference_grad)


def solution(mesh):
    return jax.shard_map(
        functools.partial(shards, rcv_total=mesh.shape["rcv"], ref_total=mesh.shape["ref"]),
        mesh=mesh,
        in_specs=(
            P("rcv", "ref"),
            P("rcv", "ref"),
            P("rcv"),
            P("ref"),
            P("ref"),
            P(None, "rcv", "ref"),
            P("rcv", "ref", None),
        ),
        out_specs=(P("rcv", "ref"), P("rcv", "ref")),
        check_vma=False,
    )
```

```python
import functools
import math

import jax
import jax.numpy as jnp
import numpy as np
from jax import lax
from jax.experimental import pallas as pl
from jax.experimental.pallas import tpu as pltpu
from jax.sharding import PartitionSpec as P

L = 512
S = 16
F = 256

env_floor = 0.05
misfit_scale = 0.03125
GROUP = 4
LANES = 128
FB = LANES // (2 * S)
WIDTH = 16
FIXED = 32000.0
PAD = 8
CODES = 16


def lag_tables(freq_total, lag_total):
    half = lag_total // 2
    freq_ids = np.arange(freq_total)[:, None]
    phase = 2.0 * np.pi * (freq_ids * np.arange(half)[None, :] % lag_total) / lag_total
    cosine = np.cos(phase) / math.sqrt(freq_total)
    sine = np.sin(phase) / math.sqrt(freq_total)
    back = [np.concatenate([cosine[p::2], sine[p::2]], axis=1) for p in (0, 1)]
    ahead = [np.concatenate([cosine[p::2].T, sine[p::2].T], axis=1) for p in (0, 1)]
    back = [np.concatenate([t[:, :half], t[:, half:]], axis=0) for t in back]
    whole = np.concatenate(ahead + back, axis=0)
    return jnp.asarray(whole.astype(np.float32)).astype(jnp.bfloat16)


def nt(a, b):
    return lax.dot_general(a, b, (((1,), (1,)), ((), ())), preferred_element_type=jnp.float32)


def nn(a, b):
    return jnp.dot(a, b, preferred_element_type=jnp.float32)


def tn(a, b):
    return lax.dot_general(a, b, (((0,), (0,)), ((), ())), preferred_element_type=jnp.float32)


def eye_of(size):
    rows = lax.broadcasted_iota(jnp.int32, (size, size), 0)
    lanes = lax.broadcasted_iota(jnp.int32, (size, size), 1)
    return jnp.where(rows == lanes, 1.0, 0.0).astype(jnp.bfloat16)


def turn_kernel(spectra_from, counts_from, v_to, spectra_ref, counts_ref, turned_ref, sems):
    k_own, col_total = spectra_ref.shape
    rcv_total, cols, _ = v_to.shape
    members = col_total // cols
    width = min(k_own, 2 * LANES)
    copies = [pltpu.make_async_copy(counts_from, counts_ref, sems.at[0])]
    for n, begin in enumerate(range(0, k_own, width)):
        rows = pl.ds(begin, width)
        copies.append(
            pltpu.make_async_copy(spectra_from.at[rows], spectra_ref.at[rows], sems.at[1 + n])
        )
    for copy in copies:
        copy.start()
    eye = eye_of(col_total)
    seg_ids = lax.broadcasted_iota(jnp.int32, (width, col_total), 0) % S
    copies[0].wait()
    inside = seg_ids < counts_ref[...]
    for n, begin in enumerate(range(0, k_own, width)):
        copies[1 + n].wait()
        part = spectra_ref[begin : begin + width, :].astype(jnp.float32)
        part = jnp.where(inside, part, 0.0).astype(jnp.bfloat16)
        turned_ref[:, begin : begin + width] = nt(eye, part).astype(jnp.bfloat16)
    copies = [
        pltpu.make_async_copy(
            turned_ref.at[pl.ds(dest % members * cols, cols)], v_to.at[dest], sems.at[dest]
        )
        for dest in range(rcv_total)
    ]
    for copy in copies:
        copy.start()
    for copy in copies:
        copy.wait()


def fold_kernel(c_ref, rcounts_ref, observed_from, rspectra_from, window_from, order_from, *rest):
    u_to, *out_to = rest[:-9]
    (
        observed_ref, rspectra_ref, window_ref, order_ref, line_ref, out_ref, u_ref, sems, out_sems,
    ) = rest[-9:]
    row_total, col_total, lag_total = observed_ref.shape
    half = lag_total // 2
    members = len(out_to)
    cols = col_total // members
    lines = col_total * row_total
    quarter = rspectra_ref.shape[1]
    copies = [
        pltpu.make_async_copy(src, dst, sems.at[row_total + n])
        for n, (src, dst) in enumerate(
            [(window_from, window_ref), (order_from, order_ref), (rspectra_from, rspectra_ref)]
        )
    ] + [
        pltpu.make_async_copy(observed_from.at[i], observed_ref.at[i], sems.at[i])
        for i in range(row_total)
    ]
    for copy in copies:
        copy.start()
    for copy in copies[:3]:
        copy.wait()
    row_ids = lax.broadcasted_iota(jnp.int32, (row_total, half), 0)
    counts = jnp.zeros((row_total, half), jnp.int32)
    for i in range(row_total):
        counts = jnp.where(row_ids == i, rcounts_ref[i], counts)
    seg_ids = lax.broadcasted_iota(jnp.int32, (row_total, half), 1) % S
    pieces = quarter // half
    for n in range(pieces):
        part = rspectra_ref[:, n * half : (n + 1) * half].astype(jnp.float32)
        u_ref[n] = jnp.where(seg_ids < counts, part, 0.0).astype(jnp.bfloat16)
    u_ref[pieces] = counts.astype(jnp.float32).astype(jnp.bfloat16)
    u_copy = pltpu.make_async_copy(u_ref, u_to, out_sems.at[members])
    u_copy.start()
    window = jnp.concatenate([window_ref[0], window_ref[1]], axis=0).astype(jnp.float32).T
    station = lax.broadcasted_iota(jnp.int32, (col_total, col_total), 0) + c_ref[1]
    pick = jnp.where(station == order_ref[...], 1.0, 0.0).astype(jnp.bfloat16)
    lag_ids = lax.broadcasted_iota(jnp.int32, (col_total, half), 1).astype(jnp.float32)
    for i in range(row_total):
        copies[3 + i].wait()
        begin = window[:, i : i + 1]
        end = begin + window[:, row_total + i : row_total + i + 1]
        values = observed_ref[i].astype(jnp.float32)
        low = (lag_ids >= begin) & (lag_ids < end)
        high = (lag_ids + half >= begin) & (lag_ids + half < end)
        folded = jnp.where(low, values[:, :half], jnp.where(high, -values[:, half:], 0.0))
        moved = nn(pick, folded.astype(jnp.bfloat16))
        for h in range(half // LANES):
            line_ref[pl.ds(h * lines + i, col_total, stride=row_total), :] = moved[
                :, h * LANES : (h + 1) * LANES
            ]
    mine = c_ref[0]
    copies = []
    for k in range(members):
        first = (mine ^ k) * (cols * row_total)
        for h in range(half // LANES):
            begin = pl.multiple_of(h * lines + first, cols * row_total)
            rows = line_ref[pl.ds(begin, cols * row_total), :]
            out_ref[k, :, :, h * LANES : (h + 1) * LANES] = rows.reshape(
                cols, row_total, LANES
            ).astype(jnp.bfloat16)
        copies.append(pltpu.make_async_copy(out_ref.at[k], out_to[k], out_sems.at[k]))
        copies[-1].start()
    for copy in copies + [u_copy]:
        copy.wait()


def near_kernel(*refs):
    *parts, out_ref, sems = refs
    copies = [
        pltpu.make_async_copy(ref, out_ref.at[k], sems.at[k]) for k, ref in enumerate(parts)
    ]
    for copy in copies:
        copy.start()
    for copy in copies:
        copy.wait()


def pair_kernel(n_e, n_r, c_ref, invn_ref, v_from, table_from, *refs):
    refs = list(refs)
    e_from, u_from = refs[:n_e], refs[n_e : n_e + n_r]
    w_to, z_to = refs[n_e + n_r : n_e + n_r + 2]
    (
        x_ref, z_ref, plain_ref, turned_ref, code_ref, u_ref, v_ref, e_ref, z_out_ref, w_ref,
        table_ref, sems, w_sems, z_sems,
    ) = refs[n_e + n_r + 2 :]

    src_total, col_total, k_own = v_ref.shape
    irec, k_quarter = plain_ref.shape[0], (u_ref.shape[2] - 1) * u_ref.shape[4]
    jj_total = LANES // (2 * irec)
    jp_total = col_total // jj_total
    k_total = src_total * k_own
    half_f = k_total // (4 * S)
    freq_total = 2 * half_f
    pitch = freq_total + PAD
    blocks = k_total // LANES
    own_blocks = k_own // LANES
    quarter_blocks = k_quarter // LANES

    quarter_me = c_ref[3]
    early = [pltpu.make_async_copy(v_from, v_ref, sems.at[0])]
    for k, ref in enumerate(u_from):
        early.append(pltpu.make_async_copy(ref, u_ref.at[quarter_me ^ k], sems.at[1 + k]))
    late = [
        pltpu.make_async_copy(ref, e_ref.at[k], sems.at[1 + n_r + k])
        for k, ref in enumerate(e_from)
    ]
    late.append(pltpu.make_async_copy(table_from, table_ref, sems.at[1 + n_r + n_e]))
    for copy in early + late:
        copy.start()
    half = e_ref.shape[-1]
    eye = eye_of(half)
    group_ids = lax.broadcasted_iota(jnp.int32, (jp_total, LANES), 1) // (2 * S)
    first_part = lax.broadcasted_iota(jnp.int32, (irec, LANES), 1) % (2 * S) < S

    def lanes_of(fb, per):
        return fb // per, pl.multiple_of(fb % per * LANES, LANES)

    def v_block(fb):
        src, off = lanes_of(fb, own_blocks)
        parts = [
            v_ref[src, jj * jp_total : (jj + 1) * jp_total, pl.ds(off, LANES)]
            for jj in range(jj_total)
        ]
        zero = jnp.zeros((jp_total, LANES), jnp.bfloat16)
        rows = [
            jnp.concatenate([jnp.where(group_ids == f, part, zero) for part in parts], axis=1)
            for f in range(FB)
        ]
        return jnp.concatenate(rows, axis=0)

    def u_block(parts):
        zero = jnp.zeros((irec, LANES), jnp.bfloat16)
        return jnp.concatenate(
            [
                jnp.concatenate([part if k == jj else zero for k in range(jj_total)], axis=1)
                for part in parts
                for jj in range(jj_total)
            ],
            axis=0,
        )

    def place(fb, f):
        return pl.ds((f % 2) * half_f + fb * (FB // 2) + f // 2, jp_total, stride=pitch)

    def forward(fb, _):
        lanes = pl.ds(pl.multiple_of(fb * LANES, LANES), LANES)
        quarter, off = lanes_of(fb, quarter_blocks)
        piece, off = off // half, pl.multiple_of(off % half, LANES)
        wide = u_ref[quarter, :, piece, :, pl.ds(off, LANES)].astype(jnp.float32)
        wide = wide.reshape(irec, LANES)
        part = wide.astype(jnp.bfloat16)
        plain_ref[:, lanes] = part
        crossed = jnp.where(first_part, pltpu.roll(wide, LANES - S, 1), -pltpu.roll(wide, S, 1))
        crossed = crossed.astype(jnp.bfloat16)
        turned_ref[:, lanes] = crossed
        out = nt(v_block(fb), u_block([part, crossed]))
        scale = invn_ref[...]
        for f in range(FB):
            x_ref[place(fb, f), :] = out[f * jp_total : (f + 1) * jp_total] * scale
        return 0

    for copy in early:
        copy.wait()
    lax.fori_loop(0, blocks, forward, 0, unroll=64)

    lane_ids = lax.broadcasted_iota(jnp.int32, (1, LANES), 1)
    sign = jnp.where(lane_ids < LANES // 2, -1.0, 1.0).astype(jnp.float32)

    sign = sign.astype(jnp.bfloat16)

    def pairs(step, _):
        cols = [step * WIDTH + k for k in range(WIDTH)]
        rhs_e, rhs_o, obs = [], [], []
        for jp in cols:
            x = x_ref[pl.ds(pl.multiple_of(jp * pitch, PAD), freq_total), :]
            plain = x.astype(jnp.bfloat16)
            turned = pltpu.roll(x, LANES // 2, 1).astype(jnp.bfloat16) * sign
            rhs_e.append(jnp.concatenate([plain[:half_f], turned[:half_f]], axis=0))
            rhs_o.append(jnp.concatenate([plain[half_f:], turned[half_f:]], axis=0))
            rows = [
                e_ref[:, jj * jp_total + jp].astype(jnp.float32).reshape(irec, half)
                for jj in range(jj_total)
            ]
            rows = jnp.concatenate(rows, axis=0).astype(jnp.bfloat16)
            obs += [rows, rows]
        even = nn(table_y[0], jnp.concatenate(rhs_e, axis=1))
        odd = nn(table_y[1], jnp.concatenate(rhs_o, axis=1))
        seen = nt(eye, jnp.concatenate(obs, axis=0))
        g_e, g_o = [], []
        for k in range(WIDTH):
            lanes = slice(k * LANES, (k + 1) * LANES)
            e, d0, d1 = seen[:, lanes], even[:, lanes], odd[:, lanes]
            d = jnp.where(e < 0.0, d0 + d1, d0 - d1)
            power = d * d
            power = power + (pltpu.roll(power, LANES // 2, 1) + env_floor)
            g = d * (1.0 - jnp.abs(e) * lax.rsqrt(power))
            side = jnp.where(e < 0.0, 1.0, jnp.where(e > 0.0, -1.0, 0.0)).astype(jnp.bfloat16)
            turned = pltpu.roll(g, LANES // 2, 1).astype(jnp.bfloat16)
            g_side = g.astype(jnp.bfloat16) * side
            t_side = turned * (side * -sign)
            g_e.append(jnp.concatenate([g_side * side, t_side * side], axis=0))
            g_o.append(jnp.concatenate([g_side, t_side], axis=0))
        z_e = nn(table_z[0], jnp.concatenate(g_e, axis=1))
        z_o = nn(table_z[1], jnp.concatenate(g_o, axis=1))
        for k, jp in enumerate(cols):
            lanes = slice(k * LANES, (k + 1) * LANES)
            scale = invn_ref[pl.ds(jp, 1), :] * misfit_scale
            base = pl.multiple_of(jp * pitch, PAD)
            z_ref[pl.ds(base, half_f), :] = z_e[:, lanes] * scale
            z_ref[pl.ds(base + half_f, half_f), :] = z_o[:, lanes] * scale
        return 0

    for copy in late:
        copy.wait()
    table_y = [table_ref[p * half : (p + 1) * half, :] for p in range(2)]
    table_z = []
    for p in range(2):
        begin = 2 * half + p * 2 * half_f
        parts = [table_ref[begin + n * half_f : begin + (n + 1) * half_f, :] for n in range(2)]
        table_z.append(jnp.concatenate(parts, axis=1))
    lax.fori_loop(0, jp_total // WIDTH, pairs, 0, unroll=2)

    def backward(src, b):
        fb = src * own_blocks + b
        z = jnp.concatenate([z_ref[place(fb, f), :] for f in range(FB)], axis=0)
        z = z.astype(jnp.bfloat16)
        lanes = pl.ds(pl.multiple_of(fb * LANES, LANES), LANES)
        w = nn(z, u_block([plain_ref[:, lanes], turned_ref[:, lanes]]))
        totals = []
        for jj in range(jj_total):
            lanes = slice(jj * LANES, (jj + 1) * LANES)
            total = w[:jp_total, lanes]
            for f in range(1, FB):
                total = jnp.where(group_ids == f, w[f * jp_total : (f + 1) * jp_total, lanes], total)
            totals.append(total)
        total = jnp.concatenate(totals, axis=0)
        largest = jnp.max(jnp.abs(total), axis=0, keepdims=True)
        power = jnp.ceil(jnp.log2(jnp.maximum(largest, 1e-30)))
        code_ref[pl.ds(fb, 1), :] = power
        fixed = jnp.round(total * (jnp.exp2(-power) * FIXED)).astype(jnp.int32)
        w_ref[src, b * col_total : (b + 1) * col_total, :] = fixed.astype(jnp.int16)
        z_out_ref[fb] = z

    def w_copy(src):
        return pltpu.make_async_copy(w_ref.at[src], w_to.at[src], w_sems.at[src])

    def z_copy(src):
        rows = pl.ds(src * own_blocks, own_blocks)
        return pltpu.make_async_copy(z_out_ref.at[rows], z_to.at[rows], z_sems.at[src])

    def from_owner(src, _):
        for b in range(own_blocks):
            backward(src, b)
        codes = code_ref[pl.ds(src * own_blocks, own_blocks), :]
        codes = jnp.concatenate(
            [codes, jnp.zeros((CODES - own_blocks, LANES), jnp.float32)], axis=0
        )
        w_ref[src, own_blocks * col_total :, :] = codes.astype(jnp.int32).astype(jnp.int16)
        w_copy(src).start()
        z_copy(src).start()
        return 0

    lax.fori_loop(0, src_total, from_owner, 0, unroll=4)
    for src in range(src_total):
        w_copy(src).wait()
        z_copy(src).wait()


def receiver_sum_kernel(c_ref, v_from, z_from, *refs):
    *r_to, v_ref, z_ref, r_ref, code_ref, sems = refs
    src_total, col_total, k_own = v_ref.shape
    ref_total = r_ref.shape[0]
    blocks = z_ref.shape[0]
    quarter_blocks = blocks // ref_total
    irec = (r_ref.shape[1] - CODES) // quarter_blocks
    jj_total = LANES // (2 * irec)
    jp_total = col_total // jj_total
    own_blocks = k_own // LANES
    copies = [
        pltpu.make_async_copy(v_from, v_ref, sems.at[0]),
        pltpu.make_async_copy(z_from, z_ref, sems.at[1]),
    ]
    for copy in copies:
        copy.start()
    group_ids = lax.broadcasted_iota(jnp.int32, (jp_total, LANES), 1) // (2 * S)
    first_part = lax.broadcasted_iota(jnp.int32, (irec, LANES), 1) % (2 * S) < S

    def lanes_of(fb, per):
        return fb // per, pl.multiple_of(fb % per * LANES, LANES)

    def v_block(fb):
        src, off = lanes_of(fb, own_blocks)
        parts = [
            v_ref[src, jj * jp_total : (jj + 1) * jp_total, pl.ds(off, LANES)]
            for jj in range(jj_total)
        ]
        zero = jnp.zeros((jp_total, LANES), jnp.bfloat16)
        rows = [
            jnp.concatenate([jnp.where(group_ids == f, part, zero) for part in parts], axis=1)
            for f in range(FB)
        ]
        return jnp.concatenate(rows, axis=0)

    def step(fb, _):
        z = z_ref[fb]
        r = tn(z, v_block(fb))
        sums = []
        for q in range(2):
            total = None
            for jj in range(jj_total):
                begin = (q * jj_total + jj) * irec
                part = r[begin : begin + irec, jj * LANES : (jj + 1) * LANES]
                total = part if total is None else total + part
            sums.append(total)
        crossed = jnp.where(
            first_part, -pltpu.roll(sums[1], LANES - S, 1), pltpu.roll(sums[1], S, 1)
        )
        total = sums[0] + crossed
        largest = jnp.max(jnp.abs(total), axis=0, keepdims=True)
        power = jnp.ceil(jnp.log2(jnp.maximum(largest, 1e-30)))
        code_ref[pl.ds(fb, 1), :] = power
        fixed = jnp.round(total * (jnp.exp2(-power) * FIXED)).astype(jnp.int32)
        rows = pl.ds(pl.multiple_of(fb % quarter_blocks * irec, irec), irec)
        r_ref[fb // quarter_blocks, rows, :] = fixed.astype(jnp.int16)
        return 0

    for copy in copies:
        copy.wait()
    lax.fori_loop(0, blocks, step, 0, unroll=32)
    for quarter in range(ref_total):
        codes = code_ref[quarter * quarter_blocks : (quarter + 1) * quarter_blocks, :]
        codes = jnp.concatenate(
            [codes, jnp.zeros((CODES - quarter_blocks, LANES), jnp.float32)], axis=0
        ) if quarter_blocks < CODES else codes
        r_ref[quarter, quarter_blocks * irec :, :] = codes.astype(jnp.int32).astype(jnp.int16)
    outs = [
        pltpu.make_async_copy(r_ref.at[c_ref[3] ^ k], ref, sems.at[2 + k])
        for k, ref in enumerate(r_to)
    ]
    for copy in outs:
        copy.start()
    for copy in outs:
        copy.wait()


def add_kernel(n_in, *refs):
    got_refs, out_refs = refs[:n_in], refs[n_in:]
    members = len(out_refs)
    rows, k_quarter = out_refs[0].shape
    blocks = k_quarter // LANES
    irec = rows * members
    scales = [
        jnp.exp2(ref[blocks * irec :, :].astype(jnp.int32).astype(jnp.float32)) * (1.0 / FIXED)
        for ref in got_refs
    ]
    for b in range(blocks):
        total = None
        for ref, scale in zip(got_refs, scales):
            part = ref[b * irec : (b + 1) * irec, :].astype(jnp.int32).astype(jnp.float32)
            part = part * scale[b : b + 1]
            total = part if total is None else total + part
        for m in range(members):
            out_refs[m][:, b * LANES : (b + 1) * LANES] = total[m * rows : (m + 1) * rows]


def join_kernel(count_ref, got_ref, out_to, out_ref, sems):
    src_total, rows_total, _ = got_ref.shape
    k_own, col_total = out_ref.shape
    own_blocks = k_own // LANES
    cols = (rows_total - CODES) // own_blocks
    members = col_total // cols
    seg_ids = lax.broadcasted_iota(jnp.int32, (LANES, col_total), 0) % S
    inside = seg_ids < count_ref[...]
    scales = []
    for src in range(src_total):
        codes = got_ref[src, own_blocks * cols :, :].astype(jnp.int32).astype(jnp.float32)
        scales.append(jnp.exp2(codes) * (1.0 / FIXED))
    copies = []
    for b in range(own_blocks):
        rows = []
        for m in range(members):
            total = None
            for src in range(m, src_total, members):
                part = got_ref[src, b * cols : (b + 1) * cols, :]
                part = part.astype(jnp.int32).astype(jnp.float32) * scales[src][b : b + 1]
                total = part if total is None else total + part
            rows.append(total)
        whole = jnp.concatenate(rows, axis=0).T
        rows = pl.ds(b * LANES, LANES)
        out_ref[rows, :] = jnp.where(inside, whole, 0.0)
        copies.append(pltpu.make_async_copy(out_ref.at[rows], out_to.at[rows], sems.at[b]))
        copies[-1].start()
    for copy in copies:
        copy.wait()


def swap(x, axis, total, k):
    return lax.ppermute(x, axis, [(r, r ^ k) for r in range(total)])


def shards(
    receiver_spectra,
    reference_spectra,
    receiver_counts,
    reference_counts,
    column_station,
    lag_window,
    observed,
    *,
    rcv_total,
    ref_total,
):
    row_total, k_quarter = receiver_spectra.shape
    k_own, col_total = reference_spectra.shape
    k_total = k_own * rcv_total
    lag_total = observed.shape[2]
    half = lag_total // 2
    members = math.gcd(GROUP, rcv_total)
    irec = row_total * members
    cols = col_total // members
    jj_total = LANES // (2 * irec)
    jp_total = cols // jj_total
    extra = k_quarter // half + 1
    bf16 = jnp.bfloat16
    place = lax.axis_index("rcv")
    mine = place % members
    quarter = lax.axis_index("ref")
    vmem = pl.BlockSpec(memory_space=pltpu.VMEM)
    smem = pl.BlockSpec(memory_space=pltpu.SMEM)
    hbm = pl.BlockSpec(memory_space=pl.ANY)
    scalars = jnp.stack([mine, quarter * col_total, place, quarter]).astype(jnp.int32)
    def params(mib):
        return pltpu.CompilerParams(vmem_limit_bytes=mib * 1024 * 1024)

    free = pl.CostEstimate(flops=0, bytes_accessed=0, transcendentals=0)

    sent = pl.pallas_call(
        turn_kernel,
        out_shape=jax.ShapeDtypeStruct((rcv_total, cols, k_own), bf16),
        in_specs=[hbm] * 2,
        out_specs=hbm,
        scratch_shapes=[
            pltpu.VMEM((k_own, col_total), bf16),
            pltpu.VMEM((1, col_total), jnp.int32),
            pltpu.VMEM((col_total, k_own), bf16),
            pltpu.SemaphoreType.DMA((max(rcv_total, 1 + k_own // min(k_own, 2 * LANES)),)),
        ],
        compiler_params=params(62),
        cost_estimate=free,
    )(reference_spectra, reference_counts.reshape(1, col_total))
    v_all = lax.all_to_all(sent, "rcv", split_axis=0, concat_axis=0, tiled=True)

    _, observed = lax.optimization_barrier((sent, observed))
    shape = (cols, row_total, half)
    u_own, *folded = pl.pallas_call(
        fold_kernel,
        out_shape=[jax.ShapeDtypeStruct((extra, row_total, half), bf16)]
        + [jax.ShapeDtypeStruct(shape, bf16)] * members,
        in_specs=[smem] * 2 + [hbm] * 4,
        out_specs=[hbm] * (1 + members),
        scratch_shapes=[
            pltpu.VMEM(observed.shape, bf16),
            pltpu.VMEM(receiver_spectra.shape, bf16),
            pltpu.VMEM(lag_window.shape, jnp.int32),
            pltpu.VMEM((1, col_total), jnp.int32),
            pltpu.VMEM((half // LANES * col_total * row_total, LANES), jnp.float32),
            pltpu.VMEM((members,) + shape, bf16),
            pltpu.VMEM((extra, row_total, half), bf16),
            pltpu.SemaphoreType.DMA((row_total + 3,)),
            pltpu.SemaphoreType.DMA((members + 1,)),
        ],
        compiler_params=params(32),
        cost_estimate=free,
    )(
        scalars,
        receiver_counts,
        observed,
        receiver_spectra,
        lag_window,
        column_station.reshape(1, col_total),
    )
    e_all = [folded[0]] + [swap(folded[k], "rcv", rcv_total, k) for k in range(1, members)]

    near = pl.pallas_call(
        near_kernel,
        out_shape=jax.ShapeDtypeStruct((members, extra, row_total, half), bf16),
        in_specs=[hbm] * members,
        out_specs=hbm,
        scratch_shapes=[pltpu.SemaphoreType.DMA((members,))],
        compiler_params=params(16),
        cost_estimate=free,
    )(u_own, *[swap(u_own, "rcv", rcv_total, k) for k in range(1, members)])
    u_all = [near] + [swap(near, "ref", ref_total, k) for k in range(1, ref_total)]

    group_counts = near[:, extra - 1, :, 0].reshape(irec).astype(jnp.float32)
    own_counts = lax.dynamic_slice_in_dim(reference_counts, mine * cols, cols).astype(jnp.float32)
    counts = own_counts.reshape(jj_total, jp_total).T
    least = jnp.minimum(counts[:, :, None], group_counts[None, None, :])
    inverse = (1.0 / least).reshape(jp_total, jj_total * irec)
    inverse = jnp.concatenate([inverse, inverse], axis=1)

    table = lag_tables(k_total // (2 * S), lag_total)
    w_rows = k_own // LANES * cols + CODES
    lines = jp_total * (k_total // (2 * S) + PAD)
    w_part, z_part = pl.pallas_call(
        functools.partial(pair_kernel, members, ref_total),
        out_shape=[
            jax.ShapeDtypeStruct((rcv_total, w_rows, LANES), jnp.int16),
            jax.ShapeDtypeStruct((k_total // LANES, FB * jp_total, LANES), bf16),
        ],
        in_specs=[smem, vmem] + [hbm] * (2 + members + ref_total),
        out_specs=[hbm] * 2,
        scratch_shapes=[
            pltpu.VMEM((lines, LANES), jnp.float32),
            pltpu.VMEM((lines, LANES), jnp.float32),
            pltpu.VMEM((irec, k_total), bf16),
            pltpu.VMEM((irec, k_total), bf16),
            pltpu.VMEM((k_total // LANES, LANES), jnp.float32),
            pltpu.VMEM((ref_total,) + near.shape, bf16),
            pltpu.VMEM((rcv_total, cols, k_own), bf16),
            pltpu.VMEM((members, cols, row_total, half), bf16),
            pltpu.VMEM((k_total // LANES, FB * jp_total, LANES), bf16),
            pltpu.VMEM((rcv_total, w_rows, LANES), jnp.int16),
            pltpu.VMEM(table.shape, bf16),
            pltpu.SemaphoreType.DMA((2 + members + ref_total,)),
            pltpu.SemaphoreType.DMA((rcv_total,)),
            pltpu.SemaphoreType.DMA((rcv_total,)),
        ],
        compiler_params=params(62),
        cost_estimate=free,
    )(scalars, inverse, v_all, table, *e_all, *u_all)

    got = lax.all_to_all(w_part, "rcv", split_axis=0, concat_axis=0, tiled=True)
    reference_grad = pl.pallas_call(
        join_kernel,
        out_shape=jax.ShapeDtypeStruct((k_own, col_total), jnp.float32),
        in_specs=[vmem] * 2,
        out_specs=hbm,
        scratch_shapes=[
            pltpu.VMEM((k_own, col_total), jnp.float32),
            pltpu.SemaphoreType.DMA((k_own // LANES,)),
        ],
        compiler_params=params(32),
        cost_estimate=free,
    )(reference_counts.reshape(1, col_total), got)

    r_rows = k_quarter // LANES * irec + CODES
    r_all = pl.pallas_call(
        receiver_sum_kernel,
        out_shape=[jax.ShapeDtypeStruct((r_rows, LANES), jnp.int16)] * ref_total,
        in_specs=[smem] + [hbm] * 2,
        out_specs=[hbm] * ref_total,
        scratch_shapes=[
            pltpu.VMEM((rcv_total, cols, k_own), bf16),
            pltpu.VMEM(z_part.shape, bf16),
            pltpu.VMEM((ref_total, r_rows, LANES), jnp.int16),
            pltpu.VMEM((k_total // LANES, LANES), jnp.float32),
            pltpu.SemaphoreType.DMA((2 + ref_total,)),
        ],
        compiler_params=params(62),
        cost_estimate=free,
    )(scalars, v_all, z_part)

    parts = pl.pallas_call(
        functools.partial(add_kernel, ref_total),
        out_shape=[jax.ShapeDtypeStruct((row_total, k_quarter), jnp.float32)] * members,
        in_specs=[vmem] * ref_total,
        out_specs=[vmem] * members,
        compiler_params=params(16),
        cost_estimate=free,
    )(r_all[0], *[swap(r_all[k], "ref", ref_total, k) for k in range(1, ref_total)])
    r_sum = parts[0]
    for k in range(1, members):
        r_sum = r_sum + swap(parts[k], "rcv", rcv_total, k)
    seg_quarter = jnp.arange(k_quarter, dtype=jnp.int32) % S
    receiver_grad = jnp.where(seg_quarter[None, :] < receiver_counts[:, None], r_sum, 0.0)
    return (receiver_grad, reference_grad)


def solution(mesh):
    return jax.shard_map(
        functools.partial(shards, rcv_total=mesh.shape["rcv"], ref_total=mesh.shape["ref"]),
        mesh=mesh,
        in_specs=(
            P("rcv", "ref"),
            P("rcv", "ref"),
            P("rcv"),
            P("ref"),
            P("ref"),
            P(None, "rcv", "ref"),
            P("rcv", "ref", None),
        ),
        out_specs=(P("rcv", "ref"), P("rcv", "ref")),
        check_vma=False,
    )
```

```python
import functools
import math

import jax
import jax.numpy as jnp
import numpy as np
from jax import lax
from jax.experimental import pallas as pl
from jax.experimental.pallas import tpu as pltpu
from jax.sharding import PartitionSpec as P

L = 512
S = 16
F = 256

env_floor = 0.05
misfit_scale = 0.03125
GROUP = 4
LANES = 128
FB = LANES // (2 * S)
WIDTH = 16
FIXED = 32000.0
PAD = 8
CODES = 16


def lag_tables(freq_total, lag_total):
    half = lag_total // 2
    freq_ids = np.arange(freq_total)[:, None]
    phase = 2.0 * np.pi * (freq_ids * np.arange(half)[None, :] % lag_total) / lag_total
    cosine = np.cos(phase) / math.sqrt(freq_total)
    sine = np.sin(phase) / math.sqrt(freq_total)
    back = [np.concatenate([cosine[p::2], sine[p::2]], axis=1) for p in (0, 1)]
    ahead = [np.concatenate([cosine[p::2].T, sine[p::2].T], axis=1) for p in (0, 1)]
    back = [np.concatenate([t[:, :half], t[:, half:]], axis=0) for t in back]
    whole = np.concatenate(ahead + back, axis=0)
    return jnp.asarray(whole.astype(np.float32)).astype(jnp.bfloat16)


def nt(a, b):
    return lax.dot_general(a, b, (((1,), (1,)), ((), ())), preferred_element_type=jnp.float32)


def nn(a, b):
    return jnp.dot(a, b, preferred_element_type=jnp.float32)


def tn(a, b):
    return lax.dot_general(a, b, (((0,), (0,)), ((), ())), preferred_element_type=jnp.float32)


def eye_of(size):
    rows = lax.broadcasted_iota(jnp.int32, (size, size), 0)
    lanes = lax.broadcasted_iota(jnp.int32, (size, size), 1)
    return jnp.where(rows == lanes, 1.0, 0.0).astype(jnp.bfloat16)


def turn_kernel(spectra_from, counts_from, v_to, spectra_ref, counts_ref, turned_ref, sems):
    k_own, col_total = spectra_ref.shape
    rcv_total, cols, _ = v_to.shape
    members = col_total // cols
    width = min(k_own, 2 * LANES)
    copies = [pltpu.make_async_copy(counts_from, counts_ref, sems.at[0])]
    for n, begin in enumerate(range(0, k_own, width)):
        rows = pl.ds(begin, width)
        copies.append(
            pltpu.make_async_copy(spectra_from.at[rows], spectra_ref.at[rows], sems.at[1 + n])
        )
    for copy in copies:
        copy.start()
    eye = eye_of(col_total)
    seg_ids = lax.broadcasted_iota(jnp.int32, (width, col_total), 0) % S
    copies[0].wait()
    inside = seg_ids < counts_ref[...]
    for n, begin in enumerate(range(0, k_own, width)):
        copies[1 + n].wait()
        part = spectra_ref[begin : begin + width, :].astype(jnp.float32)
        part = jnp.where(inside, part, 0.0).astype(jnp.bfloat16)
        turned_ref[:, begin : begin + width] = nt(eye, part).astype(jnp.bfloat16)
    copies = [
        pltpu.make_async_copy(
            turned_ref.at[pl.ds(dest % members * cols, cols)], v_to.at[dest], sems.at[dest]
        )
        for dest in range(rcv_total)
    ]
    for copy in copies:
        copy.start()
    for copy in copies:
        copy.wait()


def fold_kernel(c_ref, rcounts_ref, observed_from, rspectra_from, window_from, order_from, *rest):
    u_to, *out_to = rest[:-9]
    (
        observed_ref, rspectra_ref, window_ref, order_ref, line_ref, out_ref, u_ref, sems, out_sems,
    ) = rest[-9:]
    row_total, col_total, lag_total = observed_ref.shape
    half = lag_total // 2
    members = len(out_to)
    cols = col_total // members
    lines = col_total * row_total
    quarter = rspectra_ref.shape[1]
    copies = [
        pltpu.make_async_copy(src, dst, sems.at[row_total + n])
        for n, (src, dst) in enumerate(
            [(window_from, window_ref), (order_from, order_ref), (rspectra_from, rspectra_ref)]
        )
    ] + [
        pltpu.make_async_copy(observed_from.at[i], observed_ref.at[i], sems.at[i])
        for i in range(row_total)
    ]
    for copy in copies:
        copy.start()
    for copy in copies[:3]:
        copy.wait()
    row_ids = lax.broadcasted_iota(jnp.int32, (row_total, half), 0)
    counts = jnp.zeros((row_total, half), jnp.int32)
    for i in range(row_total):
        counts = jnp.where(row_ids == i, rcounts_ref[i], counts)
    seg_ids = lax.broadcasted_iota(jnp.int32, (row_total, half), 1) % S
    pieces = quarter // half
    for n in range(pieces):
        part = rspectra_ref[:, n * half : (n + 1) * half].astype(jnp.float32)
        u_ref[n] = jnp.where(seg_ids < counts, part, 0.0).astype(jnp.bfloat16)
    u_ref[pieces] = counts.astype(jnp.float32).astype(jnp.bfloat16)
    u_copy = pltpu.make_async_copy(u_ref, u_to, out_sems.at[members])
    u_copy.start()
    window = jnp.concatenate([window_ref[0], window_ref[1]], axis=0).astype(jnp.float32).T
    station = lax.broadcasted_iota(jnp.int32, (col_total, col_total), 0) + c_ref[1]
    pick = jnp.where(station == order_ref[...], 1.0, 0.0).astype(jnp.bfloat16)
    lag_ids = lax.broadcasted_iota(jnp.int32, (col_total, half), 1).astype(jnp.float32)
    for i in range(row_total):
        copies[3 + i].wait()
        begin = window[:, i : i + 1]
        end = begin + window[:, row_total + i : row_total + i + 1]
        values = observed_ref[i].astype(jnp.float32)
        low = (lag_ids >= begin) & (lag_ids < end)
        high = (lag_ids + half >= begin) & (lag_ids + half < end)
        folded = jnp.where(low, values[:, :half], jnp.where(high, -values[:, half:], 0.0))
        moved = nn(pick, folded.astype(jnp.bfloat16))
        for h in range(half // LANES):
            line_ref[pl.ds(h * lines + i, col_total, stride=row_total), :] = moved[
                :, h * LANES : (h + 1) * LANES
            ]
    mine = c_ref[0]
    copies = []
    for k in range(members):
        first = (mine ^ k) * (cols * row_total)
        for h in range(half // LANES):
            begin = pl.multiple_of(h * lines + first, cols * row_total)
            rows = line_ref[pl.ds(begin, cols * row_total), :]
            out_ref[k, :, :, h * LANES : (h + 1) * LANES] = rows.reshape(
                cols, row_total, LANES
            ).astype(jnp.bfloat16)
        copies.append(pltpu.make_async_copy(out_ref.at[k], out_to[k], out_sems.at[k]))
        copies[-1].start()
    for copy in copies + [u_copy]:
        copy.wait()


def near_kernel(*refs):
    *parts, out_ref, sems = refs
    copies = [
        pltpu.make_async_copy(ref, out_ref.at[k], sems.at[k]) for k, ref in enumerate(parts)
    ]
    for copy in copies:
        copy.start()
    for copy in copies:
        copy.wait()


def pair_kernel(n_e, n_r, c_ref, invn_ref, v_from, table_from, *refs):
    refs = list(refs)
    e_from, u_from = refs[:n_e], refs[n_e : n_e + n_r]
    w_to, z_to = refs[n_e + n_r : n_e + n_r + 2]
    (
        x_ref, z_ref, plain_ref, turned_ref, code_ref, u_ref, v_ref, e_ref, z_out_ref, w_ref,
        table_ref, sems, w_sems, z_sems,
    ) = refs[n_e + n_r + 2 :]

    src_total, col_total, k_own = v_ref.shape
    irec, k_quarter = plain_ref.shape[0], (u_ref.shape[2] - 1) * u_ref.shape[4]
    jj_total = LANES // (2 * irec)
    jp_total = col_total // jj_total
    k_total = src_total * k_own
    half_f = k_total // (4 * S)
    freq_total = 2 * half_f
    pitch = freq_total + PAD
    blocks = k_total // LANES
    own_blocks = k_own // LANES
    quarter_blocks = k_quarter // LANES

    quarter_me = c_ref[3]
    early = [pltpu.make_async_copy(v_from, v_ref, sems.at[0])]
    for k, ref in enumerate(u_from):
        early.append(pltpu.make_async_copy(ref, u_ref.at[quarter_me ^ k], sems.at[1 + k]))
    late = [
        pltpu.make_async_copy(ref, e_ref.at[k], sems.at[1 + n_r + k])
        for k, ref in enumerate(e_from)
    ]
    late.append(pltpu.make_async_copy(table_from, table_ref, sems.at[1 + n_r + n_e]))
    for copy in early + late:
        copy.start()
    half = e_ref.shape[-1]
    eye = eye_of(half)
    group_ids = lax.broadcasted_iota(jnp.int32, (jp_total, LANES), 1) // (2 * S)
    first_part = lax.broadcasted_iota(jnp.int32, (irec, LANES), 1) % (2 * S) < S

    def lanes_of(fb, per):
        return fb // per, pl.multiple_of(fb % per * LANES, LANES)

    def v_block(fb):
        src, off = lanes_of(fb, own_blocks)
        parts = [
            v_ref[src, jj * jp_total : (jj + 1) * jp_total, pl.ds(off, LANES)]
            for jj in range(jj_total)
        ]
        zero = jnp.zeros((jp_total, LANES), jnp.bfloat16)
        rows = [
            jnp.concatenate([jnp.where(group_ids == f, part, zero) for part in parts], axis=1)
            for f in range(FB)
        ]
        return jnp.concatenate(rows, axis=0)

    def u_block(parts):
        zero = jnp.zeros((irec, LANES), jnp.bfloat16)
        return jnp.concatenate(
            [
                jnp.concatenate([part if k == jj else zero for k in range(jj_total)], axis=1)
                for part in parts
                for jj in range(jj_total)
            ],
            axis=0,
        )

    def place(fb, f):
        return pl.ds((f % 2) * half_f + fb * (FB // 2) + f // 2, jp_total, stride=pitch)

    def forward(fb, _):
        lanes = pl.ds(pl.multiple_of(fb * LANES, LANES), LANES)
        quarter, off = lanes_of(fb, quarter_blocks)
        piece, off = off // half, pl.multiple_of(off % half, LANES)
        wide = u_ref[quarter, :, piece, :, pl.ds(off, LANES)].astype(jnp.float32)
        wide = wide.reshape(irec, LANES)
        part = wide.astype(jnp.bfloat16)
        plain_ref[:, lanes] = part
        crossed = jnp.where(first_part, pltpu.roll(wide, LANES - S, 1), -pltpu.roll(wide, S, 1))
        crossed = crossed.astype(jnp.bfloat16)
        turned_ref[:, lanes] = crossed
        out = nt(v_block(fb), u_block([part, crossed]))
        scale = invn_ref[...]
        for f in range(FB):
            x_ref[place(fb, f), :] = out[f * jp_total : (f + 1) * jp_total] * scale
        return 0

    for copy in early:
        copy.wait()
    lax.fori_loop(0, blocks, forward, 0, unroll=64)

    lane_ids = lax.broadcasted_iota(jnp.int32, (1, LANES), 1)
    sign = jnp.where(lane_ids < LANES // 2, -1.0, 1.0).astype(jnp.float32)

    sign = sign.astype(jnp.bfloat16)

    def pairs(step, _):
        cols = [step * WIDTH + k for k in range(WIDTH)]
        rhs_e, rhs_o, obs = [], [], []
        for jp in cols:
            x = x_ref[pl.ds(pl.multiple_of(jp * pitch, PAD), freq_total), :]
            plain = x.astype(jnp.bfloat16)
            turned = pltpu.roll(x, LANES // 2, 1).astype(jnp.bfloat16) * sign
            rhs_e.append(jnp.concatenate([plain[:half_f], turned[:half_f]], axis=0))
            rhs_o.append(jnp.concatenate([plain[half_f:], turned[half_f:]], axis=0))
            rows = [
                e_ref[:, jj * jp_total + jp].astype(jnp.float32).reshape(irec, half)
                for jj in range(jj_total)
            ]
            rows = jnp.concatenate(rows, axis=0).astype(jnp.bfloat16)
            obs += [rows, rows]
        even = nn(table_y[0], jnp.concatenate(rhs_e, axis=1))
        odd = nn(table_y[1], jnp.concatenate(rhs_o, axis=1))
        seen = nt(eye, jnp.concatenate(obs, axis=0))
        g_e, g_o = [], []
        for k in range(WIDTH):
            lanes = slice(k * LANES, (k + 1) * LANES)
            e, d0, d1 = seen[:, lanes], even[:, lanes], odd[:, lanes]
            d = jnp.where(e < 0.0, d0 + d1, d0 - d1)
            power = d * d
            power = power + (pltpu.roll(power, LANES // 2, 1) + env_floor)
            g = d * (1.0 - jnp.abs(e) * lax.rsqrt(power))
            side = jnp.where(e < 0.0, 1.0, jnp.where(e > 0.0, -1.0, 0.0)).astype(jnp.bfloat16)
            turned = pltpu.roll(g, LANES // 2, 1).astype(jnp.bfloat16)
            g_side = g.astype(jnp.bfloat16) * side
            t_side = turned * (side * -sign)
            g_e.append(jnp.concatenate([g_side * side, t_side * side], axis=0))
            g_o.append(jnp.concatenate([g_side, t_side], axis=0))
        z_e = nn(table_z[0], jnp.concatenate(g_e, axis=1))
        z_o = nn(table_z[1], jnp.concatenate(g_o, axis=1))
        for k, jp in enumerate(cols):
            lanes = slice(k * LANES, (k + 1) * LANES)
            scale = invn_ref[pl.ds(jp, 1), :] * misfit_scale
            base = pl.multiple_of(jp * pitch, PAD)
            z_ref[pl.ds(base, half_f), :] = z_e[:, lanes] * scale
            z_ref[pl.ds(base + half_f, half_f), :] = z_o[:, lanes] * scale
        return 0

    for copy in late:
        copy.wait()
    table_y = [table_ref[p * half : (p + 1) * half, :] for p in range(2)]
    table_z = []
    for p in range(2):
        begin = 2 * half + p * 2 * half_f
        parts = [table_ref[begin + n * half_f : begin + (n + 1) * half_f, :] for n in range(2)]
        table_z.append(jnp.concatenate(parts, axis=1))
    lax.fori_loop(0, jp_total // WIDTH, pairs, 0, unroll=2)

    def backward(src, b):
        fb = src * own_blocks + b
        z = jnp.concatenate([z_ref[place(fb, f), :] for f in range(FB)], axis=0)
        z = z.astype(jnp.bfloat16)
        lanes = pl.ds(pl.multiple_of(fb * LANES, LANES), LANES)
        w = nn(z, u_block([plain_ref[:, lanes], turned_ref[:, lanes]]))
        totals = []
        for jj in range(jj_total):
            lanes = slice(jj * LANES, (jj + 1) * LANES)
            total = w[:jp_total, lanes]
            for f in range(1, FB):
                total = jnp.where(group_ids == f, w[f * jp_total : (f + 1) * jp_total, lanes], total)
            totals.append(total)
        total = jnp.concatenate(totals, axis=0)
        largest = jnp.max(jnp.abs(total), axis=0, keepdims=True)
        power = jnp.ceil(jnp.log2(jnp.maximum(largest, 1e-30)))
        code_ref[pl.ds(fb, 1), :] = power
        fixed = jnp.round(total * (jnp.exp2(-power) * FIXED)).astype(jnp.int32)
        w_ref[src, b * col_total : (b + 1) * col_total, :] = fixed.astype(jnp.int16)
        z_out_ref[fb] = z

    def w_copy(src):
        return pltpu.make_async_copy(w_ref.at[src], w_to.at[src], w_sems.at[src])

    def z_copy(src):
        rows = pl.ds(src * own_blocks, own_blocks)
        return pltpu.make_async_copy(z_out_ref.at[rows], z_to.at[rows], z_sems.at[src])

    def from_owner(src, _):
        for b in range(own_blocks):
            backward(src, b)
        codes = code_ref[pl.ds(src * own_blocks, own_blocks), :]
        codes = jnp.concatenate(
            [codes, jnp.zeros((CODES - own_blocks, LANES), jnp.float32)], axis=0
        )
        w_ref[src, own_blocks * col_total :, :] = codes.astype(jnp.int32).astype(jnp.int16)
        w_copy(src).start()
        z_copy(src).start()
        return 0

    lax.fori_loop(0, src_total, from_owner, 0, unroll=4)
    for src in range(src_total):
        w_copy(src).wait()
        z_copy(src).wait()


def receiver_sum_kernel(c_ref, v_from, z_from, *refs):
    *r_to, v_ref, z_ref, r_ref, code_ref, sems = refs
    src_total, col_total, k_own = v_ref.shape
    ref_total = r_ref.shape[0]
    blocks = z_ref.shape[0]
    quarter_blocks = blocks // ref_total
    irec = (r_ref.shape[1] - CODES) // quarter_blocks
    jj_total = LANES // (2 * irec)
    jp_total = col_total // jj_total
    own_blocks = k_own // LANES
    copies = [
        pltpu.make_async_copy(v_from, v_ref, sems.at[0]),
        pltpu.make_async_copy(z_from, z_ref, sems.at[1]),
    ]
    for copy in copies:
        copy.start()
    group_ids = lax.broadcasted_iota(jnp.int32, (jp_total, LANES), 1) // (2 * S)
    first_part = lax.broadcasted_iota(jnp.int32, (irec, LANES), 1) % (2 * S) < S

    def lanes_of(fb, per):
        return fb // per, pl.multiple_of(fb % per * LANES, LANES)

    def v_block(fb):
        src, off = lanes_of(fb, own_blocks)
        parts = [
            v_ref[src, jj * jp_total : (jj + 1) * jp_total, pl.ds(off, LANES)]
            for jj in range(jj_total)
        ]
        zero = jnp.zeros((jp_total, LANES), jnp.bfloat16)
        rows = [
            jnp.concatenate([jnp.where(group_ids == f, part, zero) for part in parts], axis=1)
            for f in range(FB)
        ]
        return jnp.concatenate(rows, axis=0)

    def step(fb, _):
        z = z_ref[fb]
        r = tn(z, v_block(fb))
        sums = []
        for q in range(2):
            total = None
            for jj in range(jj_total):
                begin = (q * jj_total + jj) * irec
                part = r[begin : begin + irec, jj * LANES : (jj + 1) * LANES]
                total = part if total is None else total + part
            sums.append(total)
        crossed = jnp.where(
            first_part, -pltpu.roll(sums[1], LANES - S, 1), pltpu.roll(sums[1], S, 1)
        )
        total = sums[0] + crossed
        largest = jnp.max(jnp.abs(total), axis=0, keepdims=True)
        power = jnp.ceil(jnp.log2(jnp.maximum(largest, 1e-30)))
        code_ref[pl.ds(fb, 1), :] = power
        fixed = jnp.round(total * (jnp.exp2(-power) * FIXED)).astype(jnp.int32)
        rows = pl.ds(pl.multiple_of(fb % quarter_blocks * irec, irec), irec)
        r_ref[fb // quarter_blocks, rows, :] = fixed.astype(jnp.int16)
        return 0

    for copy in copies:
        copy.wait()
    lax.fori_loop(0, blocks, step, 0, unroll=32)
    for quarter in range(ref_total):
        codes = code_ref[quarter * quarter_blocks : (quarter + 1) * quarter_blocks, :]
        codes = jnp.concatenate(
            [codes, jnp.zeros((CODES - quarter_blocks, LANES), jnp.float32)], axis=0
        ) if quarter_blocks < CODES else codes
        r_ref[quarter, quarter_blocks * irec :, :] = codes.astype(jnp.int32).astype(jnp.int16)
    outs = [
        pltpu.make_async_copy(r_ref.at[c_ref[3] ^ k], ref, sems.at[2 + k])
        for k, ref in enumerate(r_to)
    ]
    for copy in outs:
        copy.start()
    for copy in outs:
        copy.wait()


def add_kernel(n_in, *refs):
    got_refs, out_refs = refs[:n_in], refs[n_in:]
    members = len(out_refs)
    rows, k_quarter = out_refs[0].shape
    blocks = k_quarter // LANES
    irec = rows * members
    scales = [
        jnp.exp2(ref[blocks * irec :, :].astype(jnp.int32).astype(jnp.float32)) * (1.0 / FIXED)
        for ref in got_refs
    ]
    for b in range(blocks):
        total = None
        for ref, scale in zip(got_refs, scales):
            part = ref[b * irec : (b + 1) * irec, :].astype(jnp.int32).astype(jnp.float32)
            part = part * scale[b : b + 1]
            total = part if total is None else total + part
        for m in range(members):
            out_refs[m][:, b * LANES : (b + 1) * LANES] = total[m * rows : (m + 1) * rows]


def join_kernel(count_ref, got_ref, out_to, out_ref, sems):
    src_total, rows_total, _ = got_ref.shape
    k_own, col_total = out_ref.shape
    own_blocks = k_own // LANES
    cols = (rows_total - CODES) // own_blocks
    members = col_total // cols
    seg_ids = lax.broadcasted_iota(jnp.int32, (LANES, col_total), 0) % S
    inside = seg_ids < count_ref[...]
    scales = []
    for src in range(src_total):
        codes = got_ref[src, own_blocks * cols :, :].astype(jnp.int32).astype(jnp.float32)
        scales.append(jnp.exp2(codes) * (1.0 / FIXED))
    copies = []
    for b in range(own_blocks):
        rows = []
        for m in range(members):
            total = None
            for src in range(m, src_total, members):
                part = got_ref[src, b * cols : (b + 1) * cols, :]
                part = part.astype(jnp.int32).astype(jnp.float32) * scales[src][b : b + 1]
                total = part if total is None else total + part
            rows.append(total)
        whole = jnp.concatenate(rows, axis=0).T
        rows = pl.ds(b * LANES, LANES)
        out_ref[rows, :] = jnp.where(inside, whole, 0.0)
        copies.append(pltpu.make_async_copy(out_ref.at[rows], out_to.at[rows], sems.at[b]))
        copies[-1].start()
    for copy in copies:
        copy.wait()


def swap(x, axis, total, k):
    return lax.ppermute(x, axis, [(r, r ^ k) for r in range(total)])


def shards(
    receiver_spectra,
    reference_spectra,
    receiver_counts,
    reference_counts,
    column_station,
    lag_window,
    observed,
    *,
    rcv_total,
    ref_total,
):
    row_total, k_quarter = receiver_spectra.shape
    k_own, col_total = reference_spectra.shape
    k_total = k_own * rcv_total
    lag_total = observed.shape[2]
    half = lag_total // 2
    members = math.gcd(GROUP, rcv_total)
    irec = row_total * members
    cols = col_total // members
    jj_total = LANES // (2 * irec)
    jp_total = cols // jj_total
    extra = k_quarter // half + 1
    bf16 = jnp.bfloat16
    place = lax.axis_index("rcv")
    mine = place % members
    quarter = lax.axis_index("ref")
    vmem = pl.BlockSpec(memory_space=pltpu.VMEM)
    smem = pl.BlockSpec(memory_space=pltpu.SMEM)
    hbm = pl.BlockSpec(memory_space=pl.ANY)
    scalars = jnp.stack([mine, quarter * col_total, place, quarter]).astype(jnp.int32)
    def params(mib):
        return pltpu.CompilerParams(vmem_limit_bytes=mib * 1024 * 1024)

    free = pl.CostEstimate(flops=0, bytes_accessed=0, transcendentals=0)

    sent = pl.pallas_call(
        turn_kernel,
        out_shape=jax.ShapeDtypeStruct((rcv_total, cols, k_own), bf16),
        in_specs=[hbm] * 2,
        out_specs=hbm,
        scratch_shapes=[
            pltpu.VMEM((k_own, col_total), bf16),
            pltpu.VMEM((1, col_total), jnp.int32),
            pltpu.VMEM((col_total, k_own), bf16),
            pltpu.SemaphoreType.DMA((max(rcv_total, 1 + k_own // min(k_own, 2 * LANES)),)),
        ],
        compiler_params=params(62),
        cost_estimate=free,
    )(reference_spectra, reference_counts.reshape(1, col_total))
    v_all = lax.all_to_all(sent, "rcv", split_axis=0, concat_axis=0, tiled=True)

    _, observed = lax.optimization_barrier((sent, observed))
    shape = (cols, row_total, half)
    u_own, *folded = pl.pallas_call(
        fold_kernel,
        out_shape=[jax.ShapeDtypeStruct((extra, row_total, half), bf16)]
        + [jax.ShapeDtypeStruct(shape, bf16)] * members,
        in_specs=[smem] * 2 + [hbm] * 4,
        out_specs=[hbm] * (1 + members),
        scratch_shapes=[
            pltpu.VMEM(observed.shape, bf16),
            pltpu.VMEM(receiver_spectra.shape, bf16),
            pltpu.VMEM(lag_window.shape, jnp.int32),
            pltpu.VMEM((1, col_total), jnp.int32),
            pltpu.VMEM(((half // LANES * col_total + 1) * row_total, LANES), jnp.float32),
            pltpu.VMEM((members,) + shape, bf16),
            pltpu.VMEM((extra, row_total, half), bf16),
            pltpu.SemaphoreType.DMA((row_total + 3,)),
            pltpu.SemaphoreType.DMA((members + 1,)),
        ],
        compiler_params=params(32),
        cost_estimate=free,
    )(
        scalars,
        receiver_counts,
        observed,
        receiver_spectra,
        lag_window,
        column_station.reshape(1, col_total),
    )
    e_all = [folded[0]] + [swap(folded[k], "rcv", rcv_total, k) for k in range(1, members)]

    near = pl.pallas_call(
        near_kernel,
        out_shape=jax.ShapeDtypeStruct((members, extra, row_total, half), bf16),
        in_specs=[hbm] * members,
        out_specs=hbm,
        scratch_shapes=[pltpu.SemaphoreType.DMA((members,))],
        compiler_params=params(16),
        cost_estimate=free,
    )(u_own, *[swap(u_own, "rcv", rcv_total, k) for k in range(1, members)])
    u_all = [near] + [swap(near, "ref", ref_total, k) for k in range(1, ref_total)]

    group_counts = near[:, extra - 1, :, 0].reshape(irec).astype(jnp.float32)
    own_counts = lax.dynamic_slice_in_dim(reference_counts, mine * cols, cols).astype(jnp.float32)
    counts = own_counts.reshape(jj_total, jp_total).T
    least = jnp.minimum(counts[:, :, None], group_counts[None, None, :])
    inverse = (1.0 / least).reshape(jp_total, jj_total * irec)
    inverse = jnp.concatenate([inverse, inverse], axis=1)

    table = lag_tables(k_total // (2 * S), lag_total)
    w_rows = k_own // LANES * cols + CODES
    lines = (jp_total + 1) * (k_total // (2 * S) + PAD)
    w_part, z_part = pl.pallas_call(
        functools.partial(pair_kernel, members, ref_total),
        out_shape=[
            jax.ShapeDtypeStruct((rcv_total, w_rows, LANES), jnp.int16),
            jax.ShapeDtypeStruct((k_total // LANES, FB * jp_total, LANES), bf16),
        ],
        in_specs=[smem, vmem] + [hbm] * (2 + members + ref_total),
        out_specs=[hbm] * 2,
        scratch_shapes=[
            pltpu.VMEM((lines, LANES), jnp.float32),
            pltpu.VMEM((lines, LANES), jnp.float32),
            pltpu.VMEM((irec, k_total), bf16),
            pltpu.VMEM((irec, k_total), bf16),
            pltpu.VMEM((k_total // LANES, LANES), jnp.float32),
            pltpu.VMEM((ref_total,) + near.shape, bf16),
            pltpu.VMEM((rcv_total, cols, k_own), bf16),
            pltpu.VMEM((members, cols, row_total, half), bf16),
            pltpu.VMEM((k_total // LANES, FB * jp_total, LANES), bf16),
            pltpu.VMEM((rcv_total, w_rows, LANES), jnp.int16),
            pltpu.VMEM(table.shape, bf16),
            pltpu.SemaphoreType.DMA((2 + members + ref_total,)),
            pltpu.SemaphoreType.DMA((rcv_total,)),
            pltpu.SemaphoreType.DMA((rcv_total,)),
        ],
        compiler_params=params(62),
        cost_estimate=free,
    )(scalars, inverse, v_all, table, *e_all, *u_all)

    got = lax.all_to_all(w_part, "rcv", split_axis=0, concat_axis=0, tiled=True)
    reference_grad = pl.pallas_call(
        join_kernel,
        out_shape=jax.ShapeDtypeStruct((k_own, col_total), jnp.float32),
        in_specs=[vmem] * 2,
        out_specs=hbm,
        scratch_shapes=[
            pltpu.VMEM((k_own, col_total), jnp.float32),
            pltpu.SemaphoreType.DMA((k_own // LANES,)),
        ],
        compiler_params=params(32),
        cost_estimate=free,
    )(reference_counts.reshape(1, col_total), got)

    r_rows = k_quarter // LANES * irec + CODES
    r_all = pl.pallas_call(
        receiver_sum_kernel,
        out_shape=[jax.ShapeDtypeStruct((r_rows, LANES), jnp.int16)] * ref_total,
        in_specs=[smem] + [hbm] * 2,
        out_specs=[hbm] * ref_total,
        scratch_shapes=[
            pltpu.VMEM((rcv_total, cols, k_own), bf16),
            pltpu.VMEM(z_part.shape, bf16),
            pltpu.VMEM((ref_total, r_rows, LANES), jnp.int16),
            pltpu.VMEM((k_total // LANES, LANES), jnp.float32),
            pltpu.SemaphoreType.DMA((2 + ref_total,)),
        ],
        compiler_params=params(62),
        cost_estimate=free,
    )(scalars, v_all, z_part)

    parts = pl.pallas_call(
        functools.partial(add_kernel, ref_total),
        out_shape=[jax.ShapeDtypeStruct((row_total, k_quarter), jnp.float32)] * members,
        in_specs=[vmem] * ref_total,
        out_specs=[vmem] * members,
        compiler_params=params(16),
        cost_estimate=free,
    )(r_all[0], *[swap(r_all[k], "ref", ref_total, k) for k in range(1, ref_total)])
    r_sum = parts[0]
    for k in range(1, members):
        r_sum = r_sum + swap(parts[k], "rcv", rcv_total, k)
    seg_quarter = jnp.arange(k_quarter, dtype=jnp.int32) % S
    receiver_grad = jnp.where(seg_quarter[None, :] < receiver_counts[:, None], r_sum, 0.0)
    return (receiver_grad, reference_grad)


def solution(mesh):
    return jax.shard_map(
        functools.partial(shards, rcv_total=mesh.shape["rcv"], ref_total=mesh.shape["ref"]),
        mesh=mesh,
        in_specs=(
            P("rcv", "ref"),
            P("rcv", "ref"),
            P("rcv"),
            P("ref"),
            P("ref"),
            P(None, "rcv", "ref"),
            P("rcv", "ref", None),
        ),
        out_specs=(P("rcv", "ref"), P("rcv", "ref")),
        check_vma=False,
    )
```

```python
import functools
import math

import jax
import jax.numpy as jnp
import numpy as np
from jax import lax
from jax.experimental import pallas as pl
from jax.experimental.pallas import tpu as pltpu
from jax.sharding import PartitionSpec as P

L = 512
S = 16
F = 256

env_floor = 0.05
misfit_scale = 0.03125
GROUP = 4
LANES = 128
FB = LANES // (2 * S)
WIDTH = 16
FIXED = 32000.0
PAD = 8
CODES = 16


def lag_tables(freq_total, lag_total):
    half = lag_total // 2
    freq_ids = np.arange(freq_total)[:, None]
    phase = 2.0 * np.pi * (freq_ids * np.arange(half)[None, :] % lag_total) / lag_total
    cosine = np.cos(phase) / math.sqrt(freq_total)
    sine = np.sin(phase) / math.sqrt(freq_total)
    back = [np.concatenate([cosine[p::2], sine[p::2]], axis=1) for p in (0, 1)]
    ahead = [np.concatenate([cosine[p::2].T, sine[p::2].T], axis=1) for p in (0, 1)]
    back = [np.concatenate([t[:, :half], t[:, half:]], axis=0) for t in back]
    whole = np.concatenate(ahead + back, axis=0)
    return jnp.asarray(whole.astype(np.float32)).astype(jnp.bfloat16)


def nt(a, b):
    return lax.dot_general(a, b, (((1,), (1,)), ((), ())), preferred_element_type=jnp.float32)


def nn(a, b):
    return jnp.dot(a, b, preferred_element_type=jnp.float32)


def tn(a, b):
    return lax.dot_general(a, b, (((0,), (0,)), ((), ())), preferred_element_type=jnp.float32)


def eye_of(size):
    rows = lax.broadcasted_iota(jnp.int32, (size, size), 0)
    lanes = lax.broadcasted_iota(jnp.int32, (size, size), 1)
    return jnp.where(rows == lanes, 1.0, 0.0).astype(jnp.bfloat16)


def turn_kernel(spectra_from, counts_from, v_to, spectra_ref, counts_ref, turned_ref, sems):
    k_own, col_total = spectra_ref.shape
    rcv_total, cols, _ = v_to.shape
    members = col_total // cols
    width = min(k_own, 4 * LANES)
    copies = [pltpu.make_async_copy(counts_from, counts_ref, sems.at[0])]
    for n, begin in enumerate(range(0, k_own, width)):
        rows = pl.ds(begin, width)
        copies.append(
            pltpu.make_async_copy(spectra_from.at[rows], spectra_ref.at[rows], sems.at[1 + n])
        )
    for copy in copies:
        copy.start()
    eye = eye_of(col_total)
    seg_ids = lax.broadcasted_iota(jnp.int32, (width, col_total), 0) % S
    copies[0].wait()
    inside = jnp.where(seg_ids < counts_ref[...], 1.0, 0.0).astype(jnp.bfloat16)
    for n, begin in enumerate(range(0, k_own, width)):
        copies[1 + n].wait()
        part = spectra_ref[begin : begin + width, :] * inside
        turned_ref[:, begin : begin + width] = nt(eye, part).astype(jnp.bfloat16)
    copies = [
        pltpu.make_async_copy(
            turned_ref.at[pl.ds(dest % members * cols, cols)], v_to.at[dest], sems.at[dest]
        )
        for dest in range(rcv_total)
    ]
    for copy in copies:
        copy.start()
    for copy in copies:
        copy.wait()


def fold_kernel(c_ref, rcounts_ref, observed_from, rspectra_from, window_from, order_from, *rest):
    u_to, *out_to = rest[:-9]
    (
        observed_ref, rspectra_ref, window_ref, order_ref, line_ref, out_ref, u_ref, sems, out_sems,
    ) = rest[-9:]
    row_total, col_total, lag_total = observed_ref.shape
    half = lag_total // 2
    members = len(out_to)
    cols = col_total // members
    lines = col_total * row_total
    quarter = rspectra_ref.shape[1]
    copies = [
        pltpu.make_async_copy(src, dst, sems.at[row_total + n])
        for n, (src, dst) in enumerate(
            [(window_from, window_ref), (order_from, order_ref), (rspectra_from, rspectra_ref)]
        )
    ] + [
        pltpu.make_async_copy(observed_from.at[i], observed_ref.at[i], sems.at[i])
        for i in range(row_total)
    ]
    for copy in copies:
        copy.start()
    for copy in copies[:3]:
        copy.wait()
    row_ids = lax.broadcasted_iota(jnp.int32, (row_total, half), 0)
    counts = jnp.zeros((row_total, half), jnp.int32)
    for i in range(row_total):
        counts = jnp.where(row_ids == i, rcounts_ref[i], counts)
    seg_ids = lax.broadcasted_iota(jnp.int32, (row_total, half), 1) % S
    pieces = quarter // half
    for n in range(pieces):
        part = rspectra_ref[:, n * half : (n + 1) * half].astype(jnp.float32)
        u_ref[n] = jnp.where(seg_ids < counts, part, 0.0).astype(jnp.bfloat16)
    u_ref[pieces] = counts.astype(jnp.float32).astype(jnp.bfloat16)
    u_copy = pltpu.make_async_copy(u_ref, u_to, out_sems.at[members])
    u_copy.start()
    window = jnp.concatenate([window_ref[0], window_ref[1]], axis=0).astype(jnp.float32).T
    station = lax.broadcasted_iota(jnp.int32, (col_total, col_total), 0) + c_ref[1]
    pick = jnp.where(station == order_ref[...], 1.0, 0.0).astype(jnp.bfloat16)
    lag_ids = lax.broadcasted_iota(jnp.int32, (col_total, half), 1).astype(jnp.float32)
    for i in range(row_total):
        copies[3 + i].wait()
        begin = window[:, i : i + 1]
        end = begin + window[:, row_total + i : row_total + i + 1]
        values = observed_ref[i].astype(jnp.float32)
        low = (lag_ids >= begin) & (lag_ids < end)
        high = (lag_ids + half >= begin) & (lag_ids + half < end)
        folded = jnp.where(low, values[:, :half], jnp.where(high, -values[:, half:], 0.0))
        moved = nn(pick, folded.astype(jnp.bfloat16))
        for h in range(half // LANES):
            line_ref[pl.ds(h * lines + i, col_total, stride=row_total), :] = moved[
                :, h * LANES : (h + 1) * LANES
            ]
    mine = c_ref[0]
    copies = []
    for k in range(members):
        first = (mine ^ k) * (cols * row_total)
        for h in range(half // LANES):
            begin = pl.multiple_of(h * lines + first, cols * row_total)
            rows = line_ref[pl.ds(begin, cols * row_total), :]
            out_ref[k, :, :, h * LANES : (h + 1) * LANES] = rows.reshape(
                cols, row_total, LANES
            ).astype(jnp.bfloat16)
        copies.append(pltpu.make_async_copy(out_ref.at[k], out_to[k], out_sems.at[k]))
        copies[-1].start()
    for copy in copies + [u_copy]:
        copy.wait()


def near_kernel(*refs):
    *parts, out_ref, sems = refs
    copies = [
        pltpu.make_async_copy(ref, out_ref.at[k], sems.at[k]) for k, ref in enumerate(parts)
    ]
    for copy in copies:
        copy.start()
    for copy in copies:
        copy.wait()


def pair_kernel(n_e, n_r, c_ref, invn_ref, v_from, table_from, *refs):
    refs = list(refs)
    e_from, u_from = refs[:n_e], refs[n_e : n_e + n_r]
    w_to, z_to = refs[n_e + n_r : n_e + n_r + 2]
    (
        x_ref, z_ref, plain_ref, turned_ref, code_ref, u_ref, v_ref, e_ref, z_out_ref, w_ref,
        table_ref, sems, w_sems, z_sems,
    ) = refs[n_e + n_r + 2 :]

    src_total, col_total, k_own = v_ref.shape
    irec, k_quarter = plain_ref.shape[0], (u_ref.shape[2] - 1) * u_ref.shape[4]
    jj_total = LANES // (2 * irec)
    jp_total = col_total // jj_total
    k_total = src_total * k_own
    half_f = k_total // (4 * S)
    freq_total = 2 * half_f
    pitch = freq_total + PAD
    blocks = k_total // LANES
    own_blocks = k_own // LANES
    quarter_blocks = k_quarter // LANES

    quarter_me = c_ref[3]
    early = [pltpu.make_async_copy(v_from, v_ref, sems.at[0])]
    for k, ref in enumerate(u_from):
        early.append(pltpu.make_async_copy(ref, u_ref.at[quarter_me ^ k], sems.at[1 + k]))
    late = [
        pltpu.make_async_copy(ref, e_ref.at[k], sems.at[1 + n_r + k])
        for k, ref in enumerate(e_from)
    ]
    late.append(pltpu.make_async_copy(table_from, table_ref, sems.at[1 + n_r + n_e]))
    for copy in early + late:
        copy.start()
    half = e_ref.shape[-1]
    eye = eye_of(half)
    group_ids = lax.broadcasted_iota(jnp.int32, (jp_total, LANES), 1) // (2 * S)
    first_part = lax.broadcasted_iota(jnp.int32, (irec, LANES), 1) % (2 * S) < S

    def lanes_of(fb, per):
        return fb // per, pl.multiple_of(fb % per * LANES, LANES)

    def v_block(fb):
        src, off = lanes_of(fb, own_blocks)
        parts = [
            v_ref[src, jj * jp_total : (jj + 1) * jp_total, pl.ds(off, LANES)]
            for jj in range(jj_total)
        ]
        zero = jnp.zeros((jp_total, LANES), jnp.bfloat16)
        rows = [
            jnp.concatenate([jnp.where(group_ids == f, part, zero) for part in parts], axis=1)
            for f in range(FB)
        ]
        return jnp.concatenate(rows, axis=0)

    def u_block(parts):
        zero = jnp.zeros((irec, LANES), jnp.bfloat16)
        return jnp.concatenate(
            [
                jnp.concatenate([part if k == jj else zero for k in range(jj_total)], axis=1)
                for part in parts
                for jj in range(jj_total)
            ],
            axis=0,
        )

    def place(fb, f):
        return pl.ds((f % 2) * half_f + fb * (FB // 2) + f // 2, jp_total, stride=pitch)

    def forward(fb, _):
        lanes = pl.ds(pl.multiple_of(fb * LANES, LANES), LANES)
        quarter, off = lanes_of(fb, quarter_blocks)
        piece, off = off // half, pl.multiple_of(off % half, LANES)
        wide = u_ref[quarter, :, piece, :, pl.ds(off, LANES)].astype(jnp.float32)
        wide = wide.reshape(irec, LANES)
        part = wide.astype(jnp.bfloat16)
        plain_ref[:, lanes] = part
        crossed = jnp.where(first_part, pltpu.roll(wide, LANES - S, 1), -pltpu.roll(wide, S, 1))
        crossed = crossed.astype(jnp.bfloat16)
        turned_ref[:, lanes] = crossed
        out = nt(v_block(fb), u_block([part, crossed]))
        scale = invn_ref[...]
        for f in range(FB):
            x_ref[place(fb, f), :] = out[f * jp_total : (f + 1) * jp_total] * scale
        return 0

    for copy in early:
        copy.wait()
    lax.fori_loop(0, blocks, forward, 0, unroll=64)

    lane_ids = lax.broadcasted_iota(jnp.int32, (1, LANES), 1)
    sign = jnp.where(lane_ids < LANES // 2, -1.0, 1.0).astype(jnp.float32)

    sign = sign.astype(jnp.bfloat16)

    def pairs(step, _):
        cols = [step * WIDTH + k for k in range(WIDTH)]
        rhs_e, rhs_o, obs = [], [], []
        for jp in cols:
            x = x_ref[pl.ds(pl.multiple_of(jp * pitch, PAD), freq_total), :]
            plain = x.astype(jnp.bfloat16)
            turned = pltpu.roll(x, LANES // 2, 1).astype(jnp.bfloat16) * sign
            rhs_e.append(jnp.concatenate([plain[:half_f], turned[:half_f]], axis=0))
            rhs_o.append(jnp.concatenate([plain[half_f:], turned[half_f:]], axis=0))
            rows = [
                e_ref[:, jj * jp_total + jp].astype(jnp.float32).reshape(irec, half)
                for jj in range(jj_total)
            ]
            rows = jnp.concatenate(rows, axis=0).astype(jnp.bfloat16)
            obs += [rows, rows]
        even = nn(table_y[0], jnp.concatenate(rhs_e, axis=1))
        odd = nn(table_y[1], jnp.concatenate(rhs_o, axis=1))
        seen = nt(eye, jnp.concatenate(obs, axis=0))
        g_e, g_o = [], []
        for k in range(WIDTH):
            lanes = slice(k * LANES, (k + 1) * LANES)
            e, d0, d1 = seen[:, lanes], even[:, lanes], odd[:, lanes]
            d = jnp.where(e < 0.0, d0 + d1, d0 - d1)
            power = d * d
            power = power + (pltpu.roll(power, LANES // 2, 1) + env_floor)
            g = d * (1.0 - jnp.abs(e) * lax.rsqrt(power))
            side = jnp.where(e < 0.0, 1.0, jnp.where(e > 0.0, -1.0, 0.0)).astype(jnp.bfloat16)
            turned = pltpu.roll(g, LANES // 2, 1).astype(jnp.bfloat16)
            g_side = g.astype(jnp.bfloat16) * side
            t_side = turned * (side * -sign)
            g_e.append(jnp.concatenate([g_side * side, t_side * side], axis=0))
            g_o.append(jnp.concatenate([g_side, t_side], axis=0))
        z_e = nn(table_z[0], jnp.concatenate(g_e, axis=1))
        z_o = nn(table_z[1], jnp.concatenate(g_o, axis=1))
        for k, jp in enumerate(cols):
            lanes = slice(k * LANES, (k + 1) * LANES)
            scale = invn_ref[pl.ds(jp, 1), :] * misfit_scale
            base = pl.multiple_of(jp * pitch, PAD)
            z_ref[pl.ds(base, half_f), :] = z_e[:, lanes] * scale
            z_ref[pl.ds(base + half_f, half_f), :] = z_o[:, lanes] * scale
        return 0

    for copy in late:
        copy.wait()
    table_y = [table_ref[p * half : (p + 1) * half, :] for p in range(2)]
    table_z = []
    for p in range(2):
        begin = 2 * half + p * 2 * half_f
        parts = [table_ref[begin + n * half_f : begin + (n + 1) * half_f, :] for n in range(2)]
        table_z.append(jnp.concatenate(parts, axis=1))
    lax.fori_loop(0, jp_total // WIDTH, pairs, 0, unroll=2)

    def backward(src, b):
        fb = src * own_blocks + b
        z = jnp.concatenate([z_ref[place(fb, f), :] for f in range(FB)], axis=0)
        z = z.astype(jnp.bfloat16)
        lanes = pl.ds(pl.multiple_of(fb * LANES, LANES), LANES)
        w = nn(z, u_block([plain_ref[:, lanes], turned_ref[:, lanes]]))
        totals = []
        for jj in range(jj_total):
            lanes = slice(jj * LANES, (jj + 1) * LANES)
            total = w[:jp_total, lanes]
            for f in range(1, FB):
                total = jnp.where(group_ids == f, w[f * jp_total : (f + 1) * jp_total, lanes], total)
            totals.append(total)
        total = jnp.concatenate(totals, axis=0)
        largest = jnp.max(jnp.abs(total), axis=0, keepdims=True)
        power = jnp.ceil(jnp.log2(jnp.maximum(largest, 1e-30)))
        code_ref[pl.ds(fb, 1), :] = power
        fixed = jnp.round(total * (jnp.exp2(-power) * FIXED)).astype(jnp.int32)
        w_ref[src, b * col_total : (b + 1) * col_total, :] = fixed.astype(jnp.int16)
        z_out_ref[fb] = z

    def w_copy(src):
        return pltpu.make_async_copy(w_ref.at[src], w_to.at[src], w_sems.at[src])

    def z_copy(src):
        rows = pl.ds(src * own_blocks, own_blocks)
        return pltpu.make_async_copy(z_out_ref.at[rows], z_to.at[rows], z_sems.at[src])

    def from_owner(src, _):
        for b in range(own_blocks):
            backward(src, b)
        codes = code_ref[pl.ds(src * own_blocks, own_blocks), :]
        codes = jnp.concatenate(
            [codes, jnp.zeros((CODES - own_blocks, LANES), jnp.float32)], axis=0
        )
        w_ref[src, own_blocks * col_total :, :] = codes.astype(jnp.int32).astype(jnp.int16)
        w_copy(src).start()
        z_copy(src).start()
        return 0

    lax.fori_loop(0, src_total, from_owner, 0, unroll=4)
    for src in range(src_total):
        w_copy(src).wait()
        z_copy(src).wait()


def receiver_sum_kernel(c_ref, v_from, z_from, *refs):
    *r_to, v_ref, z_ref, r_ref, code_ref, sems = refs
    src_total, col_total, k_own = v_ref.shape
    ref_total = r_ref.shape[0]
    blocks = z_ref.shape[0]
    quarter_blocks = blocks // ref_total
    irec = (r_ref.shape[1] - CODES) // quarter_blocks
    jj_total = LANES // (2 * irec)
    jp_total = col_total // jj_total
    own_blocks = k_own // LANES
    copies = [
        pltpu.make_async_copy(v_from, v_ref, sems.at[0]),
        pltpu.make_async_copy(z_from, z_ref, sems.at[1]),
    ]
    for copy in copies:
        copy.start()
    group_ids = lax.broadcasted_iota(jnp.int32, (jp_total, LANES), 1) // (2 * S)
    first_part = lax.broadcasted_iota(jnp.int32, (irec, LANES), 1) % (2 * S) < S

    def lanes_of(fb, per):
        return fb // per, pl.multiple_of(fb % per * LANES, LANES)

    def v_block(fb):
        src, off = lanes_of(fb, own_blocks)
        parts = [
            v_ref[src, jj * jp_total : (jj + 1) * jp_total, pl.ds(off, LANES)]
            for jj in range(jj_total)
        ]
        zero = jnp.zeros((jp_total, LANES), jnp.bfloat16)
        rows = [
            jnp.concatenate([jnp.where(group_ids == f, part, zero) for part in parts], axis=1)
            for f in range(FB)
        ]
        return jnp.concatenate(rows, axis=0)

    def step(fb, _):
        z = z_ref[fb]
        r = tn(z, v_block(fb))
        sums = []
        for q in range(2):
            total = None
            for jj in range(jj_total):
                begin = (q * jj_total + jj) * irec
                part = r[begin : begin + irec, jj * LANES : (jj + 1) * LANES]
                total = part if total is None else total + part
            sums.append(total)
        crossed = jnp.where(
            first_part, -pltpu.roll(sums[1], LANES - S, 1), pltpu.roll(sums[1], S, 1)
        )
        total = sums[0] + crossed
        largest = jnp.max(jnp.abs(total), axis=0, keepdims=True)
        power = jnp.ceil(jnp.log2(jnp.maximum(largest, 1e-30)))
        code_ref[pl.ds(fb, 1), :] = power
        fixed = jnp.round(total * (jnp.exp2(-power) * FIXED)).astype(jnp.int32)
        rows = pl.ds(pl.multiple_of(fb % quarter_blocks * irec, irec), irec)
        r_ref[fb // quarter_blocks, rows, :] = fixed.astype(jnp.int16)
        return 0

    for copy in copies:
        copy.wait()
    lax.fori_loop(0, blocks, step, 0, unroll=32)
    for quarter in range(ref_total):
        codes = code_ref[quarter * quarter_blocks : (quarter + 1) * quarter_blocks, :]
        codes = jnp.concatenate(
            [codes, jnp.zeros((CODES - quarter_blocks, LANES), jnp.float32)], axis=0
        ) if quarter_blocks < CODES else codes
        r_ref[quarter, quarter_blocks * irec :, :] = codes.astype(jnp.int32).astype(jnp.int16)
    outs = [
        pltpu.make_async_copy(r_ref.at[c_ref[3] ^ k], ref, sems.at[2 + k])
        for k, ref in enumerate(r_to)
    ]
    for copy in outs:
        copy.start()
    for copy in outs:
        copy.wait()


def add_kernel(n_in, *refs):
    got_refs, out_refs = refs[:n_in], refs[n_in:]
    members = len(out_refs)
    rows, k_quarter = out_refs[0].shape
    blocks = k_quarter // LANES
    irec = rows * members
    scales = [
        jnp.exp2(ref[blocks * irec :, :].astype(jnp.int32).astype(jnp.float32)) * (1.0 / FIXED)
        for ref in got_refs
    ]
    for b in range(blocks):
        total = None
        for ref, scale in zip(got_refs, scales):
            part = ref[b * irec : (b + 1) * irec, :].astype(jnp.int32).astype(jnp.float32)
            part = part * scale[b : b + 1]
            total = part if total is None else total + part
        for m in range(members):
            out_refs[m][:, b * LANES : (b + 1) * LANES] = total[m * rows : (m + 1) * rows]


def join_kernel(count_ref, got_ref, out_to, out_ref, sems):
    src_total, rows_total, _ = got_ref.shape
    k_own, col_total = out_ref.shape
    own_blocks = k_own // LANES
    cols = (rows_total - CODES) // own_blocks
    members = col_total // cols
    seg_ids = lax.broadcasted_iota(jnp.int32, (LANES, col_total), 0) % S
    inside = seg_ids < count_ref[...]
    scales = []
    for src in range(src_total):
        codes = got_ref[src, own_blocks * cols :, :].astype(jnp.int32).astype(jnp.float32)
        scales.append(jnp.exp2(codes) * (1.0 / FIXED))
    copies = []
    for b in range(own_blocks):
        rows = []
        for m in range(members):
            total = None
            for src in range(m, src_total, members):
                part = got_ref[src, b * cols : (b + 1) * cols, :]
                part = part.astype(jnp.int32).astype(jnp.float32) * scales[src][b : b + 1]
                total = part if total is None else total + part
            rows.append(total)
        whole = jnp.concatenate(rows, axis=0).T
        rows = pl.ds(b * LANES, LANES)
        out_ref[rows, :] = jnp.where(inside, whole, 0.0)
        copies.append(pltpu.make_async_copy(out_ref.at[rows], out_to.at[rows], sems.at[b]))
        copies[-1].start()
    for copy in copies:
        copy.wait()


def swap(x, axis, total, k):
    return lax.ppermute(x, axis, [(r, r ^ k) for r in range(total)])


def shards(
    receiver_spectra,
    reference_spectra,
    receiver_counts,
    reference_counts,
    column_station,
    lag_window,
    observed,
    *,
    rcv_total,
    ref_total,
):
    row_total, k_quarter = receiver_spectra.shape
    k_own, col_total = reference_spectra.shape
    k_total = k_own * rcv_total
    lag_total = observed.shape[2]
    half = lag_total // 2
    members = math.gcd(GROUP, rcv_total)
    irec = row_total * members
    cols = col_total // members
    jj_total = LANES // (2 * irec)
    jp_total = cols // jj_total
    extra = k_quarter // half + 1
    bf16 = jnp.bfloat16
    place = lax.axis_index("rcv")
    mine = place % members
    quarter = lax.axis_index("ref")
    vmem = pl.BlockSpec(memory_space=pltpu.VMEM)
    smem = pl.BlockSpec(memory_space=pltpu.SMEM)
    hbm = pl.BlockSpec(memory_space=pl.ANY)
    scalars = jnp.stack([mine, quarter * col_total, place, quarter]).astype(jnp.int32)
    def params(mib):
        return pltpu.CompilerParams(vmem_limit_bytes=mib * 1024 * 1024)

    free = pl.CostEstimate(flops=0, bytes_accessed=0, transcendentals=0)

    sent = pl.pallas_call(
        turn_kernel,
        out_shape=jax.ShapeDtypeStruct((rcv_total, cols, k_own), bf16),
        in_specs=[hbm] * 2,
        out_specs=hbm,
        scratch_shapes=[
            pltpu.VMEM((k_own, col_total), bf16),
            pltpu.VMEM((1, col_total), jnp.int32),
            pltpu.VMEM((col_total, k_own), bf16),
            pltpu.SemaphoreType.DMA((max(rcv_total, 1 + k_own // min(k_own, 4 * LANES)),)),
        ],
        compiler_params=params(62),
        cost_estimate=free,
    )(reference_spectra, reference_counts.reshape(1, col_total))
    v_all = lax.all_to_all(sent, "rcv", split_axis=0, concat_axis=0, tiled=True)

    _, observed = lax.optimization_barrier((sent, observed))
    shape = (cols, row_total, half)
    u_own, *folded = pl.pallas_call(
        fold_kernel,
        out_shape=[jax.ShapeDtypeStruct((extra, row_total, half), bf16)]
        + [jax.ShapeDtypeStruct(shape, bf16)] * members,
        in_specs=[smem] * 2 + [hbm] * 4,
        out_specs=[hbm] * (1 + members),
        scratch_shapes=[
            pltpu.VMEM(observed.shape, bf16),
            pltpu.VMEM(receiver_spectra.shape, bf16),
            pltpu.VMEM(lag_window.shape, jnp.int32),
            pltpu.VMEM((1, col_total), jnp.int32),
            pltpu.VMEM(((half // LANES * col_total + 1) * row_total, LANES), jnp.float32),
            pltpu.VMEM((members,) + shape, bf16),
            pltpu.VMEM((extra, row_total, half), bf16),
            pltpu.SemaphoreType.DMA((row_total + 3,)),
            pltpu.SemaphoreType.DMA((members + 1,)),
        ],
        compiler_params=params(32),
        cost_estimate=free,
    )(
        scalars,
        receiver_counts,
        observed,
        receiver_spectra,
        lag_window,
        column_station.reshape(1, col_total),
    )
    e_all = [folded[0]] + [swap(folded[k], "rcv", rcv_total, k) for k in range(1, members)]

    near = pl.pallas_call(
        near_kernel,
        out_shape=jax.ShapeDtypeStruct((members, extra, row_total, half), bf16),
        in_specs=[hbm] * members,
        out_specs=hbm,
        scratch_shapes=[pltpu.SemaphoreType.DMA((members,))],
        compiler_params=params(16),
        cost_estimate=free,
    )(u_own, *[swap(u_own, "rcv", rcv_total, k) for k in range(1, members)])
    u_all = [near] + [swap(near, "ref", ref_total, k) for k in range(1, ref_total)]

    group_counts = near[:, extra - 1, :, 0].reshape(irec).astype(jnp.float32)
    own_counts = lax.dynamic_slice_in_dim(reference_counts, mine * cols, cols).astype(jnp.float32)
    counts = own_counts.reshape(jj_total, jp_total).T
    least = jnp.minimum(counts[:, :, None], group_counts[None, None, :])
    inverse = (1.0 / least).reshape(jp_total, jj_total * irec)
    inverse = jnp.concatenate([inverse, inverse], axis=1)

    table = lag_tables(k_total // (2 * S), lag_total)
    w_rows = k_own // LANES * cols + CODES
    lines = (jp_total + 1) * (k_total // (2 * S) + PAD)
    w_part, z_part = pl.pallas_call(
        functools.partial(pair_kernel, members, ref_total),
        out_shape=[
            jax.ShapeDtypeStruct((rcv_total, w_rows, LANES), jnp.int16),
            jax.ShapeDtypeStruct((k_total // LANES, FB * jp_total, LANES), bf16),
        ],
        in_specs=[smem, vmem] + [hbm] * (2 + members + ref_total),
        out_specs=[hbm] * 2,
        scratch_shapes=[
            pltpu.VMEM((lines, LANES), jnp.float32),
            pltpu.VMEM((lines, LANES), jnp.float32),
            pltpu.VMEM((irec, k_total), bf16),
            pltpu.VMEM((irec, k_total), bf16),
            pltpu.VMEM((k_total // LANES, LANES), jnp.float32),
            pltpu.VMEM((ref_total,) + near.shape, bf16),
            pltpu.VMEM((rcv_total, cols, k_own), bf16),
            pltpu.VMEM((members, cols, row_total, half), bf16),
            pltpu.VMEM((k_total // LANES, FB * jp_total, LANES), bf16),
            pltpu.VMEM((rcv_total, w_rows, LANES), jnp.int16),
            pltpu.VMEM(table.shape, bf16),
            pltpu.SemaphoreType.DMA((2 + members + ref_total,)),
            pltpu.SemaphoreType.DMA((rcv_total,)),
            pltpu.SemaphoreType.DMA((rcv_total,)),
        ],
        compiler_params=params(62),
        cost_estimate=free,
    )(scalars, inverse, v_all, table, *e_all, *u_all)

    got = lax.all_to_all(w_part, "rcv", split_axis=0, concat_axis=0, tiled=True)
    reference_grad = pl.pallas_call(
        join_kernel,
        out_shape=jax.ShapeDtypeStruct((k_own, col_total), jnp.float32),
        in_specs=[vmem] * 2,
        out_specs=hbm,
        scratch_shapes=[
            pltpu.VMEM((k_own, col_total), jnp.float32),
            pltpu.SemaphoreType.DMA((k_own // LANES,)),
        ],
        compiler_params=params(32),
        cost_estimate=free,
    )(reference_counts.reshape(1, col_total), got)

    r_rows = k_quarter // LANES * irec + CODES
    r_all = pl.pallas_call(
        receiver_sum_kernel,
        out_shape=[jax.ShapeDtypeStruct((r_rows, LANES), jnp.int16)] * ref_total,
        in_specs=[smem] + [hbm] * 2,
        out_specs=[hbm] * ref_total,
        scratch_shapes=[
            pltpu.VMEM((rcv_total, cols, k_own), bf16),
            pltpu.VMEM(z_part.shape, bf16),
            pltpu.VMEM((ref_total, r_rows, LANES), jnp.int16),
            pltpu.VMEM((k_total // LANES, LANES), jnp.float32),
            pltpu.SemaphoreType.DMA((2 + ref_total,)),
        ],
        compiler_params=params(62),
        cost_estimate=free,
    )(scalars, v_all, z_part)

    parts = pl.pallas_call(
        functools.partial(add_kernel, ref_total),
        out_shape=[jax.ShapeDtypeStruct((row_total, k_quarter), jnp.float32)] * members,
        in_specs=[vmem] * ref_total,
        out_specs=[vmem] * members,
        compiler_params=params(16),
        cost_estimate=free,
    )(r_all[0], *[swap(r_all[k], "ref", ref_total, k) for k in range(1, ref_total)])
    r_sum = parts[0]
    for k in range(1, members):
        r_sum = r_sum + swap(parts[k], "rcv", rcv_total, k)
    seg_quarter = jnp.arange(k_quarter, dtype=jnp.int32) % S
    receiver_grad = jnp.where(seg_quarter[None, :] < receiver_counts[:, None], r_sum, 0.0)
    return (receiver_grad, reference_grad)


def solution(mesh):
    return jax.shard_map(
        functools.partial(shards, rcv_total=mesh.shape["rcv"], ref_total=mesh.shape["ref"]),
        mesh=mesh,
        in_specs=(
            P("rcv", "ref"),
            P("rcv", "ref"),
            P("rcv"),
            P("ref"),
            P("ref"),
            P(None, "rcv", "ref"),
            P("rcv", "ref", None),
        ),
        out_specs=(P("rcv", "ref"), P("rcv", "ref")),
        check_vma=False,
    )
```
